32 devices in a mesh: slab: 16 (over z, y, core), tm: 2 (over x).
Axes of the slice: x: 2, y: 2, z: 4, core: 2. Of those that a mesh axis runs over, the one named last changes fastest.
Arguments:
- recording: bfloat16 [512, 32768], P('tm', 'slab'), may hold values from -6 to 6
- footprints: bfloat16 [2176, 4096], P(None, 'slab'), may hold values from -0.125 to 0.125
- traces: float32 [512, 4096], P('tm', 'slab'), may hold values from 0 to 2
- live_count: int32 [16], replicated, may hold values from 1 to 256, 3072 in all
Outputs:
- new_traces: float32 [512, 4096], P('tm', 'slab')
- new_footprints: bfloat16 [2176, 4096], P('tm', 'slab')
The draws below stay inside these ranges and needn't reach their ends.
Inputs may be any that keep to these rules, and one draw needn't show every extreme that they name: Slots 0 .. live_count[s] - 1 of slab s are live; some slab has all 256 live.
All inputs are finite; a program needn't handle non-finite values.
Results may differ from the reference program's by a relative error of at most 0.0034.
Values may be sent and summed in bfloat16 or wider, within the bound.
No kernel may reach another device: no remote copies, remote signals or barrier semaphores. Data moves between devices by JAX's collectives and lax.ppermute only.
A program may use at most 64 MiB of HBM per device.

```python
import math
import jax
import jax.numpy as jnp
import numpy as np
from jax import lax

FRAMES = 512
GROUP = 128
GROUPS_DEV = 2
VOX_DEV = 2048
RIM = 128
K_DEV = 256
SLABS = 16
NEURONS = 4096
VOXELS = 32768
N_SLAB = 16


def level_of(rng, dims, split, least, high):
    def one(axis_at, blocks):
        draws = jax.random.uniform(jax.random.fold_in(jax.random.fold_in(rng, 6), axis_at), (blocks,), jnp.float32, least / len(split), high / len(split))
        return jnp.repeat(jnp.exp(draws), dims[axis_at] // blocks).reshape((-1,) + (1,) * (len(dims) - axis_at - 1))

    gain = one(*split[0])
    for cut in split[1:]:
        gain = gain * one(*cut)
    return gain


def split_up(number_of, total, bound, lean):
    weights = [(1 << 20) // math.isqrt(rank ** lean) + 1 for rank in range(2, number_of + 1)]
    rest, holding = total - bound - (number_of - 1), [1] * (number_of - 1)
    while rest > 0:
        free = [i for i in range(number_of - 1) if holding[i] < bound]
        pool, budget = sum([weights[i] for i in free]), rest
        for i in free:
            more = min(bound - holding[i], max(1, budget * weights[i] // pool), rest)
            holding[i] = holding[i] + more
            rest = rest - more
    return np.array([bound] + holding)


def ragged_sizes(rng, amount, total, limit, lean):
    if amount == 2:
        one = jax.random.randint(rng, (), max(1, total - limit), min(limit, total - 1) + 1)
        return jnp.stack([one, total - one])
    tallies = jnp.asarray(split_up(amount, total, limit, lean), jnp.int32)
    twos = (amount - 1) // 2
    giver, sink = tallies[1:1 + 2 * twos:2], tallies[2:2 + 2 * twos:2]
    room = jnp.minimum(giver - 1, limit - sink)
    passed = jax.random.randint(jax.random.fold_in(rng, 1), (twos,), 0, 1 << 20) % (room + 1)
    tallies = tallies.at[1:1 + 2 * twos:2].set(giver - passed).at[2:2 + 2 * twos:2].set(sink + passed)
    return tallies[jax.random.permutation(jax.random.fold_in(rng, 2), amount)]


def gaussian(stream_key, dims, width, bound, split=(), kind=jnp.bfloat16):
    entries = width * jax.random.normal(stream_key, dims, jnp.float32)
    if split:
        entries = entries * level_of(stream_key, dims, split, -0.22, 0.18)
    return jnp.clip(entries, -bound, bound).astype(kind)


def setup_inputs(seed: int = 0) -> dict:
    arg_keys = jax.random.split(jax.random.key(seed), 5)
    return {
        "recording": gaussian(arg_keys[0], (FRAMES, VOXELS), 1.0, 6.0, ((0, 2), (1, 16))),
        "footprints": gaussian(arg_keys[1], (VOX_DEV + RIM, NEURONS), (VOX_DEV + RIM) ** -0.5, 0.125, ((1, 16),)),
        "traces": jnp.clip(2.0 * jax.random.uniform(arg_keys[2], (FRAMES, NEURONS), jnp.float32) ** level_of(arg_keys[2], (FRAMES, NEURONS), ((0, 2), (1, 16)), -0.2, 0.2), 0.0, 2.0),
        "live_count": ragged_sizes(arg_keys[3], SLABS, SLABS * K_DEV * 3 // 4, K_DEV, 2).astype(jnp.int32),
    }


def contract_first(left, right):
    return lax.dot_general(left, right, (((0,), (0,)), ((), ())), preferred_element_type=jnp.float32)


def shifted_pair(stacked):
    empty = jnp.zeros_like(stacked[:1])
    return jnp.concatenate([empty, stacked[:-1]], 0), jnp.concatenate([stacked[1:], empty], 0)


def reference(recording, footprints, traces, live_count):
    extended = VOX_DEV + RIM
    slots = jnp.arange(K_DEV, dtype=jnp.int32)
    living = slots[None, :] < live_count[:, None]
    row_ids = jnp.arange(extended, dtype=jnp.int32)
    slab_ids = jnp.arange(N_SLAB, dtype=jnp.int32)
    row_keep = (row_ids[None, :] < VOX_DEV) | (slab_ids[:, None] < N_SLAB - 1)
    stacked = footprints.reshape(extended, N_SLAB, K_DEV).transpose(1, 0, 2)
    stacked = jnp.where(living[:, None, :] & row_keep[:, :, None], stacked, jnp.zeros_like(stacked))
    start_tr = traces.reshape(FRAMES, N_SLAB, K_DEV).transpose(1, 0, 2)
    start_tr = jnp.where(living[:, None, :], start_tr, jnp.zeros_like(start_tr))
    movie_slabs = recording.reshape(FRAMES, N_SLAB, VOX_DEV).transpose(1, 0, 2)
    movie_prev, movie_next = shifted_pair(movie_slabs)
    y_ext = jnp.concatenate([movie_slabs, movie_next[:, :, :RIM]], 2)
    rim_prev, unused_rim = shifted_pair(stacked[:, VOX_DEV:])
    unused_edge, edge_next = shifted_pair(stacked[:, :RIM])
    traces_prev, traces_next = shifted_pair(start_tr)

    def trace_slab(items):
        masked_foot, movie_ext, prev_rim, next_edge, current, prev_c, next_c = items
        drive = jnp.dot(movie_ext, masked_foot, preferred_element_type=jnp.float32)
        gram_own = contract_first(masked_foot, masked_foot)
        gram_prev = contract_first(masked_foot[:RIM], prev_rim)
        gram_next = contract_first(masked_foot[VOX_DEV:], next_edge)
        diag_own = jnp.diagonal(gram_own) + 1e-6
        outside = jnp.dot(prev_c, gram_prev.T, precision=lax.Precision.HIGHEST) + jnp.dot(next_c, gram_next.T, precision=lax.Precision.HIGHEST)
        for group_id in range(GROUPS_DEV):
            offset = group_id * GROUP
            coupled = jnp.dot(current, gram_own[:, offset:offset + GROUP], precision=lax.Precision.HIGHEST) + outside[:, offset:offset + GROUP]
            updated = jnp.maximum(current[:, offset:offset + GROUP] + (drive[:, offset:offset + GROUP] - coupled) / diag_own[offset:offset + GROUP], 0.0)
            current = current.at[:, offset:offset + GROUP].set(updated)
        return current

    new_tr = lax.map(trace_slab, (stacked, y_ext, rim_prev, edge_next, start_tr, traces_prev, traces_next))
    rounded = new_tr.astype(jnp.bfloat16)
    rounded_prev, rounded_next = shifted_pair(rounded)

    def foot_slab(items):
        masked_foot, movie_ext, prev_rim, next_edge, own_c, prev_c, next_c = items
        proj_rows = contract_first(movie_ext, own_c)
        q_own = contract_first(own_c, own_c)
        q_prev = contract_first(prev_c, own_c)
        q_next = contract_first(next_c, own_c)
        divisor = jnp.maximum(jnp.diagonal(q_own), 1.0)
        foot_f = masked_foot.astype(jnp.float32)
        coupling = jnp.dot(foot_f, q_own, precision=lax.Precision.HIGHEST)
        coupling = coupling.at[:RIM].add(jnp.dot(prev_rim.astype(jnp.float32), q_prev, precision=lax.Precision.HIGHEST))
        coupling = coupling.at[VOX_DEV:].add(jnp.dot(next_edge.astype(jnp.float32), q_next, precision=lax.Precision.HIGHEST))
        return jnp.maximum(foot_f + (proj_rows - coupling) / divisor, 0.0).astype(jnp.bfloat16)

    new_foot = lax.map(foot_slab, (stacked, y_ext, rim_prev, edge_next, rounded, rounded_prev, rounded_next))
    out_traces = new_tr.transpose(1, 0, 2).reshape(FRAMES, NEURONS)
    out_foot = new_foot.transpose(1, 0, 2).reshape(extended, NEURONS)
    return out_traces, out_foot
```

```python
import functools

import jax
import jax.numpy as jnp
from jax import lax
from jax.experimental import pallas as pl
from jax.experimental.pallas import tpu as pltpu
from jax.sharding import PartitionSpec as P

GROUP = 128
BF = jnp.bfloat16
F32 = jnp.float32
WHOLE = pl.BlockSpec(memory_space=pltpu.VMEM)
SCALARS = pl.BlockSpec(memory_space=pltpu.SMEM)
LEFT_THERE = pl.BlockSpec(memory_space=pl.ANY)


def mm(left, right):
    return jnp.dot(left, right, preferred_element_type=F32)


def mm_t(left, right):
    return lax.dot_general(left, right, (((1,), (1,)), ((), ())), preferred_element_type=F32)


def t_mm(left, right):
    return lax.dot_general(left, right, (((0,), (0,)), ((), ())), preferred_element_type=F32)


def halves(wide):
    high = wide.astype(BF)
    return high, (wide - high.astype(F32)).astype(BF)


def living(live_ref, block):
    slots = lax.broadcasted_iota(jnp.int32, block.shape, 1)
    return jnp.where(slots < live_ref[lax.axis_index("slab")], block, jnp.zeros_like(block))


def diagonal(square):
    rows = lax.broadcasted_iota(jnp.int32, square.shape, 0)
    columns = lax.broadcasted_iota(jnp.int32, square.shape, 1)
    return jnp.sum(jnp.where(rows == columns, square, 0.0), axis=0, keepdims=True)


def call(body, outs, in_specs, out_specs, flops, **more):
    return pl.pallas_call(
        body,
        out_shape=outs,
        in_specs=in_specs,
        out_specs=out_specs,
        compiler_params=pltpu.CompilerParams(vmem_limit_bytes=48 * 1024 * 1024),
        cost_estimate=pl.CostEstimate(flops=flops, bytes_accessed=2 ** 21, transcendentals=0),
        **more,
    )


def copied(source, target, sem):
    copy = pltpu.make_async_copy(source, target, sem)
    copy.start()
    return copy


def rim_kernel(voxels, share, live, movie, foot, start, near, far, outgoing, head, tail, sems):
    rim = head.shape[0]
    odd = lax.axis_index("slab") % 2 == 1
    last = lax.axis_index("slab") == lax.axis_size("slab") - 1
    first = copied(foot.at[pl.ds(0, rim)], head, sems.at[0])
    second = copied(foot.at[pl.ds(voxels, rim)], tail, sems.at[1])
    if outgoing is not None:
        take_share(1 - lax.axis_index("tm"), voxels, share, rim, movie, outgoing)
    high, low = halves(living(live, start[...]))
    first.wait()
    second.wait()
    ends = jnp.where(last, jnp.zeros_like(tail[...]), tail[...])
    forward = mm_t(high, ends) + mm_t(low, ends)
    backward = movie[:, :rim].astype(F32) - (mm_t(high, head[...]) + mm_t(low, head[...]))
    near[...] = jnp.where(odd, backward, forward)
    far[...] = jnp.where(odd, forward, backward)


def take_share(which, voxels, share, rim, movie, block):
    @pl.when(which == 0)
    def _():
        block[...] = movie[:, :share]

    @pl.when(which == 1)
    def _():
        block[:, :rim] = movie[:, :rim]
        block[:, rim:] = movie[:, share:]


def drive_kernel(voxels, share, live, movie, foot, drive, gram, kept, masked):
    rim = foot.shape[0] - voxels
    last = lax.axis_index("slab") == lax.axis_size("slab") - 1
    masked[:voxels] = living(live, foot[:voxels])
    ends = living(live, foot[voxels:])
    masked[voxels:] = jnp.where(last, jnp.zeros_like(ends), ends)
    drive[...] = mm(movie[...], masked[:voxels])
    gram[...] = t_mm(masked[...], masked[...])
    if kept is not None:
        take_share(lax.axis_index("tm"), voxels, share, rim, movie, kept)


def sweep_kernel(voxels, live, drive, gram, foot, start, near, far, traces, rounded, head, tail, sems):
    rim = head.shape[0]
    odd = lax.axis_index("slab") % 2 == 1
    last = lax.axis_index("slab") == lax.axis_size("slab") - 1
    first = copied(foot.at[pl.ds(0, rim)], head, sems.at[0])
    second = copied(foot.at[pl.ds(voxels, rim)], tail, sems.at[1])
    square = gram[...]
    scale = diagonal(square) + 1e-06
    square_high, square_low = halves(square)
    current = living(live, start[...])
    one, two = near[...], far[...]
    from_prev = halves(jnp.where(odd, one, two))
    from_next = halves(jnp.where(odd, two, one))
    first.wait()
    second.wait()
    begins = living(live, head[...])
    ends = living(live, tail[...])
    ends = jnp.where(last, jnp.zeros_like(ends), ends)
    pull = drive[...] - (mm(from_prev[0], begins) + mm(from_prev[1], begins))
    pull = pull + (mm(from_next[0], ends) + mm(from_next[1], ends))
    for offset in range(0, current.shape[1], GROUP):
        columns = slice(offset, offset + GROUP)
        high, low = halves(current)
        coupled = mm(high, square_high[:, columns])
        coupled = coupled + mm(high, square_low[:, columns]) + mm(low, square_high[:, columns])
        step = (pull[:, columns] - coupled) / scale[:, columns]
        updated = jnp.maximum(current[:, columns] + step, 0.0)
        parts = [current[:, :offset], updated, current[:, offset + GROUP:]]
        current = jnp.concatenate([part for part in parts if part.shape[1]], axis=1)
    traces[...] = current
    rounded[...] = current.astype(BF)


def edge_kernel(voxels, pairs, *refs):
    foot, refs = refs[0], refs[1:]
    movies, fits = refs[:pairs], refs[pairs:2 * pairs]
    sent, edge, sem = refs[2 * pairs:]
    rim = edge.shape[0]
    ending = lax.axis_index("tm") == 0
    row = pl.multiple_of(jnp.where(ending, voxels, 0), rim)
    copied(foot.at[pl.ds(row, rim)], edge, sem).wait()
    at = 0
    for movie, fit in zip(movies, fits):
        frames = fit.shape[0]
        seen = jnp.where(ending, 0.0, movie[...].astype(F32))
        sent[at:at + frames] = seen - mm_t(fit[...], edge[...])
        at += frames


def places(share, rim):
    closing = lax.axis_index("tm") == lax.axis_size("tm") - 1
    inner = pl.multiple_of(jnp.where(closing, 0, rim), 16)
    outer = pl.multiple_of(jnp.where(closing, share - rim, 0), 16)
    return closing, inner, outer


def inner_kernel(rim, pairs, live, foot, *refs):
    movies, fits = refs[:pairs], refs[pairs:2 * pairs]
    out, quad, part, sem = refs[2 * pairs:]
    share = out.shape[0]
    _, inner, _ = places(share, rim)
    row = pl.multiple_of(lax.axis_index("tm") * share + inner, 16)
    copy = copied(foot.at[pl.ds(row, share - rim)], part, sem)
    square = sum(t_mm(fit[...], fit[...]) for fit in fits)
    quad[...] = square
    scale = jnp.maximum(diagonal(square), 1.0)
    high, low = halves(square)
    total = sum(t_mm(movie[:, rim:], fit[...]) for movie, fit in zip(movies, fits))
    copy.wait()
    own = living(live, part[...])
    total = total - (mm(own, high) + mm(own, low))
    moved = jnp.maximum(own.astype(F32) + total / scale, 0.0)
    out[pl.ds(inner, share - rim)] = moved.astype(BF)


def outer_kernel(pairs, live, foot, sofar, quad, came, *refs):
    movies, fits = refs[:pairs], refs[pairs:2 * pairs]
    out, part, moved, sems = refs[2 * pairs:]
    share, rim = out.shape[0], part.shape[0]
    closing, _, outer = places(share, rim)
    last = lax.axis_index("slab") == lax.axis_size("slab") - 1
    row = pl.multiple_of(lax.axis_index("tm") * share + outer, 16)
    copy = copied(foot.at[pl.ds(row, rim)], part, sems.at[0])
    square = quad[...]
    scale = jnp.maximum(diagonal(square), 1.0)
    high, low = halves(square)
    total = 0.0
    at = 0
    for movie, fit in zip(movies, fits):
        frames = fit.shape[0]
        seen = jnp.where(closing, 0.0, movie[...].astype(F32)) + came[at:at + frames]
        seen_high, seen_low = halves(seen)
        total = total + (t_mm(seen_high, fit[...]) + t_mm(seen_low, fit[...]))
        at += frames
    copy.wait()
    own = living(live, part[...])
    own = jnp.where(closing & last, jnp.zeros_like(own), own)
    total = total - (mm(own, high) + mm(own, low))
    moved[...] = jnp.maximum(own.astype(F32) + total / scale, 0.0).astype(BF)
    copied(moved, out.at[pl.ds(outer, rim)], sems.at[1]).wait()


def on_device(recording, footprints, traces, live_count):
    slabs, parts = lax.axis_size("slab"), lax.axis_size("tm")
    frames, voxels = recording.shape
    extended, neurons = footprints.shape
    rim = extended - voxels
    share = extended // parts
    swaps = parts == 2
    shape = jax.ShapeDtypeStruct
    copies = pltpu.SemaphoreType.DMA
    share_shape = [shape((frames, share), BF)] if swaps else []

    def rims(live, movie, foot, start, near, far, *rest):
        outgoing = rest[0] if swaps else None
        rim_kernel(voxels, share, live, movie, foot, start, near, far, outgoing, *rest[-3:])

    rim_shape = shape((frames, rim), F32)
    near, far, *outgoing = call(
        rims,
        [rim_shape, rim_shape] + share_shape,
        [SCALARS, WHOLE, LEFT_THERE, WHOLE],
        [WHOLE] * (2 + len(share_shape)),
        2 * frames * neurons * rim * 4,
        scratch_shapes=[pltpu.VMEM((rim, neurons), BF)] * 2 + [copies((2,))],
    )(live_count, recording, footprints, traces)

    if swaps:
        other_movie = lax.ppermute(outgoing[0], "tm", [(0, 1), (1, 0)])
    far = lax.ppermute(
        far, "slab", [pair for i in range(1, slabs - 1, 2) for pair in ((i, i + 1), (i + 1, i))]
    )
    near = lax.ppermute(
        near, "slab", [pair for i in range(0, slabs, 2) for pair in ((i, i + 1), (i + 1, i))]
    )

    def drives(live, movie, foot, drive, gram, *rest):
        kept = rest[0] if swaps else None
        drive_kernel(voxels, share, live, movie, foot, drive, gram, kept, rest[-1])

    drive, gram, *kept = call(
        drives,
        [shape((frames, neurons), F32), shape((neurons, neurons), F32)] + share_shape,
        [SCALARS, WHOLE, WHOLE],
        [WHOLE] * (2 + len(share_shape)),
        2 * (frames + neurons) * neurons * extended,
        scratch_shapes=[pltpu.VMEM((extended, neurons), BF)],
    )(live_count, recording, footprints)

    new_tr, rounded = call(
        functools.partial(sweep_kernel, voxels),
        [shape((frames, neurons), F32), shape((frames, neurons), BF)],
        [SCALARS, WHOLE, WHOLE, LEFT_THERE, WHOLE, WHOLE, WHOLE],
        [WHOLE, WHOLE],
        2 * frames * neurons * neurons * 5,
        scratch_shapes=[pltpu.VMEM((rim, neurons), BF)] * 2 + [copies((2,))],
    )(live_count, drive, gram, footprints, traces, near, far)

    if swaps:
        movies = [kept[0], other_movie]
        fits = [rounded, lax.ppermute(rounded, "tm", [(0, 1), (1, 0)])]
    else:
        cut = (parts - 1) * share
        spread = jnp.concatenate([recording[:, :cut], recording[:, :rim], recording[:, cut:]], 1)
        movies = [lax.all_to_all(spread, "tm", split_axis=1, concat_axis=0, tiled=True)]
        fits = [lax.all_gather(rounded, "tm", axis=0, tiled=True)]
    pairs = len(fits)
    lead_specs = [
        pl.BlockSpec((movie.shape[0], rim), lambda i: (0, 0)) for movie in movies
    ]
    total = frames * parts

    sent = call(
        functools.partial(edge_kernel, voxels, pairs),
        shape((total, rim), F32),
        [LEFT_THERE] + lead_specs + [WHOLE] * pairs,
        WHOLE,
        2 * total * neurons * rim,
        grid=(1,),
        scratch_shapes=[pltpu.VMEM((rim, neurons), BF), copies],
    )(footprints, *movies, *fits)
    ahead = [(i * parts, (i + 1) * parts) for i in range(slabs - 1)]
    behind = [((i + 1) * parts - 1 + parts, (i + 1) * parts - 1) for i in range(slabs - 1)]
    came = lax.ppermute(sent, ("slab", "tm"), ahead + behind)

    sofar, quad = call(
        functools.partial(inner_kernel, rim, pairs),
        [shape((share, neurons), BF), shape((neurons, neurons), F32)],
        [SCALARS, LEFT_THERE] + [WHOLE] * (2 * pairs),
        [WHOLE, WHOLE],
        2 * total * neurons * (share + neurons) + 4 * share * neurons * neurons,
        scratch_shapes=[pltpu.VMEM((share - rim, neurons), BF), copies],
    )(live_count, footprints, *movies, *fits)

    new_foot = call(
        functools.partial(outer_kernel, pairs),
        shape((share, neurons), BF),
        [SCALARS, LEFT_THERE, LEFT_THERE, WHOLE, WHOLE] + lead_specs + [WHOLE] * pairs,
        LEFT_THERE,
        2 * total * neurons * rim * 2,
        grid=(1,),
        input_output_aliases={2: 0},
        scratch_shapes=[pltpu.VMEM((rim, neurons), BF)] * 2 + [copies((2,))],
    )(live_count, footprints, sofar, quad, came, *movies, *fits)
    return new_tr, new_foot


def solution(mesh):
    placed = (P("tm", "slab"), P(None, "slab"), P("tm", "slab"), P())
    return jax.shard_map(
        on_device,
        mesh=mesh,
        in_specs=placed,
        out_specs=(P("tm", "slab"), P("tm", "slab")),
        check_vma=False,
    )
```

```python
import functools

import jax
import jax.numpy as jnp
from jax import lax
from jax.experimental import pallas as pl
from jax.experimental.pallas import tpu as pltpu
from jax.sharding import PartitionSpec as P

GROUP = 128
EARLY = 640
BF = jnp.bfloat16
F32 = jnp.float32
WHOLE = pl.BlockSpec(memory_space=pltpu.VMEM)
LEFT_THERE = pl.BlockSpec(memory_space=pl.ANY)
COPIES = pltpu.SemaphoreType.DMA
shape = jax.ShapeDtypeStruct


def mm(left, right):
    return jnp.dot(left, right, preferred_element_type=F32)


def mm_t(left, right):
    return lax.dot_general(left, right, (((1,), (1,)), ((), ())), preferred_element_type=F32)


def t_mm(left, right):
    return lax.dot_general(left, right, (((0,), (0,)), ((), ())), preferred_element_type=F32)


def halves(wide):
    high = wide.astype(BF)
    return high, (wide - high.astype(F32)).astype(BF)


def living(count, block):
    slots = lax.broadcasted_iota(jnp.int32, block.shape, 1)
    return jnp.where(slots < count, block, jnp.zeros_like(block))


def diagonal(square):
    rows = lax.broadcasted_iota(jnp.int32, square.shape, 0)
    columns = lax.broadcasted_iota(jnp.int32, square.shape, 1)
    return jnp.sum(jnp.where(rows == columns, square, 0.0), axis=0, keepdims=True)


def at_end(axis):
    return lax.axis_index(axis) == lax.axis_size(axis) - 1


def odd_slab():
    return lax.axis_index("slab") % 2 == 1


def call(body, outs, in_specs, out_specs, flops, limit=32, **more):
    return pl.pallas_call(
        body,
        out_shape=outs,
        in_specs=in_specs,
        out_specs=out_specs,
        compiler_params=pltpu.CompilerParams(vmem_limit_bytes=limit * 1024 * 1024),
        cost_estimate=pl.CostEstimate(flops=flops, bytes_accessed=2 ** 21, transcendentals=0),
        **more,
    )


def copied(source, target, sem):
    copy = pltpu.make_async_copy(source, target, sem)
    copy.start()
    return copy


def first_column(which, voxels, rim):
    return pl.multiple_of(rim + which * (voxels // 2 - rim), 128)


def rim_kernel(voxels, live, movie, foot, start, near, far, count, *rest):
    numbers, head, tail, traces, edge, sems = rest[-6:]
    rim = head.shape[0]
    small = [
        copied(live, numbers, sems.at[0]),
        copied(start, traces, sems.at[1]),
        copied(foot.at[pl.ds(0, rim)], head, sems.at[2]),
        copied(foot.at[pl.ds(voxels, rim)], tail, sems.at[3]),
        copied(movie.at[:, pl.ds(0, rim)], edge, sems.at[4]),
    ]
    large = []
    if len(rest) > 6:
        column = first_column(1 - lax.axis_index("tm"), voxels, rim)
        large = [
            copied(movie.at[:, pl.ds(0, rim)], rest[0].at[:, pl.ds(0, rim)], sems.at[5]),
            copied(movie.at[:, pl.ds(column, EARLY)], rest[0].at[:, pl.ds(rim, EARLY)], sems.at[6]),
        ]
    for copy in small:
        copy.wait()
    alive = numbers[lax.axis_index("slab")]
    count[...] = jnp.full(count.shape, alive, jnp.int32)
    high, low = halves(living(alive, traces[...]))
    ends = jnp.where(at_end("slab"), jnp.zeros_like(tail[...]), tail[...])
    forward = mm_t(high, ends) + mm_t(low, ends)
    backward = edge[...].astype(F32) - (mm_t(high, head[...]) + mm_t(low, head[...]))
    odd = odd_slab()
    near[...] = jnp.where(odd, backward, forward)
    far[...] = jnp.where(odd, forward, backward)
    for copy in large:
        copy.wait()


def drive_kernel(voxels, count, movie, foot, start, plan, scale, cross_high, cross_low, rims, masked):
    rim = foot.shape[0] - voxels
    alive = count[0:1]
    masked[:voxels] = living(alive, foot[:voxels])
    ends = living(alive, foot[voxels:])
    masked[voxels:] = jnp.where(at_end("slab"), jnp.zeros_like(ends), ends)
    rims[:rim] = -masked[:rim]
    rims[rim:] = masked[voxels:]
    drive = mm(movie[...], masked[:voxels])
    gram = t_mm(masked[...], masked[...])
    inverse = 1.0 / (diagonal(gram) + 1e-06)
    scale[...] = jnp.broadcast_to(inverse, scale.shape)
    gram_high, gram_low = halves(gram)
    cross_high[...] = gram_high[:GROUP, GROUP:]
    cross_low[...] = gram_low[:GROUP, GROUP:]
    current = living(alive, start[...])
    high, low = halves(current)
    for at in range(0, current.shape[1], GROUP):
        columns = slice(at, at + GROUP)
        coupled = mm(high[:, at:], gram_high[at:, columns]) + mm(high[:, at:], gram_low[at:, columns])
        coupled = coupled + mm(low[:, at:], gram_high[at:, columns])
        plan[:, columns] = current[:, columns] + (drive[:, columns] - coupled) * inverse[:, columns]


def sweep_kernel(plan, scale, cross_high, cross_low, rims, near, far, traces, rounded):
    odd = odd_slab()
    one, two = near[...], far[...]
    beside = jnp.concatenate([jnp.where(odd, one, two), jnp.where(odd, two, one)], axis=1)
    high, low = halves(beside)
    edges = rims[...]
    stepped = plan[...] + (mm(high, edges) + mm(low, edges)) * scale[0:1]
    first = jnp.maximum(stepped[:, :GROUP], 0.0)
    high, low = halves(first)
    cross = cross_high[...]
    coupled = mm(high, cross) + mm(high, cross_low[...]) + mm(low, cross)
    second = jnp.maximum(stepped[:, GROUP:] - coupled * scale[0:1, GROUP:], 0.0)
    traces[:, :GROUP] = first
    traces[:, GROUP:] = second
    rounded[:, :GROUP] = first.astype(BF)
    rounded[:, GROUP:] = second.astype(BF)


def own_kernel(voxels, rim, movie, foot, fit, early, total, lead, quad, sent_own, seen_other, late, sem):
    here = lax.axis_index("tm")
    width = voxels // 2
    there = pl.multiple_of(first_column(1 - here, voxels, rim) + EARLY, 128)
    copy = copied(movie.at[:, pl.ds(there, width - EARLY)], late, sem)
    traces = fit[...]
    row = pl.multiple_of(jnp.where(here == 0, voxels, 0), rim)
    edge = foot[pl.ds(row, rim)]
    flat = movie[:, :rim].T.astype(F32)
    sent_own[...] = (jnp.where(here == 0, 0.0, flat) - mm_t(edge, traces)).astype(BF)
    seen_other[...] = jnp.where(here == 0, 0.0, early[:, :rim].T.astype(F32)).astype(BF)
    quad[...] = t_mm(traces, traces)
    lead[...] = jnp.where(here == 0, mm(flat.astype(BF), traces), 0.0)
    total[...] = t_mm(movie[:, pl.ds(first_column(here, voxels, rim), width)], traces)
    copy.wait()


def sent_kernel(voxels, foot, fit, sent_own, seen_other, sent):
    rim, frames = sent_own.shape
    row = pl.multiple_of(jnp.where(lax.axis_index("tm") == 0, voxels, 0), rim)
    sent[:, :frames] = sent_own[...]
    seen = seen_other[...].astype(F32) - mm_t(foot[pl.ds(row, rim)], fit[...])
    sent[:, frames:] = seen.astype(BF)


def rest_kernel(voxels, rim, count, foot, total, lead, quad, early, late, fit, out, base, scale, moved, sem):
    here = lax.axis_index("tm")
    width = voxels // 2
    share = foot.shape[0] // 2
    alive = count[0:1]
    traces = fit[...]
    square = quad[...] + t_mm(traces, traces)
    inverse = 1.0 / jnp.maximum(diagonal(square), 1.0)
    scale[...] = jnp.broadcast_to(inverse, scale.shape)
    high, low = halves(square)
    row = first_column(here, voxels, rim)
    for at in range(0, width, 128):
        movie = early[:, rim + at:rim + at + 128] if at < EARLY else late[:, at - EARLY:at - EARLY + 128]
        own = living(alive, foot[pl.ds(pl.multiple_of(row + at, 128), 128)])
        part = total[at:at + 128] + t_mm(movie, traces) - (mm(own, high) + mm(own, low))
        moved[at:at + 128] = jnp.maximum(own.astype(F32) + part * inverse, 0.0).astype(BF)
    kept = share - rim
    begin = pl.multiple_of(here * (rim // 2), 64)
    copy = copied(
        moved.at[pl.ds(begin, kept)], out.at[pl.ds(pl.multiple_of(rim - here * rim, rim), kept)], sem
    )
    own = living(alive, foot[pl.ds(pl.multiple_of(here * voxels, rim), rim)])
    own = jnp.where((here == 1) & at_end("slab"), jnp.zeros_like(own), own)
    part = lead[...] + jnp.where(here == 0, t_mm(early[:, :rim], traces), 0.0)
    part = part - (mm(own, high) + mm(own, low))
    base[...] = own.astype(F32) + part * inverse
    copy.wait()


def edge_kernel(sofar, came, fit_own, fit_other, base, scale, out, moved, sem):
    frames = fit_own.shape[0]
    rim = base.shape[0]
    part = mm(came[:, :frames], fit_own[...]) + mm(came[:, frames:], fit_other[...])
    moved[...] = jnp.maximum(base[...] + part * scale[0:1], 0.0).astype(BF)
    row = pl.multiple_of(lax.axis_index("tm") * (out.shape[0] - rim), 64)
    copied(moved, out.at[pl.ds(row, rim)], sem).wait()


def halved(voxels, rim, count, recording, footprints, early, rounded):
    frames = recording.shape[0]
    extended, neurons = footprints.shape
    slabs = lax.axis_size("slab")
    width, share = voxels // 2, extended // 2
    across = [(0, 1), (1, 0)]
    came_early = lax.ppermute(early, "tm", across)
    other = lax.ppermute(rounded, "tm", across)
    total, lead, quad, sent_own, seen_other, late = call(
        functools.partial(own_kernel, voxels, rim),
        [
            shape((width, neurons), F32),
            shape((rim, neurons), F32),
            shape((neurons, neurons), F32),
            shape((rim, frames), BF),
            shape((rim, frames), BF),
            shape((frames, width - EARLY), BF),
        ],
        [WHOLE] * 4,
        [WHOLE] * 6,
        2 * frames * neurons * (width + neurons + rim),
        scratch_shapes=[COPIES],
    )(recording, footprints, rounded, came_early)
    came_late = lax.ppermute(late, "tm", across)
    sent = call(
        functools.partial(sent_kernel, voxels),
        shape((rim, 2 * frames), BF),
        [WHOLE] * 4,
        WHOLE,
        2 * frames * neurons * rim,
    )(footprints, other, sent_own, seen_other)
    ahead = [(i * 2, i * 2 + 2) for i in range(slabs - 1)]
    behind = [(i * 2 + 3, i * 2 + 1) for i in range(slabs - 1)]
    came = lax.ppermute(sent, ("slab", "tm"), ahead + behind)
    sofar, base, scale = call(
        functools.partial(rest_kernel, voxels, rim),
        [shape((share, neurons), BF), shape((rim, neurons), F32), shape((8, neurons), F32)],
        [WHOLE] * 8,
        [LEFT_THERE, WHOLE, WHOLE],
        2 * neurons * (frames + 2 * neurons) * width,
        scratch_shapes=[pltpu.VMEM((width, neurons), BF), COPIES],
    )(count, footprints, total, lead, quad, came_early, came_late, other)
    return call(
        edge_kernel,
        shape((share, neurons), BF),
        [LEFT_THERE] + [WHOLE] * 5,
        LEFT_THERE,
        2 * 2 * frames * neurons * rim,
        input_output_aliases={0: 0},
        scratch_shapes=[pltpu.VMEM((rim, neurons), BF), COPIES],
    )(sofar, came, rounded, other, base, scale)


def spread(voxels, rim, count, recording, footprints, rounded):
    slabs, parts = lax.axis_size("slab"), lax.axis_size("tm")
    extended, neurons = footprints.shape
    share = extended // parts
    here = lax.axis_index("tm")
    closing = here == parts - 1
    exact = lax.Precision.HIGHEST
    cut = voxels - (share - rim)
    columns = jnp.concatenate([recording[:, :cut], recording[:, :rim], recording[:, cut:]], 1)
    movie = lax.all_to_all(columns, "tm", split_axis=1, concat_axis=0, tiled=True)
    fit = lax.all_gather(rounded, "tm", axis=0, tiled=True)
    alive = jnp.arange(neurons) < count[0]
    rows = jnp.arange(extended)[:, None]
    foot = jnp.where(alive & ((rows < voxels) | ~at_end("slab")), footprints, jnp.zeros_like(footprints))
    edge = jnp.where(here == 0, foot[voxels:], foot[:rim])
    seen = movie[:, :rim].astype(F32)
    sent = jnp.where(here == 0, 0.0, seen) - mm_t(fit, edge)
    ahead = [(i * parts, (i + 1) * parts) for i in range(slabs - 1)]
    behind = [((i + 2) * parts - 1, (i + 1) * parts - 1) for i in range(slabs - 1)]
    lead = jnp.where(closing, 0.0, seen) + lax.ppermute(sent, ("slab", "tm"), ahead + behind)
    lead = lax.dot_general(lead, fit.astype(F32), (((0,), (0,)), ((), ())), precision=exact)
    inner = t_mm(movie[:, rim:], fit)
    total = jnp.where(
        closing, jnp.concatenate([inner, lead], 0), jnp.concatenate([lead, inner], 0)
    )
    square = t_mm(fit, fit)
    own = lax.dynamic_slice_in_dim(foot, here * share, share, 0).astype(F32)
    total = total - jnp.dot(own, square, precision=exact)
    return jnp.maximum(own + total / jnp.maximum(jnp.diagonal(square), 1.0), 0.0).astype(BF)


def on_device(recording, footprints, traces, live_count):
    slabs, parts = lax.axis_size("slab"), lax.axis_size("tm")
    frames, voxels = recording.shape
    extended, neurons = footprints.shape
    rim = extended - voxels
    rim_shape = shape((frames, rim), F32)
    early_shape = [pltpu.VMEM((frames, rim + EARLY), BF)] if parts == 2 else []
    pinned = [
        pltpu.with_memory_space_constraint(x, pltpu.HBM)
        for x in (live_count, recording, footprints, traces)
    ]
    near, far, count, *early = call(
        functools.partial(rim_kernel, voxels),
        [
            pltpu.VMEM((frames, rim), F32),
            pltpu.VMEM((frames, rim), F32),
            pltpu.VMEM((8, neurons), jnp.int32),
        ]
        + early_shape,
        [LEFT_THERE] * 4,
        [WHOLE] * (3 + len(early_shape)),
        2 * frames * neurons * rim * 4,
        scratch_shapes=[
            pltpu.SMEM(live_count.shape, jnp.int32),
            pltpu.VMEM((rim, neurons), BF),
            pltpu.VMEM((rim, neurons), BF),
            pltpu.VMEM((frames, neurons), F32),
            pltpu.VMEM((frames, rim), BF),
            COPIES((7,)),
        ],
    )(*pinned)

    def swapped(block, first):
        route = [(i, i + 1) for i in range(first, slabs - 1, 2)]
        return lax.ppermute(block, "slab", route + [(j, i) for i, j in route])

    far = swapped(far, 1)
    near = swapped(near, 0)
    plan, scale, cross_high, cross_low, rims = call(
        functools.partial(drive_kernel, voxels),
        [
            shape((frames, neurons), F32),
            shape((8, neurons), F32),
            shape((GROUP, GROUP), BF),
            shape((GROUP, GROUP), BF),
            shape((2 * rim, neurons), BF),
        ],
        [WHOLE] * 4,
        [WHOLE] * 5,
        2 * (frames + neurons) * neurons * extended,
        scratch_shapes=[pltpu.VMEM((extended, neurons), BF)],
    )(count, recording, footprints, traces)

    new_tr, rounded = call(
        sweep_kernel,
        [pltpu.VMEM((frames, neurons), F32), pltpu.VMEM((frames, neurons), BF)],
        [WHOLE] * 7,
        [WHOLE, WHOLE],
        2 * frames * neurons * neurons * 3,
    )(plan, scale, cross_high, cross_low, rims, near, far)

    if parts == 2:
        return new_tr, halved(voxels, rim, count, recording, footprints, early[0], rounded)
    return new_tr, spread(voxels, rim, count, recording, footprints, rounded)


def solution(mesh):
    placed = (P("tm", "slab"), P(None, "slab"), P("tm", "slab"), P())
    return jax.shard_map(
        on_device,
        mesh=mesh,
        in_specs=placed,
        out_specs=(P("tm", "slab"), P("tm", "slab")),
        check_vma=False,
    )
```

```python
import functools

import jax
import jax.numpy as jnp
from jax import lax
from jax.experimental import pallas as pl
from jax.experimental.pallas import tpu as pltpu
from jax.sharding import PartitionSpec as P

GROUP = 128
EARLY = 512
BF = jnp.bfloat16
F32 = jnp.float32
WHOLE = pl.BlockSpec(memory_space=pltpu.VMEM)
LEFT_THERE = pl.BlockSpec(memory_space=pl.ANY)
COPIES = pltpu.SemaphoreType.DMA
shape = jax.ShapeDtypeStruct


def mm(left, right):
    return jnp.dot(left, right, preferred_element_type=F32)


def mm_t(left, right):
    return lax.dot_general(left, right, (((1,), (1,)), ((), ())), preferred_element_type=F32)


def t_mm(left, right):
    return lax.dot_general(left, right, (((0,), (0,)), ((), ())), preferred_element_type=F32)


def halves(wide):
    high = wide.astype(BF)
    return high, (wide - high.astype(F32)).astype(BF)


def living(count, block):
    slots = lax.broadcasted_iota(jnp.int32, block.shape, 1)
    return jnp.where(slots < count, block, jnp.zeros_like(block))


def diagonal(square):
    rows = lax.broadcasted_iota(jnp.int32, square.shape, 0)
    columns = lax.broadcasted_iota(jnp.int32, square.shape, 1)
    return jnp.sum(jnp.where(rows == columns, square, 0.0), axis=0, keepdims=True)


def at_end(axis):
    return lax.axis_index(axis) == lax.axis_size(axis) - 1


def odd_slab():
    return lax.axis_index("slab") % 2 == 1


def call(body, outs, in_specs, out_specs, flops, limit=32, **more):
    return pl.pallas_call(
        body,
        out_shape=outs,
        in_specs=in_specs,
        out_specs=out_specs,
        compiler_params=pltpu.CompilerParams(vmem_limit_bytes=limit * 1024 * 1024),
        cost_estimate=pl.CostEstimate(flops=flops, bytes_accessed=2 ** 21, transcendentals=0),
        **more,
    )


def copied(source, target, sem):
    copy = pltpu.make_async_copy(source, target, sem)
    copy.start()
    return copy


def first_column(which, voxels, rim):
    return pl.multiple_of(rim + which * (voxels // 2 - rim), 128)


def rim_kernel(voxels, live, movie, foot, start, far, near, count, *rest):
    numbers, head, tail, traces, edge, sems = rest[-6:]
    rim = head.shape[0]
    small = [
        copied(live, numbers, sems.at[0]),
        copied(start, traces, sems.at[1]),
        copied(foot.at[pl.ds(0, rim)], head, sems.at[2]),
        copied(foot.at[pl.ds(voxels, rim)], tail, sems.at[3]),
        copied(movie.at[:, pl.ds(0, rim)], edge, sems.at[4]),
    ]
    large = []
    if len(rest) > 6:
        column = first_column(1 - lax.axis_index("tm"), voxels, rim)
        large = [
            copied(movie.at[:, pl.ds(0, rim)], rest[0].at[:, pl.ds(0, rim)], sems.at[5]),
            copied(movie.at[:, pl.ds(column, EARLY)], rest[0].at[:, pl.ds(rim, EARLY)], sems.at[6]),
        ]
    for copy in small:
        copy.wait()
    alive = numbers[lax.axis_index("slab")]
    count[...] = jnp.full(count.shape, alive, jnp.int32)
    high, low = halves(living(alive, traces[...]))
    ends = jnp.where(at_end("slab"), jnp.zeros_like(tail[...]), tail[...])
    forward = mm_t(high, ends) + mm_t(low, ends)
    backward = edge[...].astype(F32) - (mm_t(high, head[...]) + mm_t(low, head[...]))
    odd = odd_slab()
    near[...] = jnp.where(odd, backward, forward).astype(BF)
    far[...] = jnp.where(odd, forward, backward).astype(BF)
    for copy in large:
        copy.wait()


def drive_kernel(
    voxels, count, movie, foot, start, plan, scale, cross_high, cross_low, rims, masked, shown, traces, sems
):
    rim = masked.shape[0] - voxels
    step = voxels // 4
    alive = count[0:1]
    last = copied(foot.at[pl.ds(voxels, rim)], masked.at[pl.ds(voxels, rim)], sems.at[0])
    loads = []
    for i in range(4):
        rows = pl.ds(i * step, step)
        loads.append((
            copied(foot.at[rows], masked.at[rows], sems.at[2 * i + 1]),
            copied(movie.at[:, rows], shown.at[:, rows], sems.at[2 * i + 2]),
        ))
    begun = copied(start, traces, sems.at[9])
    last.wait()
    ends = living(alive, masked[voxels:])
    ends = jnp.where(at_end("slab"), jnp.zeros_like(ends), ends)
    masked[voxels:] = ends
    rims[rim:] = ends
    gram = t_mm(ends, ends)
    drive = 0.0
    for i, pair in enumerate(loads):
        for load in pair:
            load.wait()
        rows = slice(i * step, (i + 1) * step)
        part = living(alive, masked[rows])
        masked[rows] = part
        gram = gram + t_mm(part, part)
        drive = drive + mm(shown[:, rows], part)
    rims[:rim] = -masked[:rim]
    inverse = 1.0 / (diagonal(gram) + 1e-06)
    scale[...] = jnp.broadcast_to(inverse, scale.shape)
    gram_high, gram_low = halves(gram)
    cross_high[...] = gram_high[:GROUP, GROUP:]
    cross_low[...] = gram_low[:GROUP, GROUP:]
    begun.wait()
    current = living(alive, traces[...])
    high, low = halves(current)
    for at in range(0, current.shape[1], GROUP):
        columns = slice(at, at + GROUP)
        coupled = mm(high[:, at:], gram_high[at:, columns]) + mm(high[:, at:], gram_low[at:, columns])
        coupled = coupled + mm(low[:, at:], gram_high[at:, columns])
        plan[:, columns] = current[:, columns] + (drive[:, columns] - coupled) * inverse[:, columns]


def sweep_kernel(plan, scale, cross_high, cross_low, rims, far, near, traces, rounded):
    odd = odd_slab()
    one, two = near[...], far[...]
    beside = jnp.concatenate([jnp.where(odd, one, two), jnp.where(odd, two, one)], axis=1)
    stepped = plan[...] + mm(beside, rims[...]) * scale[0:1]
    first = jnp.maximum(stepped[:, :GROUP], 0.0)
    high, low = halves(first)
    cross = cross_high[...]
    coupled = mm(high, cross) + mm(high, cross_low[...]) + mm(low, cross)
    second = jnp.maximum(stepped[:, GROUP:] - coupled * scale[0:1, GROUP:], 0.0)
    traces[:, :GROUP] = first
    traces[:, GROUP:] = second
    rounded[:, :GROUP] = first.astype(BF)
    rounded[:, GROUP:] = second.astype(BF)


def own_kernel(voxels, rim, movie, foot, fit, early, total, lead, quad, sent_own, seen_other, late, sem):
    here = lax.axis_index("tm")
    width = voxels // 2
    there = pl.multiple_of(first_column(1 - here, voxels, rim) + EARLY, 128)
    copy = copied(movie.at[:, pl.ds(there, width - EARLY)], late, sem)
    traces = fit[...]
    row = pl.multiple_of(jnp.where(here == 0, voxels, 0), rim)
    edge = foot[pl.ds(row, rim)]
    flat = movie[:, :rim].T.astype(F32)
    sent_own[...] = (jnp.where(here == 0, 0.0, flat) - mm_t(edge, traces)).astype(BF)
    seen_other[...] = jnp.where(here == 0, 0.0, early[:, :rim].T.astype(F32)).astype(BF)
    quad[...] = t_mm(traces, traces)
    lead[...] = jnp.where(here == 0, mm(flat.astype(BF), traces), 0.0)
    total[...] = t_mm(movie[:, pl.ds(first_column(here, voxels, rim), width)], traces)
    copy.wait()


def sent_kernel(voxels, foot, fit, sent_own, seen_other, sent):
    rim, frames = sent_own.shape
    row = pl.multiple_of(jnp.where(lax.axis_index("tm") == 0, voxels, 0), rim)
    sent[:, :frames] = sent_own[...]
    seen = seen_other[...].astype(F32) - mm_t(foot[pl.ds(row, rim)], fit[...])
    sent[:, frames:] = seen.astype(BF)


def rest_kernel(
    voxels, rim, foot, total, lead, quad, early, fit, traces, out, new_tr, base, waiting, scale, moved, sems
):
    here = lax.axis_index("tm")
    width = voxels // 2
    written = copied(traces, new_tr, sems.at[0])
    fitted = fit[...]
    square = quad[...] + t_mm(fitted, fitted)
    inverse = 1.0 / jnp.maximum(diagonal(square), 1.0)
    scale[...] = jnp.broadcast_to(inverse, scale.shape)
    high, low = halves(square)

    def settled(row, part):
        own = foot[pl.ds(pl.multiple_of(row, 128), part.shape[0])]
        return own.astype(F32) + (part - (mm(own, high) + mm(own, low))) * inverse

    row = first_column(here, voxels, rim)
    for at in range(0, EARLY, 128):
        part = total[at:at + 128] + t_mm(early[:, rim + at:rim + at + 128], fitted)
        moved[at:at + 128] = jnp.maximum(settled(row + at, part), 0.0).astype(BF)
    skip = rim // 2

    @pl.when(here == 0)
    def _():
        copied(moved, out.at[pl.ds(rim, EARLY)], sems.at[1])

    @pl.when(here == 1)
    def _():
        copied(moved.at[pl.ds(skip, EARLY - skip)], out.at[pl.ds(0, EARLY - skip)], sems.at[1])

    for at in range(EARLY, width, 128):
        waiting[at - EARLY:at - EARLY + 128] = settled(row + at, total[at:at + 128])
    part = lead[...] + jnp.where(here == 0, t_mm(early[:, :rim], fitted), 0.0)
    base[...] = settled(here * voxels, part)
    written.wait()

    @pl.when(here == 0)
    def _():
        pltpu.make_async_copy(moved, out.at[pl.ds(rim, EARLY)], sems.at[1]).wait()

    @pl.when(here == 1)
    def _():
        pltpu.make_async_copy(
            moved.at[pl.ds(skip, EARLY - skip)], out.at[pl.ds(0, EARLY - skip)], sems.at[1]
        ).wait()


def late_kernel(rim, sofar, waiting, late, fit, scale, out, moved, sem):
    here = lax.axis_index("tm")
    length = waiting.shape[0]
    skip = rim // 2
    fitted = fit[...]
    for at in range(0, length, 128):
        part = waiting[at:at + 128] + t_mm(late[:, at:at + 128], fitted) * scale[0:1]
        moved[at:at + 128] = jnp.maximum(part, 0.0).astype(BF)

    @pl.when(here == 0)
    def _():
        copied(moved.at[pl.ds(0, length - skip)], out.at[pl.ds(rim + EARLY, length - skip)], sem).wait()

    @pl.when(here == 1)
    def _():
        copied(moved, out.at[pl.ds(EARLY - skip, length)], sem).wait()


def edge_kernel(sofar, came, fit_own, fit_other, base, scale, out, moved, sem):
    frames = fit_own.shape[0]
    rim = base.shape[0]
    part = mm(came[:, :frames], fit_own[...]) + mm(came[:, frames:], fit_other[...])
    moved[...] = jnp.maximum(base[...] + part * scale[0:1], 0.0).astype(BF)
    row = pl.multiple_of(lax.axis_index("tm") * (out.shape[0] - rim), 64)
    copied(moved, out.at[pl.ds(row, rim)], sem).wait()


def halved(voxels, rim, foot, recording, early, new_tr, rounded):
    frames = recording.shape[0]
    extended, neurons = foot.shape
    slabs = lax.axis_size("slab")
    width, share = voxels // 2, extended // 2
    across = [(0, 1), (1, 0)]
    came_early = lax.ppermute(early, "tm", across)
    other = lax.ppermute(rounded, "tm", across)
    total, lead, quad, sent_own, seen_other, late = call(
        functools.partial(own_kernel, voxels, rim),
        [
            shape((width, neurons), F32),
            shape((rim, neurons), F32),
            shape((neurons, neurons), F32),
            shape((rim, frames), BF),
            shape((rim, frames), BF),
            shape((frames, width - EARLY), BF),
        ],
        [WHOLE] * 4,
        [WHOLE] * 6,
        2 * frames * neurons * (width + neurons + rim),
        scratch_shapes=[COPIES],
    )(recording, foot, rounded, came_early)
    came_late = lax.ppermute(late, "tm", across)
    sent = call(
        functools.partial(sent_kernel, voxels),
        shape((rim, 2 * frames), BF),
        [WHOLE] * 4,
        WHOLE,
        2 * frames * neurons * rim,
    )(foot, other, sent_own, seen_other)
    ahead = [(i * 2, i * 2 + 2) for i in range(slabs - 1)]
    behind = [(i * 2 + 3, i * 2 + 1) for i in range(slabs - 1)]
    came = lax.ppermute(sent, ("slab", "tm"), ahead + behind)
    sofar, new_tr, base, waiting, scale = call(
        functools.partial(rest_kernel, voxels, rim),
        [
            pltpu.HBM((share, neurons), BF),
            pltpu.HBM((frames, neurons), F32),
            shape((rim, neurons), F32),
            shape((width - EARLY, neurons), F32),
            shape((8, neurons), F32),
        ],
        [WHOLE] * 7,
        [LEFT_THERE] * 2 + [WHOLE] * 3,
        2 * neurons * (frames + 2 * neurons) * width,
        scratch_shapes=[pltpu.VMEM((EARLY, neurons), BF), COPIES((2,))],
    )(foot, total, lead, quad, came_early, other, new_tr)
    sofar = call(
        functools.partial(late_kernel, rim),
        pltpu.HBM((share, neurons), BF),
        [LEFT_THERE] + [WHOLE] * 4,
        LEFT_THERE,
        2 * neurons * frames * (width - EARLY),
        input_output_aliases={0: 0},
        scratch_shapes=[pltpu.VMEM((width - EARLY, neurons), BF), COPIES],
    )(sofar, waiting, came_late, other, scale)
    new_foot = call(
        edge_kernel,
        pltpu.HBM((share, neurons), BF),
        [LEFT_THERE] + [WHOLE] * 5,
        LEFT_THERE,
        2 * 2 * frames * neurons * rim,
        input_output_aliases={0: 0},
        scratch_shapes=[pltpu.VMEM((rim, neurons), BF), COPIES],
    )(sofar, came, rounded, other, base, scale)
    return new_tr, new_foot


def spread(voxels, rim, foot, recording, rounded):
    slabs, parts = lax.axis_size("slab"), lax.axis_size("tm")
    extended, neurons = foot.shape
    share = extended // parts
    here = lax.axis_index("tm")
    closing = here == parts - 1
    exact = lax.Precision.HIGHEST
    cut = voxels - (share - rim)
    columns = jnp.concatenate([recording[:, :cut], recording[:, :rim], recording[:, cut:]], 1)
    movie = lax.all_to_all(columns, "tm", split_axis=1, concat_axis=0, tiled=True)
    fit = lax.all_gather(rounded, "tm", axis=0, tiled=True)
    edge = jnp.where(here == 0, foot[voxels:], foot[:rim])
    seen = movie[:, :rim].astype(F32)
    sent = jnp.where(here == 0, 0.0, seen) - mm_t(fit, edge)
    ahead = [(i * parts, (i + 1) * parts) for i in range(slabs - 1)]
    behind = [((i + 2) * parts - 1, (i + 1) * parts - 1) for i in range(slabs - 1)]
    lead = jnp.where(closing, 0.0, seen) + lax.ppermute(sent, ("slab", "tm"), ahead + behind)
    lead = lax.dot_general(lead, fit.astype(F32), (((0,), (0,)), ((), ())), precision=exact)
    inner = t_mm(movie[:, rim:], fit)
    total = jnp.where(
        closing, jnp.concatenate([inner, lead], 0), jnp.concatenate([lead, inner], 0)
    )
    square = t_mm(fit, fit)
    own = lax.dynamic_slice_in_dim(foot, here * share, share, 0).astype(F32)
    total = total - jnp.dot(own, square, precision=exact)
    return jnp.maximum(own + total / jnp.maximum(jnp.diagonal(square), 1.0), 0.0).astype(BF)


def on_device(recording, footprints, traces, live_count):
    slabs, parts = lax.axis_size("slab"), lax.axis_size("tm")
    frames, voxels = recording.shape
    extended, neurons = footprints.shape
    rim = extended - voxels
    early_shape = [pltpu.VMEM((frames, rim + EARLY), BF)] if parts == 2 else []
    pinned = [
        pltpu.with_memory_space_constraint(x, pltpu.HBM)
        for x in (live_count, recording, footprints, traces)
    ]
    far, near, count, *early = call(
        functools.partial(rim_kernel, voxels),
        [
            pltpu.VMEM((frames, rim), BF),
            pltpu.VMEM((frames, rim), BF),
            pltpu.VMEM((8, neurons), jnp.int32),
        ]
        + early_shape,
        [LEFT_THERE] * 4,
        [WHOLE] * (3 + len(early_shape)),
        2 * frames * neurons * rim * 4,
        scratch_shapes=[
            pltpu.SMEM(live_count.shape, jnp.int32),
            pltpu.VMEM((rim, neurons), BF),
            pltpu.VMEM((rim, neurons), BF),
            pltpu.VMEM((frames, neurons), F32),
            pltpu.VMEM((frames, rim), BF),
            COPIES((7,)),
        ],
    )(*pinned)
    def swapped(block, first):
        route = [(i, i + 1) for i in range(first, slabs - 1, 2)]
        return lax.ppermute(block, "slab", route + [(j, i) for i, j in route])

    far = swapped(far, 1)
    near = swapped(near, 0)
    plan, scale, cross_high, cross_low, rims, masked, shown = call(
        functools.partial(drive_kernel, voxels),
        [
            shape((frames, neurons), F32),
            shape((8, neurons), F32),
            shape((GROUP, GROUP), BF),
            shape((GROUP, GROUP), BF),
            shape((2 * rim, neurons), BF),
            pltpu.VMEM((extended, neurons), BF),
            pltpu.VMEM((frames, voxels), BF),
        ],
        [WHOLE] + [LEFT_THERE] * 3,
        [WHOLE] * 7,
        2 * (frames + neurons) * neurons * extended,
        scratch_shapes=[pltpu.VMEM((frames, neurons), F32), COPIES((10,))],
    )(count, *pinned[1:])

    new_tr, rounded = call(
        sweep_kernel,
        [pltpu.VMEM((frames, neurons), F32), pltpu.VMEM((frames, neurons), BF)],
        [WHOLE] * 7,
        [WHOLE, WHOLE],
        2 * frames * neurons * neurons * 3,
    )(plan, scale, cross_high, cross_low, rims, far, near)

    if parts == 2:
        return halved(voxels, rim, masked, shown, early[0], new_tr, rounded)
    return new_tr, spread(voxels, rim, masked, recording, rounded)


def solution(mesh):
    placed = (P("tm", "slab"), P(None, "slab"), P("tm", "slab"), P())
    return jax.shard_map(
        on_device,
        mesh=mesh,
        in_specs=placed,
        out_specs=(P("tm", "slab"), P("tm", "slab")),
        check_vma=False,
    )
```

```python
import functools

import jax
import jax.numpy as jnp
from jax import lax
from jax.experimental import pallas as pl
from jax.experimental.pallas import tpu as pltpu
from jax.sharding import PartitionSpec as P

GROUP = 128
EARLY = 512
BF = jnp.bfloat16
F32 = jnp.float32
WHOLE = pl.BlockSpec(memory_space=pltpu.VMEM)
LEFT_THERE = pl.BlockSpec(memory_space=pl.ANY)
COPIES = pltpu.SemaphoreType.DMA
shape = jax.ShapeDtypeStruct


def mm(left, right):
    return jnp.dot(left, right, preferred_element_type=F32)


def mm_t(left, right):
    return lax.dot_general(left, right, (((1,), (1,)), ((), ())), preferred_element_type=F32)


def t_mm(left, right):
    return lax.dot_general(left, right, (((0,), (0,)), ((), ())), preferred_element_type=F32)


def halves(wide):
    high = wide.astype(BF)
    return high, (wide - high.astype(F32)).astype(BF)


def living(count, block):
    slots = lax.broadcasted_iota(jnp.int32, block.shape, 1)
    return jnp.where(slots < count, block, jnp.zeros_like(block))


def diagonal(square):
    rows = lax.broadcasted_iota(jnp.int32, square.shape, 0)
    columns = lax.broadcasted_iota(jnp.int32, square.shape, 1)
    return jnp.sum(jnp.where(rows == columns, square, 0.0), axis=0, keepdims=True)


def at_end(axis):
    return lax.axis_index(axis) == lax.axis_size(axis) - 1


def odd_slab():
    return lax.axis_index("slab") % 2 == 1


def call(body, outs, in_specs, out_specs, expected, **more):
    return pl.pallas_call(
        body,
        out_shape=outs,
        in_specs=in_specs,
        out_specs=out_specs,
        compiler_params=pltpu.CompilerParams(vmem_limit_bytes=32 * 1024 * 1024),
        cost_estimate=pl.CostEstimate(
            flops=0, bytes_accessed=int(expected * 3_690_000), transcendentals=0
        ),
        **more,
    )


def copied(source, target, sem):
    copy = pltpu.make_async_copy(source, target, sem)
    copy.start()
    return copy


def first_column(which, voxels, rim):
    return pl.multiple_of(rim + which * (voxels // 2 - rim), 128)


def rim_kernel(voxels, live, movie, foot, start, far, near, count, *rest):
    numbers, head, tail, traces, edge, sems = rest[-6:]
    rim = head.shape[0]
    small = [
        copied(live, numbers, sems.at[0]),
        copied(start, traces, sems.at[1]),
        copied(foot.at[pl.ds(0, rim)], head, sems.at[2]),
        copied(foot.at[pl.ds(voxels, rim)], tail, sems.at[3]),
        copied(movie.at[:, pl.ds(0, rim)], edge, sems.at[4]),
    ]
    large = []
    if len(rest) > 6:
        column = first_column(1 - lax.axis_index("tm"), voxels, rim)
        large = [
            copied(movie.at[:, pl.ds(0, rim)], rest[0].at[:, pl.ds(0, rim)], sems.at[5]),
            copied(movie.at[:, pl.ds(column, EARLY)], rest[0].at[:, pl.ds(rim, EARLY)], sems.at[6]),
        ]
    for copy in small:
        copy.wait()
    alive = numbers[lax.axis_index("slab")]
    count[...] = jnp.full(count.shape, alive, jnp.int32)
    high, low = halves(living(alive, traces[...]))
    ends = jnp.where(at_end("slab"), jnp.zeros_like(tail[...]), tail[...])
    forward = mm_t(high, ends) + mm_t(low, ends)
    backward = edge[...].astype(F32) - (mm_t(high, head[...]) + mm_t(low, head[...]))
    odd = odd_slab()
    near[...] = jnp.where(odd, backward, forward).astype(BF)
    far[...] = jnp.where(odd, forward, backward).astype(BF)
    for copy in large:
        copy.wait()


def drive_kernel(voxels, count, movie, foot, start, plan, scale, cross_high, cross_low, rims, masked):
    rim = foot.shape[0] - voxels
    alive = count[0:1]
    masked[:voxels] = living(alive, foot[:voxels])
    ends = living(alive, foot[voxels:])
    masked[voxels:] = jnp.where(at_end("slab"), jnp.zeros_like(ends), ends)
    rims[:rim] = -masked[:rim]
    rims[rim:] = masked[voxels:]
    drive = mm(movie[...], masked[:voxels])
    gram = t_mm(masked[...], masked[...])
    inverse = 1.0 / (diagonal(gram) + 1e-06)
    scale[...] = jnp.broadcast_to(inverse, scale.shape)
    gram_high, gram_low = halves(gram)
    cross_high[...] = gram_high[:GROUP, GROUP:]
    cross_low[...] = gram_low[:GROUP, GROUP:]
    current = living(alive, start[...])
    high, low = halves(current)
    for at in range(0, current.shape[1], GROUP):
        columns = slice(at, at + GROUP)
        coupled = mm(high[:, at:], gram_high[at:, columns]) + mm(high[:, at:], gram_low[at:, columns])
        coupled = coupled + mm(low[:, at:], gram_high[at:, columns])
        plan[:, columns] = current[:, columns] + (drive[:, columns] - coupled) * inverse[:, columns]


def sweep_kernel(plan, scale, cross_high, cross_low, rims, far, near, traces, rounded):
    odd = odd_slab()
    one, two = near[...], far[...]
    beside = jnp.concatenate([jnp.where(odd, one, two), jnp.where(odd, two, one)], axis=1)
    stepped = plan[...] + mm(beside, rims[...]) * scale[0:1]
    first = jnp.maximum(stepped[:, :GROUP], 0.0)
    high, low = halves(first)
    cross = cross_high[...]
    coupled = mm(high, cross) + mm(high, cross_low[...]) + mm(low, cross)
    second = jnp.maximum(stepped[:, GROUP:] - coupled * scale[0:1, GROUP:], 0.0)
    traces[:, :GROUP] = first
    traces[:, GROUP:] = second
    rounded[:, :GROUP] = first.astype(BF)
    rounded[:, GROUP:] = second.astype(BF)


def own_kernel(voxels, rim, movie, foot, fit, early, total, lead, quad, sent_own, seen_other, late, sem):
    here = lax.axis_index("tm")
    width = voxels // 2
    there = pl.multiple_of(first_column(1 - here, voxels, rim) + EARLY, 128)
    copy = copied(movie.at[:, pl.ds(there, width - EARLY)], late, sem)
    traces = fit[...]
    row = pl.multiple_of(jnp.where(here == 0, voxels, 0), rim)
    edge = foot[pl.ds(row, rim)]
    flat = movie[:, :rim].T.astype(F32)
    sent_own[...] = (jnp.where(here == 0, 0.0, flat) - mm_t(edge, traces)).astype(BF)
    seen_other[...] = jnp.where(here == 0, 0.0, early[:, :rim].T.astype(F32)).astype(BF)
    quad[...] = t_mm(traces, traces)
    lead[...] = jnp.where(here == 0, mm(flat.astype(BF), traces), 0.0)
    total[...] = t_mm(movie[:, pl.ds(first_column(here, voxels, rim), width)], traces)
    copy.wait()


def sent_kernel(voxels, foot, fit, sent_own, seen_other, sent):
    rim, frames = sent_own.shape
    row = pl.multiple_of(jnp.where(lax.axis_index("tm") == 0, voxels, 0), rim)
    sent[:, :frames] = sent_own[...]
    seen = seen_other[...].astype(F32) - mm_t(foot[pl.ds(row, rim)], fit[...])
    sent[:, frames:] = seen.astype(BF)


def settled(foot, row, part, high, low, inverse):
    own = foot[pl.ds(pl.multiple_of(row, 128), part.shape[0])]
    return own.astype(F32) + (part - (mm(own, high) + mm(own, low))) * inverse


def level_kernel(voxels, rim, foot, total, lead, quad, early, fit, scale, high, low, base, waiting):
    here = lax.axis_index("tm")
    fitted = fit[...]
    square = quad[...] + t_mm(fitted, fitted)
    inverse = 1.0 / jnp.maximum(diagonal(square), 1.0)
    scale[...] = jnp.broadcast_to(inverse, scale.shape)
    high[...], low[...] = halves(square)
    row = first_column(here, voxels, rim)
    for at in range(EARLY, voxels // 2, 128):
        waiting[at - EARLY:at - EARLY + 128] = settled(
            foot, row + at, total[at:at + 128], high[...], low[...], inverse
        )
    part = lead[...] + jnp.where(here == 0, t_mm(early[:, :rim], fitted), 0.0)
    base[...] = settled(foot, here * voxels, part, high[...], low[...], inverse)


def early_kernel(voxels, rim, foot, total, early, fit, scale, high, low, traces, out, new_tr, moved, sems):
    here = lax.axis_index("tm")
    written = copied(traces, new_tr, sems.at[0])
    fitted = fit[...]
    row = first_column(here, voxels, rim)
    for at in range(0, EARLY, 128):
        part = total[at:at + 128] + t_mm(early[:, rim + at:rim + at + 128], fitted)
        part = settled(foot, row + at, part, high[...], low[...], scale[0:1])
        moved[at:at + 128] = jnp.maximum(part, 0.0).astype(BF)
    skip = rim // 2

    @pl.when(here == 0)
    def _():
        copied(moved, out.at[pl.ds(rim, EARLY)], sems.at[1]).wait()

    @pl.when(here == 1)
    def _():
        copied(moved.at[pl.ds(skip, EARLY - skip)], out.at[pl.ds(0, EARLY - skip)], sems.at[1]).wait()

    written.wait()


def late_kernel(rim, sofar, waiting, late, fit, scale, out, moved, sem):
    here = lax.axis_index("tm")
    length = waiting.shape[0]
    skip = rim // 2
    fitted = fit[...]
    for at in range(0, length, 128):
        part = waiting[at:at + 128] + t_mm(late[:, at:at + 128], fitted) * scale[0:1]
        moved[at:at + 128] = jnp.maximum(part, 0.0).astype(BF)

    @pl.when(here == 0)
    def _():
        copied(moved.at[pl.ds(0, length - skip)], out.at[pl.ds(rim + EARLY, length - skip)], sem).wait()

    @pl.when(here == 1)
    def _():
        copied(moved, out.at[pl.ds(EARLY - skip, length)], sem).wait()


def edge_kernel(sofar, came, fit_own, fit_other, base, scale, out, moved, sem):
    frames = fit_own.shape[0]
    rim = base.shape[0]
    part = mm(came[:, :frames], fit_own[...]) + mm(came[:, frames:], fit_other[...])
    moved[...] = jnp.maximum(base[...] + part * scale[0:1], 0.0).astype(BF)
    row = pl.multiple_of(lax.axis_index("tm") * (out.shape[0] - rim), 64)
    copied(moved, out.at[pl.ds(row, rim)], sem).wait()


def halved(voxels, rim, foot, recording, early, new_tr, rounded):
    frames = recording.shape[0]
    extended, neurons = foot.shape
    slabs = lax.axis_size("slab")
    width, share = voxels // 2, extended // 2
    across = [(0, 1), (1, 0)]
    came_early = lax.ppermute(early, "tm", across)
    other = lax.ppermute(rounded, "tm", across)
    total, lead, quad, sent_own, seen_other, late = call(
        functools.partial(own_kernel, voxels, rim),
        [
            shape((width, neurons), F32),
            shape((rim, neurons), F32),
            shape((neurons, neurons), F32),
            shape((rim, frames), BF),
            shape((rim, frames), BF),
            shape((frames, width - EARLY), BF),
        ],
        [WHOLE] * 4,
        [WHOLE] * 6,
        0.5,
        scratch_shapes=[COPIES],
    )(recording, foot, rounded, came_early)
    came_late = lax.ppermute(late, "tm", across)
    sent = call(
        functools.partial(sent_kernel, voxels),
        shape((rim, 2 * frames), BF),
        [WHOLE] * 4,
        WHOLE,
        0.2,
    )(foot, other, sent_own, seen_other)
    ahead = [(i * 2, i * 2 + 2) for i in range(slabs - 1)]
    behind = [(i * 2 + 3, i * 2 + 1) for i in range(slabs - 1)]
    came = lax.ppermute(sent, ("slab", "tm"), ahead + behind)
    scale, high, low, base, waiting = call(
        functools.partial(level_kernel, voxels, rim),
        [
            shape((8, neurons), F32),
            shape((neurons, neurons), BF),
            shape((neurons, neurons), BF),
            shape((rim, neurons), F32),
            shape((width - EARLY, neurons), F32),
        ],
        [WHOLE] * 6,
        [WHOLE] * 5,
        0.8,
    )(foot, total, lead, quad, came_early, other)
    sofar, new_tr = call(
        functools.partial(early_kernel, voxels, rim),
        [pltpu.HBM((share, neurons), BF), pltpu.HBM((frames, neurons), F32)],
        [WHOLE] * 8,
        [LEFT_THERE] * 2,
        1.2,
        scratch_shapes=[pltpu.VMEM((EARLY, neurons), BF), COPIES((2,))],
    )(foot, total, came_early, other, scale, high, low, new_tr)
    sofar = call(
        functools.partial(late_kernel, rim),
        pltpu.HBM((share, neurons), BF),
        [LEFT_THERE] + [WHOLE] * 4,
        LEFT_THERE,
        1.0,
        input_output_aliases={0: 0},
        scratch_shapes=[pltpu.VMEM((width - EARLY, neurons), BF), COPIES],
    )(sofar, waiting, came_late, other, scale)
    new_foot = call(
        edge_kernel,
        pltpu.HBM((share, neurons), BF),
        [LEFT_THERE] + [WHOLE] * 5,
        LEFT_THERE,
        0.8,
        input_output_aliases={0: 0},
        scratch_shapes=[pltpu.VMEM((rim, neurons), BF), COPIES],
    )(sofar, came, rounded, other, base, scale)
    return new_tr, new_foot


def spread(voxels, rim, foot, recording, rounded):
    slabs, parts = lax.axis_size("slab"), lax.axis_size("tm")
    extended, neurons = foot.shape
    share = extended // parts
    here = lax.axis_index("tm")
    closing = here == parts - 1
    exact = lax.Precision.HIGHEST
    cut = voxels - (share - rim)
    columns = jnp.concatenate([recording[:, :cut], recording[:, :rim], recording[:, cut:]], 1)
    movie = lax.all_to_all(columns, "tm", split_axis=1, concat_axis=0, tiled=True)
    fit = lax.all_gather(rounded, "tm", axis=0, tiled=True)
    edge = jnp.where(here == 0, foot[voxels:], foot[:rim])
    seen = movie[:, :rim].astype(F32)
    sent = jnp.where(here == 0, 0.0, seen) - mm_t(fit, edge)
    ahead = [(i * parts, (i + 1) * parts) for i in range(slabs - 1)]
    behind = [((i + 2) * parts - 1, (i + 1) * parts - 1) for i in range(slabs - 1)]
    lead = jnp.where(closing, 0.0, seen) + lax.ppermute(sent, ("slab", "tm"), ahead + behind)
    lead = lax.dot_general(lead, fit.astype(F32), (((0,), (0,)), ((), ())), precision=exact)
    inner = t_mm(movie[:, rim:], fit)
    total = jnp.where(
        closing, jnp.concatenate([inner, lead], 0), jnp.concatenate([lead, inner], 0)
    )
    square = t_mm(fit, fit)
    own = lax.dynamic_slice_in_dim(foot, here * share, share, 0).astype(F32)
    total = total - jnp.dot(own, square, precision=exact)
    return jnp.maximum(own + total / jnp.maximum(jnp.diagonal(square), 1.0), 0.0).astype(BF)


def on_device(recording, footprints, traces, live_count):
    slabs, parts = lax.axis_size("slab"), lax.axis_size("tm")
    frames, voxels = recording.shape
    extended, neurons = footprints.shape
    rim = extended - voxels
    early_shape = [pltpu.VMEM((frames, rim + EARLY), BF)] if parts == 2 else []
    pinned = [
        pltpu.with_memory_space_constraint(x, pltpu.HBM)
        for x in (live_count, recording, footprints, traces)
    ]
    far, near, count, *early = call(
        functools.partial(rim_kernel, voxels),
        [
            pltpu.VMEM((frames, rim), BF),
            pltpu.VMEM((frames, rim), BF),
            pltpu.VMEM((8, neurons), jnp.int32),
        ]
        + early_shape,
        [LEFT_THERE] * 4,
        [WHOLE] * (3 + len(early_shape)),
        1.5,
        scratch_shapes=[
            pltpu.SMEM(live_count.shape, jnp.int32),
            pltpu.VMEM((rim, neurons), BF),
            pltpu.VMEM((rim, neurons), BF),
            pltpu.VMEM((frames, neurons), F32),
            pltpu.VMEM((frames, rim), BF),
            COPIES((7,)),
        ],
    )(*pinned)
    def swapped(block, first):
        route = [(i, i + 1) for i in range(first, slabs - 1, 2)]
        return lax.ppermute(block, "slab", route + [(j, i) for i, j in route])

    far = swapped(far, 1)
    near = swapped(near, 0)
    plan, scale, cross_high, cross_low, rims, masked = call(
        functools.partial(drive_kernel, voxels),
        [
            shape((frames, neurons), F32),
            shape((8, neurons), F32),
            shape((GROUP, GROUP), BF),
            shape((GROUP, GROUP), BF),
            shape((2 * rim, neurons), BF),
            pltpu.VMEM((extended, neurons), BF),
        ],
        [WHOLE] * 4,
        [WHOLE] * 6,
        1.2,
    )(count, recording, footprints, traces)

    new_tr, rounded = call(
        sweep_kernel,
        [pltpu.VMEM((frames, neurons), F32), pltpu.VMEM((frames, neurons), BF)],
        [WHOLE] * 7,
        [WHOLE, WHOLE],
        0.4,
    )(plan, scale, cross_high, cross_low, rims, far, near)

    if parts == 2:
        return halved(voxels, rim, masked, recording, early[0], new_tr, rounded)
    return new_tr, spread(voxels, rim, masked, recording, rounded)


def solution(mesh):
    placed = (P("tm", "slab"), P(None, "slab"), P("tm", "slab"), P())
    return jax.shard_map(
        on_device,
        mesh=mesh,
        in_specs=placed,
        out_specs=(P("tm", "slab"), P("tm", "slab")),
        check_vma=False,
    )
```

```python
import functools

import jax
import jax.numpy as jnp
from jax import lax
from jax.experimental import pallas as pl
from jax.experimental.pallas import tpu as pltpu
from jax.sharding import PartitionSpec as P

GROUP = 128
EARLY = 512
BF = jnp.bfloat16
F32 = jnp.float32
WHOLE = pl.BlockSpec(memory_space=pltpu.VMEM)
LEFT_THERE = pl.BlockSpec(memory_space=pl.ANY)
COPIES = pltpu.SemaphoreType.DMA
shape = jax.ShapeDtypeStruct


def mm(left, right):
    return jnp.dot(left, right, preferred_element_type=F32)


def mm_t(left, right):
    return lax.dot_general(left, right, (((1,), (1,)), ((), ())), preferred_element_type=F32)


def t_mm(left, right):
    return lax.dot_general(left, right, (((0,), (0,)), ((), ())), preferred_element_type=F32)


def halves(wide):
    high = wide.astype(BF)
    return high, (wide - high.astype(F32)).astype(BF)


def living(count, block):
    slots = lax.broadcasted_iota(jnp.int32, block.shape, 1)
    return jnp.where(slots < count, block, jnp.zeros_like(block))


def diagonal(square):
    rows = lax.broadcasted_iota(jnp.int32, square.shape, 0)
    columns = lax.broadcasted_iota(jnp.int32, square.shape, 1)
    return jnp.sum(jnp.where(rows == columns, square, 0.0), axis=0, keepdims=True)


def at_end(axis):
    return lax.axis_index(axis) == lax.axis_size(axis) - 1


def odd_slab():
    return lax.axis_index("slab") % 2 == 1


def call(body, outs, in_specs, out_specs, expected, **more):
    return pl.pallas_call(
        body,
        out_shape=outs,
        in_specs=in_specs,
        out_specs=out_specs,
        compiler_params=pltpu.CompilerParams(vmem_limit_bytes=32 * 1024 * 1024),
        cost_estimate=pl.CostEstimate(
            flops=0, bytes_accessed=int(expected * 3_690_000), transcendentals=0
        ),
        **more,
    )


def copied(source, target, sem):
    copy = pltpu.make_async_copy(source, target, sem)
    copy.start()
    return copy


def first_column(which, voxels, rim):
    return pl.multiple_of(rim + which * (voxels // 2 - rim), 128)


def rim_kernel(voxels, live, movie, foot, start, far, near, count, *rest):
    numbers, head, tail, traces, edge, sems = rest[-6:]
    rim = head.shape[0]
    small = [
        copied(live, numbers, sems.at[0]),
        copied(start, traces, sems.at[1]),
        copied(foot.at[pl.ds(0, rim)], head, sems.at[2]),
        copied(foot.at[pl.ds(voxels, rim)], tail, sems.at[3]),
        copied(movie.at[:, pl.ds(0, rim)], edge, sems.at[4]),
    ]
    large = []
    if len(rest) > 6:
        column = first_column(1 - lax.axis_index("tm"), voxels, rim)
        large = [
            copied(movie.at[:, pl.ds(0, rim)], rest[0].at[:, pl.ds(0, rim)], sems.at[5]),
            copied(movie.at[:, pl.ds(column, EARLY)], rest[0].at[:, pl.ds(rim, EARLY)], sems.at[6]),
        ]
    for copy in small:
        copy.wait()
    alive = numbers[lax.axis_index("slab")]
    count[...] = jnp.full(count.shape, alive, jnp.int32)
    high, low = halves(living(alive, traces[...]))
    ends = jnp.where(at_end("slab"), jnp.zeros_like(tail[...]), tail[...])
    forward = mm_t(high, ends) + mm_t(low, ends)
    backward = edge[...].astype(F32) - (mm_t(high, head[...]) + mm_t(low, head[...]))
    odd = odd_slab()
    near[...] = jnp.where(odd, backward, forward).astype(BF)
    far[...] = jnp.where(odd, forward, backward).astype(BF)
    for copy in large:
        copy.wait()


def drive_kernel(voxels, count, movie, foot, start, plan, scale, cross_high, cross_low, rims, masked):
    rim = foot.shape[0] - voxels
    alive = count[0:1]
    masked[:voxels] = living(alive, foot[:voxels])
    ends = living(alive, foot[voxels:])
    masked[voxels:] = jnp.where(at_end("slab"), jnp.zeros_like(ends), ends)
    rims[:rim] = -masked[:rim]
    rims[rim:] = masked[voxels:]
    drive = mm(movie[...], masked[:voxels])
    gram = t_mm(masked[...], masked[...])
    inverse = 1.0 / (diagonal(gram) + 1e-06)
    scale[...] = jnp.broadcast_to(inverse, scale.shape)
    gram_high, gram_low = halves(gram)
    cross_high[...] = gram_high[:GROUP, GROUP:]
    cross_low[...] = gram_low[:GROUP, GROUP:]
    current = living(alive, start[...])
    high, low = halves(current)
    for at in range(0, current.shape[1], GROUP):
        columns = slice(at, at + GROUP)
        coupled = mm(high[:, at:], gram_high[at:, columns]) + mm(high[:, at:], gram_low[at:, columns])
        coupled = coupled + mm(low[:, at:], gram_high[at:, columns])
        plan[:, columns] = current[:, columns] + (drive[:, columns] - coupled) * inverse[:, columns]


def sweep_kernel(plan, scale, cross_high, cross_low, rims, far, near, traces, rounded):
    odd = odd_slab()
    one, two = near[...], far[...]
    beside = jnp.concatenate([jnp.where(odd, one, two), jnp.where(odd, two, one)], axis=1)
    stepped = plan[...] + mm(beside, rims[...]) * scale[0:1]
    first = jnp.maximum(stepped[:, :GROUP], 0.0)
    high, low = halves(first)
    cross = cross_high[...]
    coupled = mm(high, cross) + mm(high, cross_low[...]) + mm(low, cross)
    second = jnp.maximum(stepped[:, GROUP:] - coupled * scale[0:1, GROUP:], 0.0)
    traces[:, :GROUP] = first
    traces[:, GROUP:] = second
    rounded[:, :GROUP] = first.astype(BF)
    rounded[:, GROUP:] = second.astype(BF)


def own_kernel(voxels, rim, movie, foot, fit, early, total, lead, quad, sent_own, seen_other, late, sem):
    here = lax.axis_index("tm")
    width = voxels // 2
    there = pl.multiple_of(first_column(1 - here, voxels, rim) + EARLY, 128)
    copy = copied(movie.at[:, pl.ds(there, width - EARLY)], late, sem)
    traces = fit[...]
    row = pl.multiple_of(jnp.where(here == 0, voxels, 0), rim)
    edge = foot[pl.ds(row, rim)]
    flat = movie[:, :rim].T.astype(F32)
    sent_own[...] = (jnp.where(here == 0, 0.0, flat) - mm_t(edge, traces)).astype(BF)
    seen_other[...] = jnp.where(here == 0, 0.0, early[:, :rim].T.astype(F32)).astype(BF)
    quad[...] = t_mm(traces, traces)
    lead[...] = jnp.where(here == 0, mm(flat.astype(BF), traces), 0.0)
    total[...] = t_mm(movie[:, pl.ds(first_column(here, voxels, rim), width)], traces)
    copy.wait()


def sent_kernel(voxels, foot, fit, sent_own, seen_other, sent):
    rim, frames = sent_own.shape
    row = pl.multiple_of(jnp.where(lax.axis_index("tm") == 0, voxels, 0), rim)
    sent[:, :frames] = sent_own[...]
    seen = seen_other[...].astype(F32) - mm_t(foot[pl.ds(row, rim)], fit[...])
    sent[:, frames:] = seen.astype(BF)


def settled(foot, row, part, high, low, inverse):
    own = foot[pl.ds(pl.multiple_of(row, 128), part.shape[0])]
    return own.astype(F32) + (part - (mm(own, high) + mm(own, low))) * inverse


def level_kernel(voxels, rim, foot, total, lead, quad, early, fit, scale, high, low, base, waiting):
    here = lax.axis_index("tm")
    fitted = fit[...]
    square = quad[...] + t_mm(fitted, fitted)
    inverse = 1.0 / jnp.maximum(diagonal(square), 1.0)
    scale[...] = jnp.broadcast_to(inverse, scale.shape)
    high[...], low[...] = halves(square)
    row = first_column(here, voxels, rim)
    for at in range(EARLY, voxels // 2, 128):
        waiting[at - EARLY:at - EARLY + 128] = settled(
            foot, row + at, total[at:at + 128], high[...], low[...], inverse
        )
    part = lead[...] + jnp.where(here == 0, t_mm(early[:, :rim], fitted), 0.0)
    base[...] = settled(foot, here * voxels, part, high[...], low[...], inverse)


def early_kernel(voxels, rim, foot, total, early, fit, scale, high, low, traces, out, new_tr, moved, sems):
    here = lax.axis_index("tm")
    written = copied(traces, new_tr, sems.at[0])
    fitted = fit[...]
    row = first_column(here, voxels, rim)
    for at in range(0, EARLY, 128):
        part = total[at:at + 128] + t_mm(early[:, rim + at:rim + at + 128], fitted)
        part = settled(foot, row + at, part, high[...], low[...], scale[0:1])
        moved[at:at + 128] = jnp.maximum(part, 0.0).astype(BF)
    skip = rim // 2

    @pl.when(here == 0)
    def _():
        copied(moved, out.at[pl.ds(rim, EARLY)], sems.at[1]).wait()

    @pl.when(here == 1)
    def _():
        copied(moved.at[pl.ds(skip, EARLY - skip)], out.at[pl.ds(0, EARLY - skip)], sems.at[1]).wait()

    written.wait()


def late_kernel(rim, sofar, waiting, late, fit, scale, out, moved, sem):
    here = lax.axis_index("tm")
    length = waiting.shape[0]
    skip = rim // 2
    fitted = fit[...]
    for at in range(0, length, 128):
        part = waiting[at:at + 128] + t_mm(late[:, at:at + 128], fitted) * scale[0:1]
        moved[at:at + 128] = jnp.maximum(part, 0.0).astype(BF)

    @pl.when(here == 0)
    def _():
        copied(moved.at[pl.ds(0, length - skip)], out.at[pl.ds(rim + EARLY, length - skip)], sem).wait()

    @pl.when(here == 1)
    def _():
        copied(moved, out.at[pl.ds(EARLY - skip, length)], sem).wait()


def edge_kernel(sofar, came, fit_own, fit_other, base, scale, out, moved, sem):
    frames = fit_own.shape[0]
    rim = base.shape[0]
    part = mm(came[:, :frames], fit_own[...]) + mm(came[:, frames:], fit_other[...])
    moved[...] = jnp.maximum(base[...] + part * scale[0:1], 0.0).astype(BF)
    row = pl.multiple_of(lax.axis_index("tm") * (out.shape[0] - rim), 64)
    copied(moved, out.at[pl.ds(row, rim)], sem).wait()


def halved(voxels, rim, foot, recording, early, new_tr, rounded):
    frames = recording.shape[0]
    extended, neurons = foot.shape
    slabs = lax.axis_size("slab")
    width, share = voxels // 2, extended // 2
    across = [(0, 1), (1, 0)]
    came_early = lax.ppermute(early, "tm", across)
    other = lax.ppermute(rounded, "tm", across)
    total, lead, quad, sent_own, seen_other, late = call(
        functools.partial(own_kernel, voxels, rim),
        [
            shape((width, neurons), F32),
            shape((rim, neurons), F32),
            shape((neurons, neurons), F32),
            shape((rim, frames), BF),
            shape((rim, frames), BF),
            shape((frames, width - EARLY), BF),
        ],
        [WHOLE] * 4,
        [WHOLE] * 6,
        0.5,
        scratch_shapes=[COPIES],
    )(recording, foot, rounded, came_early)
    late, other = lax.optimization_barrier((late, other))
    came_late = lax.ppermute(late, "tm", across)
    sent = call(
        functools.partial(sent_kernel, voxels),
        shape((rim, 2 * frames), BF),
        [WHOLE] * 4,
        WHOLE,
        0.2,
    )(foot, other, sent_own, seen_other)
    ahead = [(i * 2, i * 2 + 2) for i in range(slabs - 1)]
    behind = [(i * 2 + 3, i * 2 + 1) for i in range(slabs - 1)]
    came = lax.ppermute(sent, ("slab", "tm"), ahead + behind)
    scale, high, low, base, waiting = call(
        functools.partial(level_kernel, voxels, rim),
        [
            shape((8, neurons), F32),
            shape((neurons, neurons), BF),
            shape((neurons, neurons), BF),
            shape((rim, neurons), F32),
            shape((width - EARLY, neurons), F32),
        ],
        [WHOLE] * 6,
        [WHOLE] * 5,
        0.8,
    )(foot, total, lead, quad, came_early, other)
    sofar, new_tr = call(
        functools.partial(early_kernel, voxels, rim),
        [pltpu.HBM((share, neurons), BF), pltpu.HBM((frames, neurons), F32)],
        [WHOLE] * 8,
        [LEFT_THERE] * 2,
        1.2,
        scratch_shapes=[pltpu.VMEM((EARLY, neurons), BF), COPIES((2,))],
    )(foot, total, came_early, other, scale, high, low, new_tr)
    sofar = call(
        functools.partial(late_kernel, rim),
        pltpu.HBM((share, neurons), BF),
        [LEFT_THERE] + [WHOLE] * 4,
        LEFT_THERE,
        1.0,
        input_output_aliases={0: 0},
        scratch_shapes=[pltpu.VMEM((width - EARLY, neurons), BF), COPIES],
    )(sofar, waiting, came_late, other, scale)
    new_foot = call(
        edge_kernel,
        pltpu.HBM((share, neurons), BF),
        [LEFT_THERE] + [WHOLE] * 5,
        LEFT_THERE,
        0.8,
        input_output_aliases={0: 0},
        scratch_shapes=[pltpu.VMEM((rim, neurons), BF), COPIES],
    )(sofar, came, rounded, other, base, scale)
    return new_tr, new_foot


def spread(voxels, rim, foot, recording, rounded):
    slabs, parts = lax.axis_size("slab"), lax.axis_size("tm")
    extended, neurons = foot.shape
    share = extended // parts
    here = lax.axis_index("tm")
    closing = here == parts - 1
    exact = lax.Precision.HIGHEST
    cut = voxels - (share - rim)
    columns = jnp.concatenate([recording[:, :cut], recording[:, :rim], recording[:, cut:]], 1)
    movie = lax.all_to_all(columns, "tm", split_axis=1, concat_axis=0, tiled=True)
    fit = lax.all_gather(rounded, "tm", axis=0, tiled=True)
    edge = jnp.where(here == 0, foot[voxels:], foot[:rim])
    seen = movie[:, :rim].astype(F32)
    sent = jnp.where(here == 0, 0.0, seen) - mm_t(fit, edge)
    ahead = [(i * parts, (i + 1) * parts) for i in range(slabs - 1)]
    behind = [((i + 2) * parts - 1, (i + 1) * parts - 1) for i in range(slabs - 1)]
    lead = jnp.where(closing, 0.0, seen) + lax.ppermute(sent, ("slab", "tm"), ahead + behind)
    lead = lax.dot_general(lead, fit.astype(F32), (((0,), (0,)), ((), ())), precision=exact)
    inner = t_mm(movie[:, rim:], fit)
    total = jnp.where(
        closing, jnp.concatenate([inner, lead], 0), jnp.concatenate([lead, inner], 0)
    )
    square = t_mm(fit, fit)
    own = lax.dynamic_slice_in_dim(foot, here * share, share, 0).astype(F32)
    total = total - jnp.dot(own, square, precision=exact)
    return jnp.maximum(own + total / jnp.maximum(jnp.diagonal(square), 1.0), 0.0).astype(BF)


def on_device(recording, footprints, traces, live_count):
    slabs, parts = lax.axis_size("slab"), lax.axis_size("tm")
    frames, voxels = recording.shape
    extended, neurons = footprints.shape
    rim = extended - voxels
    early_shape = [pltpu.VMEM((frames, rim + EARLY), BF)] if parts == 2 else []
    pinned = [
        pltpu.with_memory_space_constraint(x, pltpu.HBM)
        for x in (live_count, recording, footprints, traces)
    ]
    far, near, count, *early = call(
        functools.partial(rim_kernel, voxels),
        [
            pltpu.VMEM((frames, rim), BF),
            pltpu.VMEM((frames, rim), BF),
            pltpu.VMEM((8, neurons), jnp.int32),
        ]
        + early_shape,
        [LEFT_THERE] * 4,
        [WHOLE] * (3 + len(early_shape)),
        1.5,
        scratch_shapes=[
            pltpu.SMEM(live_count.shape, jnp.int32),
            pltpu.VMEM((rim, neurons), BF),
            pltpu.VMEM((rim, neurons), BF),
            pltpu.VMEM((frames, neurons), F32),
            pltpu.VMEM((frames, rim), BF),
            COPIES((7,)),
        ],
    )(*pinned)
    def swapped(block, first):
        route = [(i, i + 1) for i in range(first, slabs - 1, 2)]
        return lax.ppermute(block, "slab", route + [(j, i) for i, j in route])

    far = swapped(far, 1)
    near = swapped(near, 0)
    plan, scale, cross_high, cross_low, rims, masked = call(
        functools.partial(drive_kernel, voxels),
        [
            shape((frames, neurons), F32),
            shape((8, neurons), F32),
            shape((GROUP, GROUP), BF),
            shape((GROUP, GROUP), BF),
            shape((2 * rim, neurons), BF),
            pltpu.VMEM((extended, neurons), BF),
        ],
        [WHOLE] * 4,
        [WHOLE] * 6,
        1.2,
    )(count, recording, footprints, traces)

    new_tr, rounded = call(
        sweep_kernel,
        [pltpu.VMEM((frames, neurons), F32), pltpu.VMEM((frames, neurons), BF)],
        [WHOLE] * 7,
        [WHOLE, WHOLE],
        0.4,
    )(plan, scale, cross_high, cross_low, rims, far, near)

    if parts == 2:
        return halved(voxels, rim, masked, recording, early[0], new_tr, rounded)
    return new_tr, spread(voxels, rim, masked, recording, rounded)


def solution(mesh):
    placed = (P("tm", "slab"), P(None, "slab"), P("tm", "slab"), P())
    return jax.shard_map(
        on_device,
        mesh=mesh,
        in_specs=placed,
        out_specs=(P("tm", "slab"), P("tm", "slab")),
        check_vma=False,
    )
```

```python
import functools

import jax
import jax.numpy as jnp
from jax import lax
from jax.experimental import pallas as pl
from jax.experimental.pallas import tpu as pltpu
from jax.sharding import PartitionSpec as P

GROUP = 128
BF = jnp.bfloat16
F32 = jnp.float32
WHOLE = pl.BlockSpec(memory_space=pltpu.VMEM)
LEFT_THERE = pl.BlockSpec(memory_space=pl.ANY)
COPIES = pltpu.SemaphoreType.DMA
shape = jax.ShapeDtypeStruct


def mm(left, right):
    return jnp.dot(left, right, preferred_element_type=F32)


def mm_t(left, right):
    return lax.dot_general(left, right, (((1,), (1,)), ((), ())), preferred_element_type=F32)


def t_mm(left, right):
    return lax.dot_general(left, right, (((0,), (0,)), ((), ())), preferred_element_type=F32)


def halves(wide):
    high = wide.astype(BF)
    return high, (wide - high.astype(F32)).astype(BF)


def living(count, block):
    slots = lax.broadcasted_iota(jnp.int32, block.shape, 1)
    return jnp.where(slots < count, block, jnp.zeros_like(block))


def diagonal(square):
    rows = lax.broadcasted_iota(jnp.int32, square.shape, 0)
    columns = lax.broadcasted_iota(jnp.int32, square.shape, 1)
    return jnp.sum(jnp.where(rows == columns, square, 0.0), axis=0, keepdims=True)


def at_end(axis):
    return lax.axis_index(axis) == lax.axis_size(axis) - 1


def odd_slab():
    return lax.axis_index("slab") % 2 == 1


def call(body, outs, in_specs, out_specs, expected, **more):
    return pl.pallas_call(
        body,
        out_shape=outs,
        in_specs=in_specs,
        out_specs=out_specs,
        compiler_params=pltpu.CompilerParams(vmem_limit_bytes=32 * 1024 * 1024),
        cost_estimate=pl.CostEstimate(
            flops=0, bytes_accessed=int(expected * 3_690_000), transcendentals=0
        ),
        **more,
    )


def copied(source, target, sem):
    copy = pltpu.make_async_copy(source, target, sem)
    copy.start()
    return copy


def first_column(which, voxels, rim):
    return pl.multiple_of(rim + which * (voxels // 2), 128)


def rolled(block):
    half = block.shape[1] // 2
    return jnp.concatenate([block[:, half:], block[:, :half]], axis=1)


def packed(which, middle):
    frames = middle.shape[0] // 2
    top, bottom = middle[:frames], middle[frames:]
    low = jnp.where(which == 0, top, rolled(top))
    high = jnp.where(which == 0, rolled(bottom), bottom)
    slots = lax.broadcasted_iota(jnp.int32, low.shape, 1)
    return jnp.where(slots < low.shape[1] // 2, low, high)


def unpacked(which, block):
    turned = rolled(block)
    top = jnp.where(which == 0, block, turned)
    bottom = jnp.where(which == 0, turned, block)
    return jnp.concatenate([top, bottom], axis=0)


def for_near_and_far(forward, backward):
    odd = odd_slab()
    return jnp.where(odd, backward, forward), jnp.where(odd, forward, backward)


def from_prev_and_next(near, far):
    odd = odd_slab()
    return jnp.where(odd, near, far), jnp.where(odd, far, near)


def rim_kernel(voxels, live, movie, foot, start, far, near, count, *rest):
    numbers, head, tail, traces, edge, middle, sems = rest[-7:]
    rim = head.shape[0]
    frames = edge.shape[0]
    there = 1 - lax.axis_index("tm")
    small = [
        copied(live, numbers, sems.at[0]),
        copied(start, traces, sems.at[1]),
        copied(foot.at[pl.ds(0, rim)], head, sems.at[2]),
        copied(foot.at[pl.ds(voxels, rim)], tail, sems.at[3]),
        copied(movie.at[:, pl.ds(0, rim)], edge, sems.at[4]),
        copied(movie.at[:, pl.ds(voxels // 2, rim)], middle, sems.at[5]),
    ]
    large = []
    if len(rest) > 7:
        first = first_column(there, voxels, rim)
        for i in range(voxels // 2 // rim - 1):
            column = movie.at[:, pl.ds(pl.multiple_of(first + i * rim, 128), rim)]
            large.append(copied(column, rest[0].at[pl.ds(i * frames, frames)], sems.at[6 + i]))
    for copy in small:
        copy.wait()
    alive = numbers[lax.axis_index("slab")]
    count[...] = jnp.full(count.shape, alive, jnp.int32)
    high, low = halves(living(alive, traces[...]))
    ends = jnp.where(at_end("slab"), jnp.zeros_like(tail[...]), tail[...])
    forward = mm_t(high, ends) + mm_t(low, ends)
    backward = edge[...].astype(F32) - (mm_t(high, head[...]) + mm_t(low, head[...]))
    one, two = for_near_and_far(forward, backward)
    near[...] = one.astype(BF)
    far[...] = two.astype(BF)
    if large:
        rest[0][(voxels // 2 // rim - 1) * frames:] = packed(there, middle[...])
    for copy in large:
        copy.wait()


def drive_kernel(voxels, count, movie, foot, start, plan, scale, cross_high, cross_low, rims, flat, masked):
    rim = foot.shape[0] - voxels
    alive = count[0:1]
    masked[:voxels] = living(alive, foot[:voxels])
    ends = living(alive, foot[voxels:])
    masked[voxels:] = jnp.where(at_end("slab"), jnp.zeros_like(ends), ends)
    rims[:rim] = -masked[:rim]
    rims[rim:] = masked[voxels:]
    flat[...] = movie[:, :rim].T
    drive = mm(movie[...], masked[:voxels])
    gram = t_mm(masked[...], masked[...])
    inverse = 1.0 / (diagonal(gram) + 1e-06)
    scale[...] = jnp.broadcast_to(inverse, scale.shape)
    gram_high, gram_low = halves(gram)
    cross_high[...] = gram_high[:GROUP, GROUP:]
    cross_low[...] = gram_low[:GROUP, GROUP:]
    current = living(alive, start[...])
    high, low = halves(current)
    for at in range(0, current.shape[1], GROUP):
        columns = slice(at, at + GROUP)
        coupled = mm(high[:, at:], gram_high[at:, columns]) + mm(high[:, at:], gram_low[at:, columns])
        coupled = coupled + mm(low[:, at:], gram_high[at:, columns])
        plan[:, columns] = current[:, columns] + (drive[:, columns] - coupled) * inverse[:, columns]


def sweep_kernel(
    plan, scale, cross_high, cross_low, rims, flat, far, near, traces, rounded, far_next, near_next
):
    rim = flat.shape[0]
    edges = rims[...]
    beside = jnp.concatenate(from_prev_and_next(near[...], far[...]), axis=1)
    stepped = plan[...] + mm(beside, edges) * scale[0:1]
    first = jnp.maximum(stepped[:, :GROUP], 0.0)
    high, low = halves(first)
    cross = cross_high[...]
    coupled = mm(high, cross) + mm(high, cross_low[...]) + mm(low, cross)
    second = jnp.maximum(stepped[:, GROUP:] - coupled * scale[0:1, GROUP:], 0.0)
    whole = jnp.concatenate([high, second.astype(BF)], axis=1)
    rounded[...] = whole
    forward = mm_t(edges[rim:], whole)
    backward = flat[...].astype(F32) + mm_t(edges[:rim], whole)
    one, two = for_near_and_far(forward, backward)
    near_next[...] = one.astype(BF)
    far_next[...] = two.astype(BF)
    traces[:, :GROUP] = first
    traces[:, GROUP:] = second


def own_kernel(voxels, movie, foot, fit, flat, total, quad, rim_part):
    rim = flat.shape[0]
    main = voxels // 2 - rim
    traces = fit[...]
    square = t_mm(traces, traces)
    quad[...] = square
    high, low = halves(square)
    begins, ends = foot[:rim], foot[voxels:]
    rim_part[:rim] = mm(flat[...], traces) - (mm(begins, high) + mm(begins, low))
    rim_part[rim:] = -(mm(ends, high) + mm(ends, low))
    first = first_column(lax.axis_index("tm"), voxels, rim)
    total[:main] = t_mm(movie[:, pl.ds(first, main)], traces)
    total[main:] = t_mm(movie[:, voxels // 2:voxels // 2 + rim], traces)


def both_kernel(rim_part, fit, far, near, lead, sent):
    rim = lead.shape[0]
    first = lax.axis_index("tm") == 0
    before, after = from_prev_and_next(near[...], far[...])
    traces = fit[...]
    begins = rim_part[:rim] - mm(before, traces)
    ends = rim_part[rim:] + mm(after, traces)
    lead[...] = jnp.where(first, begins, ends)
    sent[...] = jnp.where(first, ends, begins).astype(BF)


def main_kernel(voxels, rim, foot, total, quad, movie, fit, traces, out, new_tr, scale, moved, sems):
    here = lax.axis_index("tm")
    frames = fit.shape[0]
    width = voxels // 2
    main = width - rim
    written = [copied(traces, new_tr, sems.at[0])]
    fitted = fit[...]
    square = quad[...] + t_mm(fitted, fitted)
    inverse = 1.0 / jnp.maximum(diagonal(square), 1.0)
    scale[...] = jnp.broadcast_to(inverse, scale.shape)
    high, low = halves(square)
    first = first_column(here, voxels, rim)
    row = pl.multiple_of(rim - here * (rim // 2), 64)
    for begin, end in ((0, width // 2), (width // 2, main), (main, width)):
        if begin < main:
            own = foot[pl.ds(pl.multiple_of(first + begin, 128), end - begin)]
            columns = range(begin // rim, end // rim)
            shown = jnp.concatenate([movie[i * frames:(i + 1) * frames] for i in columns], axis=1)
        else:
            own = foot[width:width + rim]
            shown = unpacked(here, movie[main // rim * frames:])
        part = total[begin:end] + t_mm(shown, fitted) - (mm(own, high) + mm(own, low))
        moved[begin:end] = jnp.maximum(own.astype(F32) + part * inverse, 0.0).astype(BF)
        if begin < main:
            target = out.at[pl.ds(row + begin, end - begin)]
            written.append(copied(moved.at[pl.ds(begin, end - begin)], target, sems.at[len(written)]))
        else:
            half = rim // 2
            source = moved.at[pl.ds(pl.multiple_of(main + here * half, 64), half)]
            target = out.at[pl.ds(pl.multiple_of((1 - here) * (out.shape[0] - half), 64), half)]
            written.append(copied(source, target, sems.at[len(written)]))
    for copy in written:
        copy.wait()


def edge_kernel(voxels, sofar, foot, lead, came, scale, out, moved, sem):
    rim = lead.shape[0]
    here = lax.axis_index("tm")
    own = foot[pl.ds(pl.multiple_of(here * voxels, 128), rim)].astype(F32)
    moved[...] = jnp.maximum(own + (lead[...] + came[...].astype(F32)) * scale[0:1], 0.0).astype(BF)
    row = pl.multiple_of(here * (out.shape[0] - rim), 64)
    copied(moved, out.at[pl.ds(row, rim)], sem).wait()


def swapped(block, first):
    route = [(i, i + 1) for i in range(first, lax.axis_size("slab") - 1, 2)]
    return lax.ppermute(block, "slab", route + [(j, i) for i, j in route])


def halved(voxels, rim, foot, recording, flat, outgoing, new_tr, rounded, far, near):
    frames = recording.shape[0]
    extended, neurons = foot.shape
    width, share = voxels // 2, extended // 2
    across = [(0, 1), (1, 0)]
    movie = lax.ppermute(outgoing, "tm", across)
    far = swapped(far, 1)
    near = swapped(near, 0)
    other = lax.ppermute(rounded, "tm", across)
    total, quad, rim_part = call(
        functools.partial(own_kernel, voxels),
        [
            shape((width, neurons), F32),
            shape((neurons, neurons), F32),
            shape((2 * rim, neurons), F32),
        ],
        [WHOLE] * 4,
        [WHOLE] * 3,
        0.6,
    )(recording, foot, rounded, flat)
    lead, sent = call(
        both_kernel,
        [shape((rim, neurons), F32), pltpu.VMEM((rim, neurons), BF)],
        [WHOLE] * 4,
        [WHOLE] * 2,
        0.3,
    )(rim_part, rounded, far, near)
    came = lax.ppermute(sent, "tm", across)
    sofar, new_tr, scale = call(
        functools.partial(main_kernel, voxels, rim),
        [pltpu.HBM((share, neurons), BF), pltpu.HBM((frames, neurons), F32), shape((8, neurons), F32)],
        [WHOLE] * 6,
        [LEFT_THERE] * 2 + [WHOLE],
        2.0,
        scratch_shapes=[pltpu.VMEM((width, neurons), BF), COPIES((4,))],
    )(foot, total, quad, movie, other, new_tr)
    new_foot = call(
        functools.partial(edge_kernel, voxels),
        pltpu.HBM((share, neurons), BF),
        [LEFT_THERE] + [WHOLE] * 4,
        LEFT_THERE,
        0.8,
        input_output_aliases={0: 0},
        scratch_shapes=[pltpu.VMEM((rim, neurons), BF), COPIES],
    )(sofar, foot, lead, came, scale)
    return new_tr, new_foot


def spread(voxels, rim, foot, recording, rounded):
    slabs, parts = lax.axis_size("slab"), lax.axis_size("tm")
    extended, neurons = foot.shape
    share = extended // parts
    here = lax.axis_index("tm")
    closing = here == parts - 1
    exact = lax.Precision.HIGHEST
    cut = voxels - (share - rim)
    columns = jnp.concatenate([recording[:, :cut], recording[:, :rim], recording[:, cut:]], 1)
    movie = lax.all_to_all(columns, "tm", split_axis=1, concat_axis=0, tiled=True)
    fit = lax.all_gather(rounded, "tm", axis=0, tiled=True)
    edge = jnp.where(here == 0, foot[voxels:], foot[:rim])
    seen = movie[:, :rim].astype(F32)
    sent = jnp.where(here == 0, 0.0, seen) - mm_t(fit, edge)
    ahead = [(i * parts, (i + 1) * parts) for i in range(slabs - 1)]
    behind = [((i + 2) * parts - 1, (i + 1) * parts - 1) for i in range(slabs - 1)]
    lead = jnp.where(closing, 0.0, seen) + lax.ppermute(sent, ("slab", "tm"), ahead + behind)
    lead = lax.dot_general(lead, fit.astype(F32), (((0,), (0,)), ((), ())), precision=exact)
    inner = t_mm(movie[:, rim:], fit)
    total = jnp.where(
        closing, jnp.concatenate([inner, lead], 0), jnp.concatenate([lead, inner], 0)
    )
    square = t_mm(fit, fit)
    own = lax.dynamic_slice_in_dim(foot, here * share, share, 0).astype(F32)
    total = total - jnp.dot(own, square, precision=exact)
    return jnp.maximum(own + total / jnp.maximum(jnp.diagonal(square), 1.0), 0.0).astype(BF)


def on_device(recording, footprints, traces, live_count):
    frames, voxels = recording.shape
    extended, neurons = footprints.shape
    rim = extended - voxels
    main = voxels // 2 // rim - 1
    split = lax.axis_size("tm") == 2
    share_shape = [pltpu.VMEM((main * frames + frames // 2, rim), BF)] if split else []
    pinned = [
        pltpu.with_memory_space_constraint(x, pltpu.HBM)
        for x in (live_count, recording, footprints, traces)
    ]
    far, near, count, *outgoing = call(
        functools.partial(rim_kernel, voxels),
        [
            pltpu.VMEM((frames, rim), BF),
            pltpu.VMEM((frames, rim), BF),
            pltpu.VMEM((8, neurons), jnp.int32),
        ]
        + share_shape,
        [LEFT_THERE] * 4,
        [WHOLE] * (3 + len(share_shape)),
        1.5,
        scratch_shapes=[
            pltpu.SMEM(live_count.shape, jnp.int32),
            pltpu.VMEM((rim, neurons), BF),
            pltpu.VMEM((rim, neurons), BF),
            pltpu.VMEM((frames, neurons), F32),
            pltpu.VMEM((frames, rim), BF),
            pltpu.VMEM((frames, rim), BF),
            COPIES((6 + main,)),
        ],
    )(*pinned)
    far = swapped(far, 1)
    near = swapped(near, 0)
    plan, scale, cross_high, cross_low, rims, flat, masked = call(
        functools.partial(drive_kernel, voxels),
        [
            shape((frames, neurons), F32),
            shape((8, neurons), F32),
            shape((GROUP, GROUP), BF),
            shape((GROUP, GROUP), BF),
            shape((2 * rim, neurons), BF),
            shape((rim, frames), BF),
            pltpu.VMEM((extended, neurons), BF),
        ],
        [WHOLE] * 4,
        [WHOLE] * 7,
        1.2,
    )(count, recording, footprints, traces)
    new_tr, rounded, far, near = call(
        sweep_kernel,
        [
            pltpu.VMEM((frames, neurons), F32),
            pltpu.VMEM((frames, neurons), BF),
            pltpu.VMEM((rim, frames), BF),
            pltpu.VMEM((rim, frames), BF),
        ],
        [WHOLE] * 8,
        [WHOLE] * 4,
        0.5,
    )(plan, scale, cross_high, cross_low, rims, flat, far, near)
    if split:
        return halved(voxels, rim, masked, recording, flat, outgoing[0], new_tr, rounded, far, near)
    return new_tr, spread(voxels, rim, masked, recording, rounded)


def solution(mesh):
    placed = (P("tm", "slab"), P(None, "slab"), P("tm", "slab"), P())
    return jax.shard_map(
        on_device,
        mesh=mesh,
        in_specs=placed,
        out_specs=(P("tm", "slab"), P("tm", "slab")),
        check_vma=False,
    )
```

```python
import functools

import jax
import jax.numpy as jnp
from jax import lax
from jax.experimental import pallas as pl
from jax.experimental.pallas import tpu as pltpu
from jax.sharding import PartitionSpec as P

GROUP = 128
BF = jnp.bfloat16
F32 = jnp.float32
WHOLE = pl.BlockSpec(memory_space=pltpu.VMEM)
LEFT_THERE = pl.BlockSpec(memory_space=pl.ANY)
COPIES = pltpu.SemaphoreType.DMA
shape = jax.ShapeDtypeStruct


def mm(left, right):
    return jnp.dot(left, right, preferred_element_type=F32)


def mm_t(left, right):
    return lax.dot_general(left, right, (((1,), (1,)), ((), ())), preferred_element_type=F32)


def t_mm(left, right):
    return lax.dot_general(left, right, (((0,), (0,)), ((), ())), preferred_element_type=F32)


def halves(wide):
    high = wide.astype(BF)
    return high, (wide - high.astype(F32)).astype(BF)


def living(count, block):
    slots = lax.broadcasted_iota(jnp.int32, block.shape, 1)
    return jnp.where(slots < count, block, jnp.zeros_like(block))


def diagonal(square):
    rows = lax.broadcasted_iota(jnp.int32, square.shape, 0)
    columns = lax.broadcasted_iota(jnp.int32, square.shape, 1)
    return jnp.sum(jnp.where(rows == columns, square, 0.0), axis=0, keepdims=True)


def at_end(axis):
    return lax.axis_index(axis) == lax.axis_size(axis) - 1


def odd_slab():
    return lax.axis_index("slab") % 2 == 1


def call(body, outs, in_specs, out_specs, expected, **more):
    return pl.pallas_call(
        body,
        out_shape=outs,
        in_specs=in_specs,
        out_specs=out_specs,
        compiler_params=pltpu.CompilerParams(vmem_limit_bytes=32 * 1024 * 1024),
        cost_estimate=pl.CostEstimate(
            flops=0, bytes_accessed=int(expected * 3_690_000), transcendentals=0
        ),
        **more,
    )


def copied(source, target, sem):
    copy = pltpu.make_async_copy(source, target, sem)
    copy.start()
    return copy


def first_column(which, voxels, rim):
    return pl.multiple_of(rim + which * (voxels // 2), 128)


def rolled(block):
    half = block.shape[1] // 2
    return jnp.concatenate([block[:, half:], block[:, :half]], axis=1)


def packed(which, middle):
    frames = middle.shape[0] // 2
    top, bottom = middle[:frames], middle[frames:]
    low = jnp.where(which == 0, top, rolled(top))
    high = jnp.where(which == 0, rolled(bottom), bottom)
    slots = lax.broadcasted_iota(jnp.int32, low.shape, 1)
    return jnp.where(slots < low.shape[1] // 2, low, high)


def unpacked(which, block):
    turned = rolled(block)
    top = jnp.where(which == 0, block, turned)
    bottom = jnp.where(which == 0, turned, block)
    return jnp.concatenate([top, bottom], axis=0)


def for_near_and_far(forward, backward):
    odd = odd_slab()
    return jnp.where(odd, backward, forward), jnp.where(odd, forward, backward)


def from_prev_and_next(near, far):
    odd = odd_slab()
    return jnp.where(odd, near, far), jnp.where(odd, far, near)


def rim_kernel(voxels, live, movie, foot, start, far, near, count, *rest):
    numbers, rims, traces, edge, middle, sems = rest[-6:]
    rim = edge.shape[1]
    frames = edge.shape[0]
    there = 1 - lax.axis_index("tm")
    small = [
        copied(live, numbers, sems.at[0]),
        copied(start, traces, sems.at[1]),
        copied(foot.at[pl.ds(0, rim)], rims.at[pl.ds(0, rim)], sems.at[2]),
        copied(foot.at[pl.ds(voxels, rim)], rims.at[pl.ds(rim, rim)], sems.at[3]),
        copied(movie.at[:, pl.ds(0, rim)], edge, sems.at[4]),
        copied(movie.at[:, pl.ds(voxels // 2, rim)], middle, sems.at[5]),
    ]
    large = []
    if len(rest) > 6:
        first = first_column(there, voxels, rim)
        for i in range(voxels // 2 // rim - 1):
            column = movie.at[:, pl.ds(pl.multiple_of(first + i * rim, 128), rim)]
            large.append(copied(column, rest[0].at[pl.ds(i * frames, frames)], sems.at[6 + i]))
    for copy in small:
        copy.wait()
    alive = numbers[lax.axis_index("slab")]
    count[...] = jnp.full(count.shape, alive, jnp.int32)
    seen = mm_t(living(alive, traces[...]).astype(BF), rims[...])
    backward = edge[...].astype(F32) - seen[:, :rim]
    one, two = for_near_and_far(seen[:, rim:], backward)
    near[...] = one.astype(BF)
    far[...] = two.astype(BF)
    if large:
        rest[0][(voxels // 2 // rim - 1) * frames:] = packed(there, middle[...])
    for copy in large:
        copy.wait()


def drive_kernel(voxels, count, movie, foot, start, plan, scale, cross_high, cross_low, rims, flat, masked):
    rim = foot.shape[0] - voxels
    alive = count[0:1]
    masked[:voxels] = living(alive, foot[:voxels])
    ends = living(alive, foot[voxels:])
    masked[voxels:] = jnp.where(at_end("slab"), jnp.zeros_like(ends), ends)
    rims[:rim] = -masked[:rim]
    rims[rim:] = masked[voxels:]
    flat[...] = movie[:, :rim].T
    drive = mm(movie[...], masked[:voxels])
    gram = t_mm(masked[...], masked[...])
    inverse = 1.0 / (diagonal(gram) + 1e-06)
    scale[...] = jnp.broadcast_to(inverse, scale.shape)
    gram_high, gram_low = halves(gram)
    cross_high[...] = gram_high[:GROUP, GROUP:]
    cross_low[...] = gram_low[:GROUP, GROUP:]
    current = living(alive, start[...])
    high, low = halves(current)
    for at in range(0, current.shape[1], GROUP):
        columns = slice(at, at + GROUP)
        coupled = mm(high[:, at:], gram_high[at:, columns]) + mm(high[:, at:], gram_low[at:, columns])
        coupled = coupled + mm(low[:, at:], gram_high[at:, columns])
        plan[:, columns] = current[:, columns] + (drive[:, columns] - coupled) * inverse[:, columns]


def sweep_kernel(
    plan, scale, cross_high, cross_low, rims, flat, far, near, traces, rounded, far_next, near_next
):
    rim = flat.shape[0]
    edges = rims[...]
    beside = jnp.concatenate(from_prev_and_next(near[...], far[...]), axis=1)
    stepped = plan[...] + mm(beside, edges) * scale[0:1]
    first = jnp.maximum(stepped[:, :GROUP], 0.0)
    high, low = halves(first)
    cross = cross_high[...]
    coupled = mm(high, cross) + mm(high, cross_low[...]) + mm(low, cross)
    second = jnp.maximum(stepped[:, GROUP:] - coupled * scale[0:1, GROUP:], 0.0)
    whole = jnp.concatenate([high, second.astype(BF)], axis=1)
    rounded[...] = whole
    seen = mm_t(edges, whole)
    one, two = for_near_and_far(seen[rim:], flat[...].astype(F32) + seen[:rim])
    near_next[...] = one.astype(BF)
    far_next[...] = two.astype(BF)
    traces[:, :GROUP] = first
    traces[:, GROUP:] = second


def own_kernel(voxels, movie, foot, fit, flat, total, quad, rim_part):
    rim = flat.shape[0]
    main = voxels // 2 - rim
    traces = fit[...]
    square = t_mm(traces, traces)
    quad[...] = square
    high, low = halves(square)
    begins, ends = foot[:rim], foot[voxels:]
    rim_part[:rim] = mm(flat[...], traces) - (mm(begins, high) + mm(begins, low))
    rim_part[rim:] = -(mm(ends, high) + mm(ends, low))
    first = first_column(lax.axis_index("tm"), voxels, rim)
    total[:main] = t_mm(movie[:, pl.ds(first, main)], traces)
    total[main:] = t_mm(movie[:, voxels // 2:voxels // 2 + rim], traces)


def both_kernel(rim_part, fit, far, near, lead, sent):
    rim = lead.shape[0]
    first = lax.axis_index("tm") == 0
    before, after = from_prev_and_next(near[...], far[...])
    traces = fit[...]
    begins = rim_part[:rim] - mm(before, traces)
    ends = rim_part[rim:] + mm(after, traces)
    lead[...] = jnp.where(first, begins, ends)
    sent[...] = jnp.where(first, ends, begins).astype(BF)


def main_kernel(voxels, rim, foot, total, quad, movie, fit, traces, out, new_tr, scale, moved, sems):
    here = lax.axis_index("tm")
    frames = fit.shape[0]
    width = voxels // 2
    main = width - rim
    written = [copied(traces, new_tr, sems.at[0])]
    fitted = fit[...]
    square = quad[...] + t_mm(fitted, fitted)
    inverse = 1.0 / jnp.maximum(diagonal(square), 1.0)
    scale[...] = jnp.broadcast_to(inverse, scale.shape)
    high, low = halves(square)
    first = first_column(here, voxels, rim)
    row = pl.multiple_of(rim - here * (rim // 2), 64)
    for begin, end in ((0, width // 2), (width // 2, main), (main, width)):
        if begin < main:
            own = foot[pl.ds(pl.multiple_of(first + begin, 128), end - begin)]
            columns = range(begin // rim, end // rim)
            shown = jnp.concatenate([movie[i * frames:(i + 1) * frames] for i in columns], axis=1)
        else:
            own = foot[width:width + rim]
            shown = unpacked(here, movie[main // rim * frames:])
        part = total[begin:end] + t_mm(shown, fitted) - (mm(own, high) + mm(own, low))
        moved[begin:end] = jnp.maximum(own.astype(F32) + part * inverse, 0.0).astype(BF)
        if begin < main:
            target = out.at[pl.ds(row + begin, end - begin)]
            written.append(copied(moved.at[pl.ds(begin, end - begin)], target, sems.at[len(written)]))
        else:
            half = rim // 2
            source = moved.at[pl.ds(pl.multiple_of(main + here * half, 64), half)]
            target = out.at[pl.ds(pl.multiple_of((1 - here) * (out.shape[0] - half), 64), half)]
            written.append(copied(source, target, sems.at[len(written)]))
    for copy in written:
        copy.wait()


def edge_kernel(voxels, sofar, foot, lead, came, scale, out, moved, sem):
    rim = lead.shape[0]
    here = lax.axis_index("tm")
    own = foot[pl.ds(pl.multiple_of(here * voxels, 128), rim)].astype(F32)
    moved[...] = jnp.maximum(own + (lead[...] + came[...].astype(F32)) * scale[0:1], 0.0).astype(BF)
    row = pl.multiple_of(here * (out.shape[0] - rim), 64)
    copied(moved, out.at[pl.ds(row, rim)], sem).wait()


def swapped(block, first):
    route = [(i, i + 1) for i in range(first, lax.axis_size("slab") - 1, 2)]
    return lax.ppermute(block, "slab", route + [(j, i) for i, j in route])


def halved(voxels, rim, foot, recording, flat, outgoing, new_tr, rounded, far, near):
    frames = recording.shape[0]
    extended, neurons = foot.shape
    width, share = voxels // 2, extended // 2
    across = [(0, 1), (1, 0)]
    movie = lax.ppermute(outgoing, "tm", across)
    far = swapped(far, 1)
    near = swapped(near, 0)
    other = lax.ppermute(rounded, "tm", across)
    total, quad, rim_part = call(
        functools.partial(own_kernel, voxels),
        [
            shape((width, neurons), F32),
            shape((neurons, neurons), F32),
            shape((2 * rim, neurons), F32),
        ],
        [WHOLE] * 4,
        [WHOLE] * 3,
        0.6,
    )(recording, foot, rounded, flat)
    lead, sent = call(
        both_kernel,
        [shape((rim, neurons), F32), pltpu.VMEM((rim, neurons), BF)],
        [WHOLE] * 4,
        [WHOLE] * 2,
        0.3,
    )(rim_part, rounded, far, near)
    came = lax.ppermute(sent, "tm", across)
    sofar, new_tr, scale = call(
        functools.partial(main_kernel, voxels, rim),
        [pltpu.HBM((share, neurons), BF), pltpu.HBM((frames, neurons), F32), shape((8, neurons), F32)],
        [WHOLE] * 6,
        [LEFT_THERE] * 2 + [WHOLE],
        2.0,
        scratch_shapes=[pltpu.VMEM((width, neurons), BF), COPIES((4,))],
    )(foot, total, quad, movie, other, new_tr)
    new_foot = call(
        functools.partial(edge_kernel, voxels),
        pltpu.HBM((share, neurons), BF),
        [LEFT_THERE] + [WHOLE] * 4,
        LEFT_THERE,
        0.8,
        input_output_aliases={0: 0},
        scratch_shapes=[pltpu.VMEM((rim, neurons), BF), COPIES],
    )(sofar, foot, lead, came, scale)
    return new_tr, new_foot


def spread(voxels, rim, foot, recording, rounded):
    slabs, parts = lax.axis_size("slab"), lax.axis_size("tm")
    extended, neurons = foot.shape
    share = extended // parts
    here = lax.axis_index("tm")
    closing = here == parts - 1
    exact = lax.Precision.HIGHEST
    cut = voxels - (share - rim)
    columns = jnp.concatenate([recording[:, :cut], recording[:, :rim], recording[:, cut:]], 1)
    movie = lax.all_to_all(columns, "tm", split_axis=1, concat_axis=0, tiled=True)
    fit = lax.all_gather(rounded, "tm", axis=0, tiled=True)
    edge = jnp.where(here == 0, foot[voxels:], foot[:rim])
    seen = movie[:, :rim].astype(F32)
    sent = jnp.where(here == 0, 0.0, seen) - mm_t(fit, edge)
    ahead = [(i * parts, (i + 1) * parts) for i in range(slabs - 1)]
    behind = [((i + 2) * parts - 1, (i + 1) * parts - 1) for i in range(slabs - 1)]
    lead = jnp.where(closing, 0.0, seen) + lax.ppermute(sent, ("slab", "tm"), ahead + behind)
    lead = lax.dot_general(lead, fit.astype(F32), (((0,), (0,)), ((), ())), precision=exact)
    inner = t_mm(movie[:, rim:], fit)
    total = jnp.where(
        closing, jnp.concatenate([inner, lead], 0), jnp.concatenate([lead, inner], 0)
    )
    square = t_mm(fit, fit)
    own = lax.dynamic_slice_in_dim(foot, here * share, share, 0).astype(F32)
    total = total - jnp.dot(own, square, precision=exact)
    return jnp.maximum(own + total / jnp.maximum(jnp.diagonal(square), 1.0), 0.0).astype(BF)


def on_device(recording, footprints, traces, live_count):
    frames, voxels = recording.shape
    extended, neurons = footprints.shape
    rim = extended - voxels
    main = voxels // 2 // rim - 1
    split = lax.axis_size("tm") == 2
    share_shape = [pltpu.VMEM((main * frames + frames // 2, rim), BF)] if split else []
    pinned = [
        pltpu.with_memory_space_constraint(x, pltpu.HBM)
        for x in (live_count, recording, footprints, traces)
    ]
    far, near, count, *outgoing = call(
        functools.partial(rim_kernel, voxels),
        [
            pltpu.VMEM((frames, rim), BF),
            pltpu.VMEM((frames, rim), BF),
            pltpu.VMEM((8, neurons), jnp.int32),
        ]
        + share_shape,
        [LEFT_THERE] * 4,
        [WHOLE] * (3 + len(share_shape)),
        1.5,
        scratch_shapes=[
            pltpu.SMEM(live_count.shape, jnp.int32),
            pltpu.VMEM((2 * rim, neurons), BF),
            pltpu.VMEM((frames, neurons), F32),
            pltpu.VMEM((frames, rim), BF),
            pltpu.VMEM((frames, rim), BF),
            COPIES((6 + main,)),
        ],
    )(*pinned)
    far = swapped(far, 1)
    near = swapped(near, 0)
    plan, scale, cross_high, cross_low, rims, flat, masked = call(
        functools.partial(drive_kernel, voxels),
        [
            shape((frames, neurons), F32),
            shape((8, neurons), F32),
            shape((GROUP, GROUP), BF),
            shape((GROUP, GROUP), BF),
            shape((2 * rim, neurons), BF),
            shape((rim, frames), BF),
            pltpu.VMEM((extended, neurons), BF),
        ],
        [WHOLE] * 4,
        [WHOLE] * 7,
        1.2,
    )(count, recording, footprints, traces)
    new_tr, rounded, far, near = call(
        sweep_kernel,
        [
            pltpu.VMEM((frames, neurons), F32),
            pltpu.VMEM((frames, neurons), BF),
            pltpu.VMEM((rim, frames), BF),
            pltpu.VMEM((rim, frames), BF),
        ],
        [WHOLE] * 8,
        [WHOLE] * 4,
        0.5,
    )(plan, scale, cross_high, cross_low, rims, flat, far, near)
    if split:
        return halved(voxels, rim, masked, recording, flat, outgoing[0], new_tr, rounded, far, near)
    return new_tr, spread(voxels, rim, masked, recording, rounded)


def solution(mesh):
    placed = (P("tm", "slab"), P(None, "slab"), P("tm", "slab"), P())
    return jax.shard_map(
        on_device,
        mesh=mesh,
        in_specs=placed,
        out_specs=(P("tm", "slab"), P("tm", "slab")),
        check_vma=False,
    )
```

```python
import functools

import jax
import jax.numpy as jnp
from jax import lax
from jax.experimental import pallas as pl
from jax.experimental.pallas import tpu as pltpu
from jax.sharding import PartitionSpec as P

GROUP = 128
BF = jnp.bfloat16
F32 = jnp.float32
WHOLE = pl.BlockSpec(memory_space=pltpu.VMEM)
LEFT_THERE = pl.BlockSpec(memory_space=pl.ANY)
COPIES = pltpu.SemaphoreType.DMA
shape = jax.ShapeDtypeStruct


def mm(left, right):
    return jnp.dot(left, right, preferred_element_type=F32)


def mm_t(left, right):
    return lax.dot_general(left, right, (((1,), (1,)), ((), ())), preferred_element_type=F32)


def t_mm(left, right):
    return lax.dot_general(left, right, (((0,), (0,)), ((), ())), preferred_element_type=F32)


def halves(wide):
    high = wide.astype(BF)
    return high, (wide - high.astype(F32)).astype(BF)


def living(count, block):
    slots = lax.broadcasted_iota(jnp.int32, block.shape, 1)
    return jnp.where(slots < count, block, jnp.zeros_like(block))


def diagonal(square):
    rows = lax.broadcasted_iota(jnp.int32, square.shape, 0)
    columns = lax.broadcasted_iota(jnp.int32, square.shape, 1)
    return jnp.sum(jnp.where(rows == columns, square, 0.0), axis=0, keepdims=True)


def at_end(axis):
    return lax.axis_index(axis) == lax.axis_size(axis) - 1


def odd_slab():
    return lax.axis_index("slab") % 2 == 1


def call(body, outs, in_specs, out_specs, expected, **more):
    return pl.pallas_call(
        body,
        out_shape=outs,
        in_specs=in_specs,
        out_specs=out_specs,
        compiler_params=pltpu.CompilerParams(vmem_limit_bytes=32 * 1024 * 1024),
        cost_estimate=pl.CostEstimate(
            flops=0, bytes_accessed=int(expected * 3_690_000), transcendentals=0
        ),
        **more,
    )


def copied(source, target, sem):
    copy = pltpu.make_async_copy(source, target, sem)
    copy.start()
    return copy


def first_column(which, voxels, rim):
    return pl.multiple_of(rim + which * (voxels // 2), 128)


def rolled(block):
    half = block.shape[1] // 2
    return jnp.concatenate([block[:, half:], block[:, :half]], axis=1)


def packed(which, middle):
    frames = middle.shape[0] // 2
    top, bottom = middle[:frames], middle[frames:]
    low = jnp.where(which == 0, top, rolled(top))
    high = jnp.where(which == 0, rolled(bottom), bottom)
    slots = lax.broadcasted_iota(jnp.int32, low.shape, 1)
    return jnp.where(slots < low.shape[1] // 2, low, high)


def unpacked(which, block):
    turned = rolled(block)
    top = jnp.where(which == 0, block, turned)
    bottom = jnp.where(which == 0, turned, block)
    return jnp.concatenate([top, bottom], axis=0)


def for_near_and_far(forward, backward):
    odd = odd_slab()
    return jnp.where(odd, backward, forward), jnp.where(odd, forward, backward)


def from_prev_and_next(near, far):
    odd = odd_slab()
    return jnp.where(odd, near, far), jnp.where(odd, far, near)


def rim_kernel(voxels, live, movie, foot, start, far, near, count, *rest):
    numbers, rims, traces, edge, middle, half, sems = rest[-7:]
    rim = edge.shape[1]
    frames = edge.shape[0]
    there = 1 - lax.axis_index("tm")
    small = [
        copied(live, numbers, sems.at[0]),
        copied(start, traces, sems.at[1]),
        copied(foot.at[pl.ds(0, rim)], rims.at[pl.ds(0, rim)], sems.at[2]),
        copied(foot.at[pl.ds(voxels, rim)], rims.at[pl.ds(rim, rim)], sems.at[3]),
        copied(movie.at[:, pl.ds(0, rim)], edge, sems.at[4]),
        copied(movie.at[:, pl.ds(voxels // 2, rim)], middle, sems.at[5]),
    ]
    large = []
    if len(rest) > 7:
        first = first_column(there, voxels, rim)
        for i in range(voxels // 2 // rim - 1):
            column = movie.at[:, pl.ds(pl.multiple_of(first + i * rim, 128), rim)]
            large.append(copied(column, rest[0].at[pl.ds(i * frames, frames)], sems.at[6 + i]))
    for copy in small:
        copy.wait()
    if large:
        half[...] = packed(there, middle[...])
        rows = pl.ds((voxels // 2 // rim - 1) * frames, frames // 2)
        large.append(copied(half, rest[0].at[rows], sems.at[5]))
    alive = numbers[lax.axis_index("slab")]
    count[...] = jnp.full(count.shape, alive, jnp.int32)
    seen = mm_t(living(alive, traces[...]).astype(BF), rims[...])
    backward = edge[...].astype(F32) - seen[:, :rim]
    one, two = for_near_and_far(seen[:, rim:], backward)
    near[...] = one.astype(BF)
    far[...] = two.astype(BF)
    for copy in large:
        copy.wait()


def drive_kernel(voxels, count, movie, foot, start, plan, scale, cross_high, cross_low, rims, flat, masked):
    rim = foot.shape[0] - voxels
    alive = count[0:1]
    masked[:voxels] = living(alive, foot[:voxels])
    ends = living(alive, foot[voxels:])
    masked[voxels:] = jnp.where(at_end("slab"), jnp.zeros_like(ends), ends)
    rims[:rim] = -masked[:rim]
    rims[rim:] = masked[voxels:]
    flat[...] = movie[:, :rim].T
    drive = mm(movie[...], masked[:voxels])
    gram = t_mm(masked[...], masked[...])
    inverse = 1.0 / (diagonal(gram) + 1e-06)
    scale[...] = jnp.broadcast_to(inverse, scale.shape)
    gram_high, gram_low = halves(gram)
    cross_high[...] = gram_high[:GROUP, GROUP:]
    cross_low[...] = gram_low[:GROUP, GROUP:]
    current = living(alive, start[...])
    high, low = halves(current)
    for at in range(0, current.shape[1], GROUP):
        columns = slice(at, at + GROUP)
        coupled = mm(high[:, at:], gram_high[at:, columns]) + mm(high[:, at:], gram_low[at:, columns])
        coupled = coupled + mm(low[:, at:], gram_high[at:, columns])
        plan[:, columns] = current[:, columns] + (drive[:, columns] - coupled) * inverse[:, columns]


def sweep_kernel(
    plan, scale, cross_high, cross_low, rims, flat, far, near, traces, rounded, far_next, near_next
):
    rim = flat.shape[0]
    edges = rims[...]
    beside = jnp.concatenate(from_prev_and_next(near[...], far[...]), axis=1)
    stepped = plan[...] + mm(beside, edges) * scale[0:1]
    first = jnp.maximum(stepped[:, :GROUP], 0.0)
    high, low = halves(first)
    cross = cross_high[...]
    coupled = mm(
        jnp.concatenate([high, low, high], axis=1), jnp.concatenate([cross, cross, cross_low[...]], axis=0)
    )
    second = jnp.maximum(stepped[:, GROUP:] - coupled * scale[0:1, GROUP:], 0.0)
    whole = jnp.concatenate([high, second.astype(BF)], axis=1)
    rounded[...] = whole
    seen = mm_t(edges, whole)
    one, two = for_near_and_far(seen[rim:], flat[...].astype(F32) + seen[:rim])
    near_next[...] = one.astype(BF)
    far_next[...] = two.astype(BF)
    traces[:, :GROUP] = first
    traces[:, GROUP:] = second


def own_kernel(voxels, movie, foot, fit, flat, total, quad, rim_part):
    rim = flat.shape[0]
    main = voxels // 2 - rim
    traces = fit[...]
    square = t_mm(traces, traces)
    quad[...] = square
    high, low = halves(square)
    begins, ends = foot[:rim], foot[voxels:]
    rim_part[:rim] = mm(flat[...], traces) - (mm(begins, high) + mm(begins, low))
    rim_part[rim:] = -(mm(ends, high) + mm(ends, low))
    first = first_column(lax.axis_index("tm"), voxels, rim)
    total[:main] = t_mm(movie[:, pl.ds(first, main)], traces)
    total[main:] = t_mm(movie[:, voxels // 2:voxels // 2 + rim], traces)


def both_kernel(rim_part, fit, far, near, lead, sent):
    rim = lead.shape[0]
    first = lax.axis_index("tm") == 0
    before, after = from_prev_and_next(near[...], far[...])
    traces = fit[...]
    begins = rim_part[:rim] - mm(before, traces)
    ends = rim_part[rim:] + mm(after, traces)
    lead[...] = jnp.where(first, begins, ends)
    sent[...] = jnp.where(first, ends, begins).astype(BF)


def fetch_kernel(movies, movie, sem):
    rows = movie.shape[0]
    first = pl.multiple_of((1 - lax.axis_index("tm")) * rows, 128)
    copied(movies.at[pl.ds(first, rows)], movie, sem).wait()


def main_kernel(voxels, rim, foot, total, quad, movie, fit, traces, out, new_tr, scale, moved, sems):
    here = lax.axis_index("tm")
    frames = fit.shape[0]
    width = voxels // 2
    main = width - rim
    written = [copied(traces, new_tr, sems.at[0])]
    fitted = fit[...]
    square = quad[...] + t_mm(fitted, fitted)
    inverse = 1.0 / jnp.maximum(diagonal(square), 1.0)
    scale[...] = jnp.broadcast_to(inverse, scale.shape)
    high, low = halves(square)
    first = first_column(here, voxels, rim)
    row = pl.multiple_of(rim - here * (rim // 2), 64)
    for begin, end in ((0, width // 2), (width // 2, main), (main, width)):
        if begin < main:
            own = foot[pl.ds(pl.multiple_of(first + begin, 128), end - begin)]
            columns = range(begin // rim, end // rim)
            shown = jnp.concatenate([movie[i * frames:(i + 1) * frames] for i in columns], axis=1)
        else:
            own = foot[width:width + rim]
            shown = unpacked(here, movie[main // rim * frames:])
        part = total[begin:end] + t_mm(shown, fitted) - (mm(own, high) + mm(own, low))
        moved[begin:end] = jnp.maximum(own.astype(F32) + part * inverse, 0.0).astype(BF)
        if begin < main:
            target = out.at[pl.ds(row + begin, end - begin)]
            written.append(copied(moved.at[pl.ds(begin, end - begin)], target, sems.at[len(written)]))
        else:
            half = rim // 2
            source = moved.at[pl.ds(pl.multiple_of(main + here * half, 64), half)]
            target = out.at[pl.ds(pl.multiple_of((1 - here) * (out.shape[0] - half), 64), half)]
            written.append(copied(source, target, sems.at[len(written)]))
    for copy in written:
        copy.wait()


def edge_kernel(voxels, sofar, foot, lead, came, scale, out, moved, sem):
    rim = lead.shape[0]
    here = lax.axis_index("tm")
    own = foot[pl.ds(pl.multiple_of(here * voxels, 128), rim)].astype(F32)
    moved[...] = jnp.maximum(own + (lead[...] + came[...].astype(F32)) * scale[0:1], 0.0).astype(BF)
    row = pl.multiple_of(here * (out.shape[0] - rim), 64)
    copied(moved, out.at[pl.ds(row, rim)], sem).wait()


def swapped(block, first):
    route = [(i, i + 1) for i in range(first, lax.axis_size("slab") - 1, 2)]
    return lax.ppermute(block, "slab", route + [(j, i) for i, j in route])


def halved(voxels, rim, foot, recording, flat, outgoing, new_tr, rounded, far, near):
    frames = recording.shape[0]
    extended, neurons = foot.shape
    width, share = voxels // 2, extended // 2
    across = [(0, 1), (1, 0)]
    movies = lax.all_gather(outgoing, "tm", axis=0, tiled=True)
    far = swapped(far, 1)
    near = swapped(near, 0)
    other = lax.ppermute(rounded, "tm", across)
    total, quad, rim_part = call(
        functools.partial(own_kernel, voxels),
        [
            shape((width, neurons), F32),
            shape((neurons, neurons), F32),
            shape((2 * rim, neurons), F32),
        ],
        [WHOLE] * 4,
        [WHOLE] * 3,
        0.6,
    )(recording, foot, rounded, flat)
    lead, sent = call(
        both_kernel,
        [shape((rim, neurons), F32), pltpu.VMEM((rim, neurons), BF)],
        [WHOLE] * 4,
        [WHOLE] * 2,
        0.3,
    )(rim_part, rounded, far, near)
    came = lax.ppermute(sent, "tm", across)
    movie = call(
        fetch_kernel,
        pltpu.VMEM(outgoing.shape, BF),
        [LEFT_THERE],
        WHOLE,
        0.9,
        scratch_shapes=[COPIES],
    )(pltpu.with_memory_space_constraint(movies, pltpu.HBM))
    sofar, new_tr, scale = call(
        functools.partial(main_kernel, voxels, rim),
        [pltpu.HBM((share, neurons), BF), pltpu.HBM((frames, neurons), F32), shape((8, neurons), F32)],
        [WHOLE] * 6,
        [LEFT_THERE] * 2 + [WHOLE],
        2.0,
        scratch_shapes=[pltpu.VMEM((width, neurons), BF), COPIES((4,))],
    )(foot, total, quad, movie, other, new_tr)
    new_foot = call(
        functools.partial(edge_kernel, voxels),
        pltpu.HBM((share, neurons), BF),
        [LEFT_THERE] + [WHOLE] * 4,
        LEFT_THERE,
        0.8,
        input_output_aliases={0: 0},
        scratch_shapes=[pltpu.VMEM((rim, neurons), BF), COPIES],
    )(sofar, foot, lead, came, scale)
    return new_tr, new_foot


def spread(voxels, rim, foot, recording, rounded):
    slabs, parts = lax.axis_size("slab"), lax.axis_size("tm")
    extended, neurons = foot.shape
    share = extended // parts
    here = lax.axis_index("tm")
    closing = here == parts - 1
    exact = lax.Precision.HIGHEST
    cut = voxels - (share - rim)
    columns = jnp.concatenate([recording[:, :cut], recording[:, :rim], recording[:, cut:]], 1)
    movie = lax.all_to_all(columns, "tm", split_axis=1, concat_axis=0, tiled=True)
    fit = lax.all_gather(rounded, "tm", axis=0, tiled=True)
    edge = jnp.where(here == 0, foot[voxels:], foot[:rim])
    seen = movie[:, :rim].astype(F32)
    sent = jnp.where(here == 0, 0.0, seen) - mm_t(fit, edge)
    ahead = [(i * parts, (i + 1) * parts) for i in range(slabs - 1)]
    behind = [((i + 2) * parts - 1, (i + 1) * parts - 1) for i in range(slabs - 1)]
    lead = jnp.where(closing, 0.0, seen) + lax.ppermute(sent, ("slab", "tm"), ahead + behind)
    lead = lax.dot_general(lead, fit.astype(F32), (((0,), (0,)), ((), ())), precision=exact)
    inner = t_mm(movie[:, rim:], fit)
    total = jnp.where(
        closing, jnp.concatenate([inner, lead], 0), jnp.concatenate([lead, inner], 0)
    )
    square = t_mm(fit, fit)
    own = lax.dynamic_slice_in_dim(foot, here * share, share, 0).astype(F32)
    total = total - jnp.dot(own, square, precision=exact)
    return jnp.maximum(own + total / jnp.maximum(jnp.diagonal(square), 1.0), 0.0).astype(BF)


def on_device(recording, footprints, traces, live_count):
    frames, voxels = recording.shape
    extended, neurons = footprints.shape
    rim = extended - voxels
    main = voxels // 2 // rim - 1
    split = lax.axis_size("tm") == 2
    share_shape = [pltpu.HBM((main * frames + frames // 2, rim), BF)] if split else []
    pinned = [
        pltpu.with_memory_space_constraint(x, pltpu.HBM)
        for x in (live_count, recording, footprints, traces)
    ]
    far, near, count, *outgoing = call(
        functools.partial(rim_kernel, voxels),
        [
            pltpu.VMEM((frames, rim), BF),
            pltpu.VMEM((frames, rim), BF),
            pltpu.VMEM((8, neurons), jnp.int32),
        ]
        + share_shape,
        [LEFT_THERE] * 4,
        [WHOLE] * 3 + [LEFT_THERE] * len(share_shape),
        1.5,
        scratch_shapes=[
            pltpu.SMEM(live_count.shape, jnp.int32),
            pltpu.VMEM((2 * rim, neurons), BF),
            pltpu.VMEM((frames, neurons), F32),
            pltpu.VMEM((frames, rim), BF),
            pltpu.VMEM((frames, rim), BF),
            pltpu.VMEM((frames // 2, rim), BF),
            COPIES((6 + main,)),
        ],
    )(*pinned)
    far = swapped(far, 1)
    near = swapped(near, 0)
    plan, scale, cross_high, cross_low, rims, flat, masked = call(
        functools.partial(drive_kernel, voxels),
        [
            shape((frames, neurons), F32),
            shape((8, neurons), F32),
            shape((GROUP, GROUP), BF),
            shape((GROUP, GROUP), BF),
            shape((2 * rim, neurons), BF),
            shape((rim, frames), BF),
            pltpu.VMEM((extended, neurons), BF),
        ],
        [WHOLE] * 4,
        [WHOLE] * 7,
        1.2,
    )(count, recording, footprints, traces)
    new_tr, rounded, far, near = call(
        sweep_kernel,
        [
            pltpu.VMEM((frames, neurons), F32),
            pltpu.VMEM((frames, neurons), BF),
            pltpu.VMEM((rim, frames), BF),
            pltpu.VMEM((rim, frames), BF),
        ],
        [WHOLE] * 8,
        [WHOLE] * 4,
        0.5,
    )(plan, scale, cross_high, cross_low, rims, flat, far, near)
    if split:
        return halved(voxels, rim, masked, recording, flat, outgoing[0], new_tr, rounded, far, near)
    return new_tr, spread(voxels, rim, masked, recording, rounded)


def solution(mesh):
    placed = (P("tm", "slab"), P(None, "slab"), P("tm", "slab"), P())
    return jax.shard_map(
        on_device,
        mesh=mesh,
        in_specs=placed,
        out_specs=(P("tm", "slab"), P("tm", "slab")),
        check_vma=False,
    )
```

```python
import functools

import jax
import jax.numpy as jnp
from jax import lax
from jax.experimental import pallas as pl
from jax.experimental.pallas import tpu as pltpu
from jax.sharding import PartitionSpec as P

GROUP = 128
BF = jnp.bfloat16
F32 = jnp.float32
WHOLE = pl.BlockSpec(memory_space=pltpu.VMEM)
LEFT_THERE = pl.BlockSpec(memory_space=pl.ANY)
COPIES = pltpu.SemaphoreType.DMA
shape = jax.ShapeDtypeStruct


def mm(left, right):
    return jnp.dot(left, right, preferred_element_type=F32)


def mm_t(left, right):
    return lax.dot_general(left, right, (((1,), (1,)), ((), ())), preferred_element_type=F32)


def t_mm(left, right):
    return lax.dot_general(left, right, (((0,), (0,)), ((), ())), preferred_element_type=F32)


def halves(wide):
    high = wide.astype(BF)
    return high, (wide - high.astype(F32)).astype(BF)


def living(count, block):
    slots = lax.broadcasted_iota(jnp.int32, block.shape, 1)
    return jnp.where(slots < count, block, jnp.zeros_like(block))


def diagonal(square):
    rows = lax.broadcasted_iota(jnp.int32, square.shape, 0)
    columns = lax.broadcasted_iota(jnp.int32, square.shape, 1)
    return jnp.sum(jnp.where(rows == columns, square, 0.0), axis=0, keepdims=True)


def at_end(axis):
    return lax.axis_index(axis) == lax.axis_size(axis) - 1


def odd_slab():
    return lax.axis_index("slab") % 2 == 1


def call(body, outs, in_specs, out_specs, expected, **more):
    return pl.pallas_call(
        body,
        out_shape=outs,
        in_specs=in_specs,
        out_specs=out_specs,
        compiler_params=pltpu.CompilerParams(vmem_limit_bytes=32 * 1024 * 1024),
        cost_estimate=pl.CostEstimate(
            flops=0, bytes_accessed=int(expected * 3_690_000), transcendentals=0
        ),
        **more,
    )


def copied(source, target, sem):
    copy = pltpu.make_async_copy(source, target, sem)
    copy.start()
    return copy


def first_column(which, voxels, rim):
    return pl.multiple_of(rim + which * (voxels // 2), 128)


def rolled(block):
    half = block.shape[1] // 2
    return jnp.concatenate([block[:, half:], block[:, :half]], axis=1)


def packed(which, middle):
    frames = middle.shape[0] // 2
    top, bottom = middle[:frames], middle[frames:]
    low = jnp.where(which == 0, top, rolled(top))
    high = jnp.where(which == 0, rolled(bottom), bottom)
    slots = lax.broadcasted_iota(jnp.int32, low.shape, 1)
    return jnp.where(slots < low.shape[1] // 2, low, high)


def unpacked(which, block):
    turned = rolled(block)
    top = jnp.where(which == 0, block, turned)
    bottom = jnp.where(which == 0, turned, block)
    return jnp.concatenate([top, bottom], axis=0)


def for_near_and_far(forward, backward):
    odd = odd_slab()
    return jnp.where(odd, backward, forward), jnp.where(odd, forward, backward)


def from_prev_and_next(near, far):
    odd = odd_slab()
    return jnp.where(odd, near, far), jnp.where(odd, far, near)


def rim_kernel(voxels, live, movie, foot, start, far, near, count, *rest):
    numbers, rims, traces, edge, middle, sems = rest[-6:]
    rim = edge.shape[1]
    frames = edge.shape[0]
    there = 1 - lax.axis_index("tm")
    small = [
        copied(live, numbers, sems.at[0]),
        copied(start, traces, sems.at[1]),
        copied(foot.at[pl.ds(0, rim)], rims.at[pl.ds(0, rim)], sems.at[2]),
        copied(foot.at[pl.ds(voxels, rim)], rims.at[pl.ds(rim, rim)], sems.at[3]),
        copied(movie.at[:, pl.ds(0, rim)], edge, sems.at[4]),
        copied(movie.at[:, pl.ds(voxels // 2, rim)], middle, sems.at[5]),
    ]
    large = []
    if len(rest) > 6:
        first = first_column(there, voxels, rim)
        for i in range(voxels // 2 // rim - 1):
            column = movie.at[:, pl.ds(pl.multiple_of(first + i * rim, 128), rim)]
            large.append(copied(column, rest[0].at[pl.ds(i * frames, frames)], sems.at[6 + i]))
    for copy in small:
        copy.wait()
    alive = numbers[lax.axis_index("slab")]
    count[...] = jnp.full(count.shape, alive, jnp.int32)
    seen = mm_t(living(alive, traces[...]).astype(BF), rims[...])
    backward = edge[...].astype(F32) - seen[:, :rim]
    one, two = for_near_and_far(seen[:, rim:], backward)
    near[...] = one.astype(BF)
    far[...] = two.astype(BF)
    if large:
        rest[0][(voxels // 2 // rim - 1) * frames:] = packed(there, middle[...])
    for copy in large:
        copy.wait()


def drive_kernel(voxels, count, movie, foot, start, plan, scale, cross_high, cross_low, rims, flat, masked):
    rim = foot.shape[0] - voxels
    alive = count[0:1]
    masked[:voxels] = living(alive, foot[:voxels])
    ends = living(alive, foot[voxels:])
    masked[voxels:] = jnp.where(at_end("slab"), jnp.zeros_like(ends), ends)
    rims[:rim] = -masked[:rim]
    rims[rim:] = masked[voxels:]
    flat[...] = movie[:, :rim].T
    drive = mm(movie[...], masked[:voxels])
    gram = t_mm(masked[...], masked[...])
    inverse = 1.0 / (diagonal(gram) + 1e-06)
    scale[...] = jnp.broadcast_to(inverse, scale.shape)
    gram_high, gram_low = halves(gram)
    cross_high[...] = gram_high[:GROUP, GROUP:]
    cross_low[...] = gram_low[:GROUP, GROUP:]
    current = living(alive, start[...])
    high, low = halves(current)
    for at in range(0, current.shape[1], GROUP):
        columns = slice(at, at + GROUP)
        coupled = mm(high[:, at:], gram_high[at:, columns]) + mm(high[:, at:], gram_low[at:, columns])
        coupled = coupled + mm(low[:, at:], gram_high[at:, columns])
        plan[:, columns] = current[:, columns] + (drive[:, columns] - coupled) * inverse[:, columns]


def sweep_kernel(
    plan, scale, cross_high, cross_low, rims, flat, far, near, traces, rounded, far_next, near_next
):
    rim = flat.shape[0]
    edges = rims[...]
    beside = jnp.concatenate(from_prev_and_next(near[...], far[...]), axis=1)
    stepped = plan[...] + mm(beside, edges) * scale[0:1]
    first = jnp.maximum(stepped[:, :GROUP], 0.0)
    high, low = halves(first)
    cross = cross_high[...]
    coupled = mm(
        jnp.concatenate([high, low, high], axis=1), jnp.concatenate([cross, cross, cross_low[...]], axis=0)
    )
    second = jnp.maximum(stepped[:, GROUP:] - coupled * scale[0:1, GROUP:], 0.0)
    whole = jnp.concatenate([high, second.astype(BF)], axis=1)
    rounded[...] = whole
    seen = mm_t(edges, whole)
    one, two = for_near_and_far(seen[rim:], flat[...].astype(F32) + seen[:rim])
    near_next[...] = one.astype(BF)
    far_next[...] = two.astype(BF)
    traces[:, :GROUP] = first
    traces[:, GROUP:] = second


def own_kernel(voxels, movie, foot, fit, flat, total, quad, rim_part):
    rim = flat.shape[0]
    main = voxels // 2 - rim
    traces = fit[...]
    square = t_mm(traces, traces)
    quad[...] = square
    high, low = halves(square)
    begins, ends = foot[:rim], foot[voxels:]
    rim_part[:rim] = mm(flat[...], traces) - (mm(begins, high) + mm(begins, low))
    rim_part[rim:] = -(mm(ends, high) + mm(ends, low))
    first = first_column(lax.axis_index("tm"), voxels, rim)
    total[:main] = t_mm(movie[:, pl.ds(first, main)], traces)
    total[main:] = t_mm(movie[:, voxels // 2:voxels // 2 + rim], traces)


def both_kernel(rim_part, fit, far, near, lead, sent):
    rim = lead.shape[0]
    first = lax.axis_index("tm") == 0
    before, after = from_prev_and_next(near[...], far[...])
    traces = fit[...]
    begins = rim_part[:rim] - mm(before, traces)
    ends = rim_part[rim:] + mm(after, traces)
    lead[...] = jnp.where(first, begins, ends)
    sent[...] = jnp.where(first, ends, begins).astype(BF)


def main_kernel(voxels, rim, foot, total, quad, movie, fit, traces, out, new_tr, scale, moved, sems):
    here = lax.axis_index("tm")
    frames = fit.shape[0]
    width = voxels // 2
    main = width - rim
    written = [copied(traces, new_tr, sems.at[0])]
    fitted = fit[...]
    square = quad[...] + t_mm(fitted, fitted)
    inverse = 1.0 / jnp.maximum(diagonal(square), 1.0)
    scale[...] = jnp.broadcast_to(inverse, scale.shape)
    high, low = halves(square)
    first = first_column(here, voxels, rim)
    row = pl.multiple_of(rim - here * (rim // 2), 64)
    for begin, end in ((0, width // 2), (width // 2, main), (main, width)):
        if begin < main:
            own = foot[pl.ds(pl.multiple_of(first + begin, 128), end - begin)]
            columns = range(begin // rim, end // rim)
            shown = jnp.concatenate([movie[i * frames:(i + 1) * frames] for i in columns], axis=1)
        else:
            own = foot[width:width + rim]
            shown = unpacked(here, movie[main // rim * frames:])
        part = total[begin:end] + t_mm(shown, fitted) - (mm(own, high) + mm(own, low))
        moved[begin:end] = jnp.maximum(own.astype(F32) + part * inverse, 0.0).astype(BF)
        if begin < main:
            target = out.at[pl.ds(row + begin, end - begin)]
            written.append(copied(moved.at[pl.ds(begin, end - begin)], target, sems.at[len(written)]))
        else:
            half = rim // 2
            source = moved.at[pl.ds(pl.multiple_of(main + here * half, 64), half)]
            target = out.at[pl.ds(pl.multiple_of((1 - here) * (out.shape[0] - half), 64), half)]
            written.append(copied(source, target, sems.at[len(written)]))
    for copy in written:
        copy.wait()


def edge_kernel(voxels, sofar, foot, lead, came, scale, out, moved, sem):
    rim = lead.shape[0]
    here = lax.axis_index("tm")
    own = foot[pl.ds(pl.multiple_of(here * voxels, 128), rim)].astype(F32)
    moved[...] = jnp.maximum(own + (lead[...] + came[...].astype(F32)) * scale[0:1], 0.0).astype(BF)
    row = pl.multiple_of(here * (out.shape[0] - rim), 64)
    copied(moved, out.at[pl.ds(row, rim)], sem).wait()


def swapped(block, first):
    route = [(i, i + 1) for i in range(first, lax.axis_size("slab") - 1, 2)]
    return lax.ppermute(block, "slab", [(j, i) for i, j in route] + route)


def halved(voxels, rim, foot, recording, flat, outgoing, new_tr, rounded, far, near):
    frames = recording.shape[0]
    extended, neurons = foot.shape
    width, share = voxels // 2, extended // 2
    across = [(0, 1), (1, 0)]
    movie = lax.ppermute(outgoing, "tm", across)
    far = swapped(far, 1)
    near = swapped(near, 0)
    other = lax.ppermute(rounded, "tm", across)
    total, quad, rim_part = call(
        functools.partial(own_kernel, voxels),
        [
            shape((width, neurons), F32),
            shape((neurons, neurons), F32),
            shape((2 * rim, neurons), F32),
        ],
        [WHOLE] * 4,
        [WHOLE] * 3,
        0.6,
    )(recording, foot, rounded, flat)
    lead, sent = call(
        both_kernel,
        [shape((rim, neurons), F32), pltpu.VMEM((rim, neurons), BF)],
        [WHOLE] * 4,
        [WHOLE] * 2,
        0.3,
    )(rim_part, rounded, far, near)
    came = lax.ppermute(sent, "tm", across)
    sofar, new_tr, scale = call(
        functools.partial(main_kernel, voxels, rim),
        [pltpu.HBM((share, neurons), BF), pltpu.HBM((frames, neurons), F32), shape((8, neurons), F32)],
        [WHOLE] * 6,
        [LEFT_THERE] * 2 + [WHOLE],
        2.0,
        scratch_shapes=[pltpu.VMEM((width, neurons), BF), COPIES((4,))],
    )(foot, total, quad, movie, other, new_tr)
    new_foot = call(
        functools.partial(edge_kernel, voxels),
        pltpu.HBM((share, neurons), BF),
        [LEFT_THERE] + [WHOLE] * 4,
        LEFT_THERE,
        0.8,
        input_output_aliases={0: 0},
        scratch_shapes=[pltpu.VMEM((rim, neurons), BF), COPIES],
    )(sofar, foot, lead, came, scale)
    return new_tr, new_foot


def spread(voxels, rim, foot, recording, rounded):
    slabs, parts = lax.axis_size("slab"), lax.axis_size("tm")
    extended, neurons = foot.shape
    share = extended // parts
    here = lax.axis_index("tm")
    closing = here == parts - 1
    exact = lax.Precision.HIGHEST
    cut = voxels - (share - rim)
    columns = jnp.concatenate([recording[:, :cut], recording[:, :rim], recording[:, cut:]], 1)
    movie = lax.all_to_all(columns, "tm", split_axis=1, concat_axis=0, tiled=True)
    fit = lax.all_gather(rounded, "tm", axis=0, tiled=True)
    edge = jnp.where(here == 0, foot[voxels:], foot[:rim])
    seen = movie[:, :rim].astype(F32)
    sent = jnp.where(here == 0, 0.0, seen) - mm_t(fit, edge)
    ahead = [(i * parts, (i + 1) * parts) for i in range(slabs - 1)]
    behind = [((i + 2) * parts - 1, (i + 1) * parts - 1) for i in range(slabs - 1)]
    lead = jnp.where(closing, 0.0, seen) + lax.ppermute(sent, ("slab", "tm"), ahead + behind)
    lead = lax.dot_general(lead, fit.astype(F32), (((0,), (0,)), ((), ())), precision=exact)
    inner = t_mm(movie[:, rim:], fit)
    total = jnp.where(
        closing, jnp.concatenate([inner, lead], 0), jnp.concatenate([lead, inner], 0)
    )
    square = t_mm(fit, fit)
    own = lax.dynamic_slice_in_dim(foot, here * share, share, 0).astype(F32)
    total = total - jnp.dot(own, square, precision=exact)
    return jnp.maximum(own + total / jnp.maximum(jnp.diagonal(square), 1.0), 0.0).astype(BF)


def on_device(recording, footprints, traces, live_count):
    frames, voxels = recording.shape
    extended, neurons = footprints.shape
    rim = extended - voxels
    main = voxels // 2 // rim - 1
    split = lax.axis_size("tm") == 2
    share_shape = [pltpu.VMEM((main * frames + frames // 2, rim), BF)] if split else []
    pinned = [
        pltpu.with_memory_space_constraint(x, pltpu.HBM)
        for x in (live_count, recording, footprints, traces)
    ]
    far, near, count, *outgoing = call(
        functools.partial(rim_kernel, voxels),
        [
            pltpu.VMEM((frames, rim), BF),
            pltpu.VMEM((frames, rim), BF),
            pltpu.VMEM((8, neurons), jnp.int32),
        ]
        + share_shape,
        [LEFT_THERE] * 4,
        [WHOLE] * (3 + len(share_shape)),
        1.5,
        scratch_shapes=[
            pltpu.SMEM(live_count.shape, jnp.int32),
            pltpu.VMEM((2 * rim, neurons), BF),
            pltpu.VMEM((frames, neurons), F32),
            pltpu.VMEM((frames, rim), BF),
            pltpu.VMEM((frames, rim), BF),
            COPIES((6 + main,)),
        ],
    )(*pinned)
    far = swapped(far, 1)
    near = swapped(near, 0)
    plan, scale, cross_high, cross_low, rims, flat, masked = call(
        functools.partial(drive_kernel, voxels),
        [
            shape((frames, neurons), F32),
            shape((8, neurons), F32),
            shape((GROUP, GROUP), BF),
            shape((GROUP, GROUP), BF),
            shape((2 * rim, neurons), BF),
            shape((rim, frames), BF),
            pltpu.VMEM((extended, neurons), BF),
        ],
        [WHOLE] * 4,
        [WHOLE] * 7,
        1.2,
    )(count, recording, footprints, traces)
    new_tr, rounded, far, near = call(
        sweep_kernel,
        [
            pltpu.VMEM((frames, neurons), F32),
            pltpu.VMEM((frames, neurons), BF),
            pltpu.VMEM((rim, frames), BF),
            pltpu.VMEM((rim, frames), BF),
        ],
        [WHOLE] * 8,
        [WHOLE] * 4,
        0.5,
    )(plan, scale, cross_high, cross_low, rims, flat, far, near)
    if split:
        return halved(voxels, rim, masked, recording, flat, outgoing[0], new_tr, rounded, far, near)
    return new_tr, spread(voxels, rim, masked, recording, rounded)


def solution(mesh):
    placed = (P("tm", "slab"), P(None, "slab"), P("tm", "slab"), P())
    return jax.shard_map(
        on_device,
        mesh=mesh,
        in_specs=placed,
        out_specs=(P("tm", "slab"), P("tm", "slab")),
        check_vma=False,
    )
```

```python
import functools

import jax
import jax.numpy as jnp
from jax import lax
from jax.experimental import pallas as pl
from jax.experimental.pallas import tpu as pltpu
from jax.sharding import PartitionSpec as P

GROUP = 128
BF = jnp.bfloat16
F32 = jnp.float32
WHOLE = pl.BlockSpec(memory_space=pltpu.VMEM)
LEFT_THERE = pl.BlockSpec(memory_space=pl.ANY)
COPIES = pltpu.SemaphoreType.DMA
shape = jax.ShapeDtypeStruct


def mm(left, right):
    return jnp.dot(left, right, preferred_element_type=F32)


def mm_t(left, right):
    return lax.dot_general(left, right, (((1,), (1,)), ((), ())), preferred_element_type=F32)


def t_mm(left, right):
    return lax.dot_general(left, right, (((0,), (0,)), ((), ())), preferred_element_type=F32)


def halves(wide):
    high = wide.astype(BF)
    return high, (wide - high.astype(F32)).astype(BF)


def living(count, block):
    slots = lax.broadcasted_iota(jnp.int32, block.shape, 1)
    return jnp.where(slots < count, block, jnp.zeros_like(block))


def diagonal(square):
    rows = lax.broadcasted_iota(jnp.int32, square.shape, 0)
    columns = lax.broadcasted_iota(jnp.int32, square.shape, 1)
    return jnp.sum(jnp.where(rows == columns, square, 0.0), axis=0, keepdims=True)


def at_end(axis):
    return lax.axis_index(axis) == lax.axis_size(axis) - 1


def odd_slab():
    return lax.axis_index("slab") % 2 == 1


def call(body, outs, in_specs, out_specs, expected, **more):
    return pl.pallas_call(
        body,
        out_shape=outs,
        in_specs=in_specs,
        out_specs=out_specs,
        compiler_params=pltpu.CompilerParams(vmem_limit_bytes=32 * 1024 * 1024),
        cost_estimate=pl.CostEstimate(
            flops=0, bytes_accessed=int(expected * 3_690_000), transcendentals=0
        ),
        **more,
    )


def copied(source, target, sem):
    copy = pltpu.make_async_copy(source, target, sem)
    copy.start()
    return copy


def first_column(which, voxels, rim):
    return pl.multiple_of(rim + which * (voxels // 2), 128)


def rolled(block):
    half = block.shape[1] // 2
    return jnp.concatenate([block[:, half:], block[:, :half]], axis=1)


def packed(which, middle):
    frames = middle.shape[0] // 2
    top, bottom = middle[:frames], middle[frames:]
    low = jnp.where(which == 0, top, rolled(top))
    high = jnp.where(which == 0, rolled(bottom), bottom)
    slots = lax.broadcasted_iota(jnp.int32, low.shape, 1)
    return jnp.where(slots < low.shape[1] // 2, low, high)


def unpacked(which, block):
    turned = rolled(block)
    top = jnp.where(which == 0, block, turned)
    bottom = jnp.where(which == 0, turned, block)
    return jnp.concatenate([top, bottom], axis=0)


def for_near_and_far(forward, backward):
    odd = odd_slab()
    return jnp.where(odd, backward, forward), jnp.where(odd, forward, backward)


def from_prev_and_next(near, far):
    odd = odd_slab()
    return jnp.where(odd, near, far), jnp.where(odd, far, near)


def rim_kernel(voxels, live, movie, foot, start, far, near, count, *rest):
    numbers, rims, traces, edge, middle, sems = rest[-6:]
    rim = edge.shape[1]
    frames = edge.shape[0]
    there = 1 - lax.axis_index("tm")
    small = [
        copied(live, numbers, sems.at[0]),
        copied(start, traces, sems.at[1]),
        copied(foot.at[pl.ds(0, rim)], rims.at[pl.ds(0, rim)], sems.at[2]),
        copied(foot.at[pl.ds(voxels, rim)], rims.at[pl.ds(rim, rim)], sems.at[3]),
        copied(movie.at[:, pl.ds(0, rim)], edge, sems.at[4]),
        copied(movie.at[:, pl.ds(voxels // 2, rim)], middle, sems.at[5]),
    ]
    large = []
    if len(rest) > 6:
        first = first_column(there, voxels, rim)
        for i in range(voxels // 2 // rim - 1):
            column = movie.at[:, pl.ds(pl.multiple_of(first + i * rim, 128), rim)]
            large.append(copied(column, rest[0].at[pl.ds(i * frames, frames)], sems.at[6 + i]))
    for copy in small:
        copy.wait()
    alive = numbers[lax.axis_index("slab")]
    count[...] = jnp.full(count.shape, alive, jnp.int32)
    seen = mm_t(living(alive, traces[...]).astype(BF), rims[...])
    backward = edge[...].astype(F32) - seen[:, :rim]
    one, two = for_near_and_far(seen[:, rim:], backward)
    near[...] = one.astype(BF)
    far[...] = two.astype(BF)
    if large:
        rest[0][(voxels // 2 // rim - 1) * frames:] = packed(there, middle[...])
    for copy in large:
        copy.wait()


def drive_kernel(voxels, count, movie, foot, start, plan, scale, cross_high, cross_low, rims, flat, masked):
    rim = foot.shape[0] - voxels
    alive = count[0:1]
    masked[:voxels] = living(alive, foot[:voxels])
    ends = living(alive, foot[voxels:])
    masked[voxels:] = jnp.where(at_end("slab"), jnp.zeros_like(ends), ends)
    rims[:rim] = -masked[:rim]
    rims[rim:] = masked[voxels:]
    flat[...] = movie[:, :rim].T
    drive = mm(movie[...], masked[:voxels])
    gram = t_mm(masked[...], masked[...])
    inverse = 1.0 / (diagonal(gram) + 1e-06)
    scale[...] = jnp.broadcast_to(inverse, scale.shape)
    gram_high, gram_low = halves(gram)
    cross_high[...] = gram_high[:GROUP, GROUP:]
    cross_low[...] = gram_low[:GROUP, GROUP:]
    current = living(alive, start[...])
    high, low = halves(current)
    for at in range(0, current.shape[1], GROUP):
        columns = slice(at, at + GROUP)
        coupled = mm(high[:, at:], gram_high[at:, columns]) + mm(high[:, at:], gram_low[at:, columns])
        coupled = coupled + mm(low[:, at:], gram_high[at:, columns])
        plan[:, columns] = current[:, columns] + (drive[:, columns] - coupled) * inverse[:, columns]


def sweep_kernel(
    plan, scale, cross_high, cross_low, rims, flat, far, near, traces, rounded, far_next, near_next
):
    rim = flat.shape[0]
    edges = rims[...]
    beside = jnp.concatenate(from_prev_and_next(near[...], far[...]), axis=1)
    stepped = plan[...] + mm(beside, edges) * scale[0:1]
    first = jnp.maximum(stepped[:, :GROUP], 0.0)
    high, low = halves(first)
    cross = cross_high[...]
    coupled = mm(
        jnp.concatenate([high, low, high], axis=1), jnp.concatenate([cross, cross, cross_low[...]], axis=0)
    )
    second = jnp.maximum(stepped[:, GROUP:] - coupled * scale[0:1, GROUP:], 0.0)
    whole = jnp.concatenate([high, second.astype(BF)], axis=1)
    rounded[...] = whole
    seen = mm_t(edges, whole)
    one, two = for_near_and_far(seen[rim:], flat[...].astype(F32) + seen[:rim])
    near_next[...] = one.astype(BF)
    far_next[...] = two.astype(BF)
    traces[:, :GROUP] = first
    traces[:, GROUP:] = second


def own_kernel(voxels, movie, foot, fit, flat, total, quad, rim_part):
    rim = flat.shape[0]
    main = voxels // 2 - rim
    traces = fit[...]
    square = t_mm(traces, traces)
    quad[...] = square
    high, low = halves(square)
    begins, ends = foot[:rim], foot[voxels:]
    rim_part[:rim] = mm(flat[...], traces) - (mm(begins, high) + mm(begins, low))
    rim_part[rim:] = -(mm(ends, high) + mm(ends, low))
    first = first_column(lax.axis_index("tm"), voxels, rim)
    total[:main] = t_mm(movie[:, pl.ds(first, main)], traces)
    total[main:] = t_mm(movie[:, voxels // 2:voxels // 2 + rim], traces)


def begins_kernel(rim_part, fit, far, near, sent):
    before, _ = from_prev_and_next(near[...], far[...])
    sent[...] = (rim_part[:sent.shape[0]] - mm(before, fit[...])).astype(BF)


def ends_kernel(rim_part, fit, far_closing, far_opening, near, lead, sent):
    rim = lead.shape[0]
    first = lax.axis_index("tm") == 0
    far = jnp.where(first, far_opening[...], far_closing[...])
    before, after = from_prev_and_next(near[...], far)
    traces = fit[...]
    ends = rim_part[rim:] + mm(after, traces)
    lead[...] = jnp.where(first, rim_part[:rim] - mm(before, traces), ends)
    sent[...] = ends.astype(BF)


def main_kernel(voxels, rim, foot, total, quad, movie, fit, traces, out, new_tr, scale, moved, sems):
    here = lax.axis_index("tm")
    frames = fit.shape[0]
    width = voxels // 2
    main = width - rim
    written = [copied(traces, new_tr, sems.at[0])]
    fitted = fit[...]
    square = quad[...] + t_mm(fitted, fitted)
    inverse = 1.0 / jnp.maximum(diagonal(square), 1.0)
    scale[...] = jnp.broadcast_to(inverse, scale.shape)
    high, low = halves(square)
    first = first_column(here, voxels, rim)
    row = pl.multiple_of(rim - here * (rim // 2), 64)
    for begin, end in ((0, width // 2), (width // 2, main), (main, width)):
        if begin < main:
            own = foot[pl.ds(pl.multiple_of(first + begin, 128), end - begin)]
            columns = range(begin // rim, end // rim)
            shown = jnp.concatenate([movie[i * frames:(i + 1) * frames] for i in columns], axis=1)
        else:
            own = foot[width:width + rim]
            shown = unpacked(here, movie[main // rim * frames:])
        part = total[begin:end] + t_mm(shown, fitted) - (mm(own, high) + mm(own, low))
        moved[begin:end] = jnp.maximum(own.astype(F32) + part * inverse, 0.0).astype(BF)
        if begin < main:
            target = out.at[pl.ds(row + begin, end - begin)]
            written.append(copied(moved.at[pl.ds(begin, end - begin)], target, sems.at[len(written)]))
        else:
            half = rim // 2
            source = moved.at[pl.ds(pl.multiple_of(main + here * half, 64), half)]
            target = out.at[pl.ds(pl.multiple_of((1 - here) * (out.shape[0] - half), 64), half)]
            written.append(copied(source, target, sems.at[len(written)]))
    for copy in written:
        copy.wait()


def edge_kernel(voxels, sofar, foot, lead, begins, ends, scale, out, moved, sem):
    rim = lead.shape[0]
    here = lax.axis_index("tm")
    came = jnp.where(here == 0, begins[...], ends[...]).astype(F32)
    own = foot[pl.ds(pl.multiple_of(here * voxels, 128), rim)].astype(F32)
    moved[...] = jnp.maximum(own + (lead[...] + came) * scale[0:1], 0.0).astype(BF)
    row = pl.multiple_of(here * (out.shape[0] - rim), 64)
    copied(moved, out.at[pl.ds(row, rim)], sem).wait()


def swapped(block, first):
    route = [(i, i + 1) for i in range(first, lax.axis_size("slab") - 1, 2)]
    return lax.ppermute(block, "slab", [(j, i) for i, j in route] + route)


def halved(voxels, rim, foot, recording, flat, outgoing, new_tr, rounded, far, near):
    frames = recording.shape[0]
    extended, neurons = foot.shape
    width, share = voxels // 2, extended // 2
    across = [(0, 1), (1, 0)]
    movie = lax.ppermute(outgoing, "tm", across)
    slabs = lax.axis_size("slab")
    far_closing, far_opening = [
        lax.ppermute(
            far,
            ("slab", "tm"),
            [pair for i in range(2, 2 * slabs - 2, 4) for pair in ((i + t, i + 2 + t), (i + 2 + t, i + t))],
        )
        for t in (1, 0)
    ]
    near = swapped(near, 0)
    ready, near = lax.optimization_barrier((rounded, near))
    other = lax.ppermute(ready, "tm", across)
    total, quad, rim_part = call(
        functools.partial(own_kernel, voxels),
        [
            shape((width, neurons), F32),
            shape((neurons, neurons), F32),
            shape((2 * rim, neurons), F32),
        ],
        [WHOLE] * 4,
        [WHOLE] * 3,
        0.6,
    )(recording, foot, rounded, flat)
    begins = call(
        begins_kernel,
        pltpu.VMEM((rim, neurons), BF),
        [WHOLE] * 4,
        WHOLE,
        0.2,
    )(rim_part, rounded, far_closing, near)
    begins_sent = begins
    begins = lax.ppermute(begins, "tm", [(1, 0)])
    far_opening, _ = lax.optimization_barrier((far_opening, begins_sent))
    lead, ends = call(
        ends_kernel,
        [shape((rim, neurons), F32), pltpu.VMEM((rim, neurons), BF)],
        [WHOLE] * 5,
        [WHOLE] * 2,
        0.2,
    )(rim_part, lax.optimization_barrier((rounded, movie))[0], far_closing, far_opening, near)
    ends = lax.ppermute(ends, "tm", [(0, 1)])
    sofar, new_tr, scale = call(
        functools.partial(main_kernel, voxels, rim),
        [pltpu.HBM((share, neurons), BF), pltpu.HBM((frames, neurons), F32), shape((8, neurons), F32)],
        [WHOLE] * 6,
        [LEFT_THERE] * 2 + [WHOLE],
        2.0,
        scratch_shapes=[pltpu.VMEM((width, neurons), BF), COPIES((4,))],
    )(foot, total, quad, movie, other, new_tr)
    new_foot = call(
        functools.partial(edge_kernel, voxels),
        pltpu.HBM((share, neurons), BF),
        [LEFT_THERE] + [WHOLE] * 5,
        LEFT_THERE,
        0.8,
        input_output_aliases={0: 0},
        scratch_shapes=[pltpu.VMEM((rim, neurons), BF), COPIES],
    )(sofar, foot, lead, begins, ends, scale)
    return new_tr, new_foot


def spread(voxels, rim, foot, recording, rounded):
    slabs, parts = lax.axis_size("slab"), lax.axis_size("tm")
    extended, neurons = foot.shape
    share = extended // parts
    here = lax.axis_index("tm")
    closing = here == parts - 1
    exact = lax.Precision.HIGHEST
    cut = voxels - (share - rim)
    columns = jnp.concatenate([recording[:, :cut], recording[:, :rim], recording[:, cut:]], 1)
    movie = lax.all_to_all(columns, "tm", split_axis=1, concat_axis=0, tiled=True)
    fit = lax.all_gather(rounded, "tm", axis=0, tiled=True)
    edge = jnp.where(here == 0, foot[voxels:], foot[:rim])
    seen = movie[:, :rim].astype(F32)
    sent = jnp.where(here == 0, 0.0, seen) - mm_t(fit, edge)
    ahead = [(i * parts, (i + 1) * parts) for i in range(slabs - 1)]
    behind = [((i + 2) * parts - 1, (i + 1) * parts - 1) for i in range(slabs - 1)]
    lead = jnp.where(closing, 0.0, seen) + lax.ppermute(sent, ("slab", "tm"), ahead + behind)
    lead = lax.dot_general(lead, fit.astype(F32), (((0,), (0,)), ((), ())), precision=exact)
    inner = t_mm(movie[:, rim:], fit)
    total = jnp.where(
        closing, jnp.concatenate([inner, lead], 0), jnp.concatenate([lead, inner], 0)
    )
    square = t_mm(fit, fit)
    own = lax.dynamic_slice_in_dim(foot, here * share, share, 0).astype(F32)
    total = total - jnp.dot(own, square, precision=exact)
    return jnp.maximum(own + total / jnp.maximum(jnp.diagonal(square), 1.0), 0.0).astype(BF)


def on_device(recording, footprints, traces, live_count):
    frames, voxels = recording.shape
    extended, neurons = footprints.shape
    rim = extended - voxels
    main = voxels // 2 // rim - 1
    split = lax.axis_size("tm") == 2
    share_shape = [pltpu.VMEM((main * frames + frames // 2, rim), BF)] if split else []
    pinned = [
        pltpu.with_memory_space_constraint(x, pltpu.HBM)
        for x in (live_count, recording, footprints, traces)
    ]
    far, near, count, *outgoing = call(
        functools.partial(rim_kernel, voxels),
        [
            pltpu.VMEM((frames, rim), BF),
            pltpu.VMEM((frames, rim), BF),
            pltpu.VMEM((8, neurons), jnp.int32),
        ]
        + share_shape,
        [LEFT_THERE] * 4,
        [WHOLE] * (3 + len(share_shape)),
        1.5,
        scratch_shapes=[
            pltpu.SMEM(live_count.shape, jnp.int32),
            pltpu.VMEM((2 * rim, neurons), BF),
            pltpu.VMEM((frames, neurons), F32),
            pltpu.VMEM((frames, rim), BF),
            pltpu.VMEM((frames, rim), BF),
            COPIES((6 + main,)),
        ],
    )(*pinned)
    far = swapped(far, 1)
    near = swapped(near, 0)
    plan, scale, cross_high, cross_low, rims, flat, masked = call(
        functools.partial(drive_kernel, voxels),
        [
            shape((frames, neurons), F32),
            shape((8, neurons), F32),
            shape((GROUP, GROUP), BF),
            shape((GROUP, GROUP), BF),
            shape((2 * rim, neurons), BF),
            shape((rim, frames), BF),
            pltpu.VMEM((extended, neurons), BF),
        ],
        [WHOLE] * 4,
        [WHOLE] * 7,
        1.2,
    )(count, recording, footprints, traces)
    new_tr, rounded, far, near = call(
        sweep_kernel,
        [
            pltpu.VMEM((frames, neurons), F32),
            pltpu.VMEM((frames, neurons), BF),
            pltpu.VMEM((rim, frames), BF),
            pltpu.VMEM((rim, frames), BF),
        ],
        [WHOLE] * 8,
        [WHOLE] * 4,
        0.5,
    )(plan, scale, cross_high, cross_low, rims, flat, far, near)
    if split:
        return halved(voxels, rim, masked, recording, flat, outgoing[0], new_tr, rounded, far, near)
    return new_tr, spread(voxels, rim, masked, recording, rounded)


def solution(mesh):
    placed = (P("tm", "slab"), P(None, "slab"), P("tm", "slab"), P())
    return jax.shard_map(
        on_device,
        mesh=mesh,
        in_specs=placed,
        out_specs=(P("tm", "slab"), P("tm", "slab")),
        check_vma=False,
    )
```

```python
import functools

import jax
import jax.numpy as jnp
from jax import lax
from jax.experimental import pallas as pl
from jax.experimental.pallas import tpu as pltpu
from jax.sharding import PartitionSpec as P

GROUP = 128
BF = jnp.bfloat16
F32 = jnp.float32
WHOLE = pl.BlockSpec(memory_space=pltpu.VMEM)
LEFT_THERE = pl.BlockSpec(memory_space=pl.ANY)
COPIES = pltpu.SemaphoreType.DMA
shape = jax.ShapeDtypeStruct


def mm(left, right):
    return jnp.dot(left, right, preferred_element_type=F32)


def mm_t(left, right):
    return lax.dot_general(left, right, (((1,), (1,)), ((), ())), preferred_element_type=F32)


def t_mm(left, right):
    return lax.dot_general(left, right, (((0,), (0,)), ((), ())), preferred_element_type=F32)


def halves(wide):
    high = wide.astype(BF)
    return high, (wide - high.astype(F32)).astype(BF)


def living(count, block):
    slots = lax.broadcasted_iota(jnp.int32, block.shape, 1)
    return jnp.where(slots < count, block, jnp.zeros_like(block))


def diagonal(square):
    rows = lax.broadcasted_iota(jnp.int32, square.shape, 0)
    columns = lax.broadcasted_iota(jnp.int32, square.shape, 1)
    return jnp.sum(jnp.where(rows == columns, square, 0.0), axis=0, keepdims=True)


def at_end(axis):
    return lax.axis_index(axis) == lax.axis_size(axis) - 1


def odd_slab():
    return lax.axis_index("slab") % 2 == 1


def call(body, outs, in_specs, out_specs, expected, **more):
    return pl.pallas_call(
        body,
        out_shape=outs,
        in_specs=in_specs,
        out_specs=out_specs,
        compiler_params=pltpu.CompilerParams(vmem_limit_bytes=32 * 1024 * 1024),
        cost_estimate=pl.CostEstimate(
            flops=0, bytes_accessed=int(expected * 3_690_000), transcendentals=0
        ),
        **more,
    )


def copied(source, target, sem):
    copy = pltpu.make_async_copy(source, target, sem)
    copy.start()
    return copy


def first_column(which, voxels, rim):
    return pl.multiple_of(rim + which * (voxels // 2), 128)


def rolled(block):
    half = block.shape[1] // 2
    return jnp.concatenate([block[:, half:], block[:, :half]], axis=1)


def packed(which, middle):
    frames = middle.shape[0] // 2
    top, bottom = middle[:frames], middle[frames:]
    low = jnp.where(which == 0, top, rolled(top))
    high = jnp.where(which == 0, rolled(bottom), bottom)
    slots = lax.broadcasted_iota(jnp.int32, low.shape, 1)
    return jnp.where(slots < low.shape[1] // 2, low, high)


def unpacked(which, block):
    turned = rolled(block)
    top = jnp.where(which == 0, block, turned)
    bottom = jnp.where(which == 0, turned, block)
    return jnp.concatenate([top, bottom], axis=0)


def for_near_and_far(forward, backward):
    odd = odd_slab()
    return jnp.where(odd, backward, forward), jnp.where(odd, forward, backward)


def from_prev_and_next(near, far):
    odd = odd_slab()
    return jnp.where(odd, near, far), jnp.where(odd, far, near)


def rim_kernel(voxels, live, movie, foot, start, far, near, count, traces, *rest):
    numbers, rims, edge, middle, sems = rest[-5:]
    rim = edge.shape[1]
    frames = edge.shape[0]
    there = 1 - lax.axis_index("tm")
    small = [
        copied(live, numbers, sems.at[0]),
        copied(start, traces, sems.at[1]),
        copied(foot.at[pl.ds(0, rim)], rims.at[pl.ds(0, rim)], sems.at[2]),
        copied(foot.at[pl.ds(voxels, rim)], rims.at[pl.ds(rim, rim)], sems.at[3]),
        copied(movie.at[:, pl.ds(0, rim)], edge, sems.at[4]),
        copied(movie.at[:, pl.ds(voxels // 2, rim)], middle, sems.at[5]),
    ]
    large = []
    if len(rest) > 5:
        first = first_column(there, voxels, rim)
        for i in range(voxels // 2 // rim - 1):
            column = movie.at[:, pl.ds(pl.multiple_of(first + i * rim, 128), rim)]
            large.append(copied(column, rest[0].at[pl.ds(i * frames, frames)], sems.at[6 + i]))
    for copy in small:
        copy.wait()
    alive = numbers[lax.axis_index("slab")]
    count[...] = jnp.full(count.shape, alive, jnp.int32)
    seen = mm_t(living(alive, traces[...]).astype(BF), rims[...])
    backward = edge[...].astype(F32) - seen[:, :rim]
    one, two = for_near_and_far(seen[:, rim:], backward)
    near[...] = one.astype(BF)
    far[...] = two.astype(BF)
    if large:
        rest[0][(voxels // 2 // rim - 1) * frames:] = packed(there, middle[...])
    for copy in large:
        copy.wait()


def drive_kernel(
    voxels, count, movie, foot, start, plan, scale, cross_high, cross_low, rims, flat, masked, shown, sems
):
    rim = foot.shape[0] - voxels
    step = voxels // 2
    loads = []
    for i in range(2):
        columns = pl.ds(i * step, step)
        loads.append(copied(movie.at[:, columns], shown.at[:, columns], sems.at[i]))
    alive = count[0:1]
    masked[:voxels] = living(alive, foot[:voxels])
    ends = living(alive, foot[voxels:])
    masked[voxels:] = jnp.where(at_end("slab"), jnp.zeros_like(ends), ends)
    rims[:rim] = -masked[:rim]
    rims[rim:] = masked[voxels:]
    gram = t_mm(masked[...], masked[...])
    loads[0].wait()
    flat[...] = shown[:, :rim].T
    drive = mm(shown[:, :step], masked[:step])
    loads[1].wait()
    drive = drive + mm(shown[:, step:], masked[step:voxels])
    inverse = 1.0 / (diagonal(gram) + 1e-06)
    scale[...] = jnp.broadcast_to(inverse, scale.shape)
    gram_high, gram_low = halves(gram)
    cross_high[...] = gram_high[:GROUP, GROUP:]
    cross_low[...] = gram_low[:GROUP, GROUP:]
    current = living(alive, start[...])
    high, low = halves(current)
    for at in range(0, current.shape[1], GROUP):
        columns = slice(at, at + GROUP)
        coupled = mm(high[:, at:], gram_high[at:, columns]) + mm(high[:, at:], gram_low[at:, columns])
        coupled = coupled + mm(low[:, at:], gram_high[at:, columns])
        plan[:, columns] = current[:, columns] + (drive[:, columns] - coupled) * inverse[:, columns]


def sweep_kernel(
    plan, scale, cross_high, cross_low, rims, flat, far, near, traces, rounded, far_next, near_next
):
    rim = flat.shape[0]
    edges = rims[...]
    beside = jnp.concatenate(from_prev_and_next(near[...], far[...]), axis=1)
    stepped = plan[...] + mm(beside, edges) * scale[0:1]
    first = jnp.maximum(stepped[:, :GROUP], 0.0)
    high, low = halves(first)
    cross = cross_high[...]
    coupled = mm(
        jnp.concatenate([high, low, high], axis=1), jnp.concatenate([cross, cross, cross_low[...]], axis=0)
    )
    second = jnp.maximum(stepped[:, GROUP:] - coupled * scale[0:1, GROUP:], 0.0)
    whole = jnp.concatenate([high, second.astype(BF)], axis=1)
    rounded[...] = whole
    seen = mm_t(edges, whole)
    one, two = for_near_and_far(seen[rim:], flat[...].astype(F32) + seen[:rim])
    near_next[...] = one.astype(BF)
    far_next[...] = two.astype(BF)
    traces[:, :GROUP] = first
    traces[:, GROUP:] = second


def own_kernel(voxels, movie, foot, fit, flat, total, quad, rim_part):
    rim = flat.shape[0]
    main = voxels // 2 - rim
    traces = fit[...]
    square = t_mm(traces, traces)
    quad[...] = square
    high, low = halves(square)
    begins, ends = foot[:rim], foot[voxels:]
    rim_part[:rim] = mm(flat[...], traces) - (mm(begins, high) + mm(begins, low))
    rim_part[rim:] = -(mm(ends, high) + mm(ends, low))
    first = first_column(lax.axis_index("tm"), voxels, rim)
    total[:main] = t_mm(movie[:, pl.ds(first, main)], traces)
    total[main:] = t_mm(movie[:, voxels // 2:voxels // 2 + rim], traces)


def both_kernel(rim_part, fit, far, near, lead, sent):
    rim = lead.shape[0]
    first = lax.axis_index("tm") == 0
    before, after = from_prev_and_next(near[...], far[...])
    traces = fit[...]
    begins = rim_part[:rim] - mm(before, traces)
    ends = rim_part[rim:] + mm(after, traces)
    lead[...] = jnp.where(first, begins, ends)
    sent[...] = jnp.where(first, ends, begins).astype(BF)


def main_kernel(voxels, rim, foot, total, quad, movie, fit, traces, out, new_tr, scale, moved, sems):
    here = lax.axis_index("tm")
    frames = fit.shape[0]
    width = voxels // 2
    main = width - rim
    written = [copied(traces, new_tr, sems.at[0])]
    fitted = fit[...]
    square = quad[...] + t_mm(fitted, fitted)
    inverse = 1.0 / jnp.maximum(diagonal(square), 1.0)
    scale[...] = jnp.broadcast_to(inverse, scale.shape)
    high, low = halves(square)
    first = first_column(here, voxels, rim)
    row = pl.multiple_of(rim - here * (rim // 2), 64)
    for begin, end in ((0, width // 2), (width // 2, main), (main, width)):
        if begin < main:
            own = foot[pl.ds(pl.multiple_of(first + begin, 128), end - begin)]
            columns = range(begin // rim, end // rim)
            shown = jnp.concatenate([movie[i * frames:(i + 1) * frames] for i in columns], axis=1)
        else:
            own = foot[width:width + rim]
            shown = unpacked(here, movie[main // rim * frames:])
        part = total[begin:end] + t_mm(shown, fitted) - (mm(own, high) + mm(own, low))
        moved[begin:end] = jnp.maximum(own.astype(F32) + part * inverse, 0.0).astype(BF)
        if begin < main:
            target = out.at[pl.ds(row + begin, end - begin)]
            written.append(copied(moved.at[pl.ds(begin, end - begin)], target, sems.at[len(written)]))
        else:
            half = rim // 2
            source = moved.at[pl.ds(pl.multiple_of(main + here * half, 64), half)]
            target = out.at[pl.ds(pl.multiple_of((1 - here) * (out.shape[0] - half), 64), half)]
            written.append(copied(source, target, sems.at[len(written)]))
    for copy in written:
        copy.wait()


def edge_kernel(voxels, sofar, foot, lead, came, scale, out, moved, sem):
    rim = lead.shape[0]
    here = lax.axis_index("tm")
    own = foot[pl.ds(pl.multiple_of(here * voxels, 128), rim)].astype(F32)
    moved[...] = jnp.maximum(own + (lead[...] + came[...].astype(F32)) * scale[0:1], 0.0).astype(BF)
    row = pl.multiple_of(here * (out.shape[0] - rim), 64)
    copied(moved, out.at[pl.ds(row, rim)], sem).wait()


def swapped(block, first):
    route = [(i, i + 1) for i in range(first, lax.axis_size("slab") - 1, 2)]
    return lax.ppermute(block, "slab", [(j, i) for i, j in route] + route)


def halved(voxels, rim, foot, recording, flat, outgoing, new_tr, rounded, far, near):
    frames = recording.shape[0]
    extended, neurons = foot.shape
    width, share = voxels // 2, extended // 2
    across = [(0, 1), (1, 0)]
    movie = lax.ppermute(outgoing, "tm", across)
    far = swapped(far, 1)
    near = swapped(near, 0)
    other = lax.ppermute(rounded, "tm", across)
    total, quad, rim_part = call(
        functools.partial(own_kernel, voxels),
        [
            shape((width, neurons), F32),
            shape((neurons, neurons), F32),
            shape((2 * rim, neurons), F32),
        ],
        [WHOLE] * 4,
        [WHOLE] * 3,
        0.6,
    )(recording, foot, rounded, flat)
    lead, sent = call(
        both_kernel,
        [shape((rim, neurons), F32), pltpu.VMEM((rim, neurons), BF)],
        [WHOLE] * 4,
        [WHOLE] * 2,
        0.3,
    )(rim_part, rounded, far, near)
    came = lax.ppermute(sent, "tm", across)
    sofar, new_tr, scale = call(
        functools.partial(main_kernel, voxels, rim),
        [pltpu.HBM((share, neurons), BF), pltpu.HBM((frames, neurons), F32), shape((8, neurons), F32)],
        [WHOLE] * 6,
        [LEFT_THERE] * 2 + [WHOLE],
        2.0,
        scratch_shapes=[pltpu.VMEM((width, neurons), BF), COPIES((4,))],
    )(foot, total, quad, movie, other, new_tr)
    new_foot = call(
        functools.partial(edge_kernel, voxels),
        pltpu.HBM((share, neurons), BF),
        [LEFT_THERE] + [WHOLE] * 4,
        LEFT_THERE,
        0.8,
        input_output_aliases={0: 0},
        scratch_shapes=[pltpu.VMEM((rim, neurons), BF), COPIES],
    )(sofar, foot, lead, came, scale)
    return new_tr, new_foot


def spread(voxels, rim, foot, recording, rounded):
    slabs, parts = lax.axis_size("slab"), lax.axis_size("tm")
    extended, neurons = foot.shape
    share = extended // parts
    here = lax.axis_index("tm")
    closing = here == parts - 1
    exact = lax.Precision.HIGHEST
    cut = voxels - (share - rim)
    columns = jnp.concatenate([recording[:, :cut], recording[:, :rim], recording[:, cut:]], 1)
    movie = lax.all_to_all(columns, "tm", split_axis=1, concat_axis=0, tiled=True)
    fit = lax.all_gather(rounded, "tm", axis=0, tiled=True)
    edge = jnp.where(here == 0, foot[voxels:], foot[:rim])
    seen = movie[:, :rim].astype(F32)
    sent = jnp.where(here == 0, 0.0, seen) - mm_t(fit, edge)
    ahead = [(i * parts, (i + 1) * parts) for i in range(slabs - 1)]
    behind = [((i + 2) * parts - 1, (i + 1) * parts - 1) for i in range(slabs - 1)]
    lead = jnp.where(closing, 0.0, seen) + lax.ppermute(sent, ("slab", "tm"), ahead + behind)
    lead = lax.dot_general(lead, fit.astype(F32), (((0,), (0,)), ((), ())), precision=exact)
    inner = t_mm(movie[:, rim:], fit)
    total = jnp.where(
        closing, jnp.concatenate([inner, lead], 0), jnp.concatenate([lead, inner], 0)
    )
    square = t_mm(fit, fit)
    own = lax.dynamic_slice_in_dim(foot, here * share, share, 0).astype(F32)
    total = total - jnp.dot(own, square, precision=exact)
    return jnp.maximum(own + total / jnp.maximum(jnp.diagonal(square), 1.0), 0.0).astype(BF)


def on_device(recording, footprints, traces, live_count):
    frames, voxels = recording.shape
    extended, neurons = footprints.shape
    rim = extended - voxels
    main = voxels // 2 // rim - 1
    split = lax.axis_size("tm") == 2
    share_shape = [pltpu.VMEM((main * frames + frames // 2, rim), BF)] if split else []
    pinned = [
        pltpu.with_memory_space_constraint(x, pltpu.HBM)
        for x in (live_count, recording, footprints, traces)
    ]
    far, near, count, begun, *outgoing = call(
        functools.partial(rim_kernel, voxels),
        [
            pltpu.VMEM((frames, rim), BF),
            pltpu.VMEM((frames, rim), BF),
            pltpu.VMEM((8, neurons), jnp.int32),
            pltpu.VMEM((frames, neurons), F32),
        ]
        + share_shape,
        [LEFT_THERE] * 4,
        [WHOLE] * (4 + len(share_shape)),
        1.5,
        scratch_shapes=[
            pltpu.SMEM(live_count.shape, jnp.int32),
            pltpu.VMEM((2 * rim, neurons), BF),
            pltpu.VMEM((frames, rim), BF),
            pltpu.VMEM((frames, rim), BF),
            COPIES((6 + main,)),
        ],
    )(*pinned)
    far = swapped(far, 1)
    near = swapped(near, 0)
    plan, scale, cross_high, cross_low, rims, flat, masked, shown = call(
        functools.partial(drive_kernel, voxels),
        [
            shape((frames, neurons), F32),
            shape((8, neurons), F32),
            shape((GROUP, GROUP), BF),
            shape((GROUP, GROUP), BF),
            shape((2 * rim, neurons), BF),
            shape((rim, frames), BF),
            pltpu.VMEM((extended, neurons), BF),
            pltpu.VMEM((frames, voxels), BF),
        ],
        [WHOLE, LEFT_THERE, WHOLE, WHOLE],
        [WHOLE] * 8,
        1.6,
        scratch_shapes=[COPIES((2,))],
    )(count, pinned[1], footprints, begun)
    new_tr, rounded, far, near = call(
        sweep_kernel,
        [
            pltpu.VMEM((frames, neurons), F32),
            pltpu.VMEM((frames, neurons), BF),
            pltpu.VMEM((rim, frames), BF),
            pltpu.VMEM((rim, frames), BF),
        ],
        [WHOLE] * 8,
        [WHOLE] * 4,
        0.5,
    )(plan, scale, cross_high, cross_low, rims, flat, far, near)
    if split:
        return halved(voxels, rim, masked, shown, flat, outgoing[0], new_tr, rounded, far, near)
    return new_tr, spread(voxels, rim, masked, recording, rounded)


def solution(mesh):
    placed = (P("tm", "slab"), P(None, "slab"), P("tm", "slab"), P())
    return jax.shard_map(
        on_device,
        mesh=mesh,
        in_specs=placed,
        out_specs=(P("tm", "slab"), P("tm", "slab")),
        check_vma=False,
    )
```

```python
import functools

import jax
import jax.numpy as jnp
from jax import lax
from jax.experimental import pallas as pl
from jax.experimental.pallas import tpu as pltpu
from jax.sharding import PartitionSpec as P

GROUP = 128
BF = jnp.bfloat16
F32 = jnp.float32
WHOLE = pl.BlockSpec(memory_space=pltpu.VMEM)
LEFT_THERE = pl.BlockSpec(memory_space=pl.ANY)
COPIES = pltpu.SemaphoreType.DMA
shape = jax.ShapeDtypeStruct


def mm(left, right):
    return jnp.dot(left, right, preferred_element_type=F32)


def mm_t(left, right):
    return lax.dot_general(left, right, (((1,), (1,)), ((), ())), preferred_element_type=F32)


def t_mm(left, right):
    return lax.dot_general(left, right, (((0,), (0,)), ((), ())), preferred_element_type=F32)


def halves(wide):
    high = wide.astype(BF)
    return high, (wide - high.astype(F32)).astype(BF)


def living(count, block):
    slots = lax.broadcasted_iota(jnp.int32, block.shape, 1)
    return jnp.where(slots < count, block, jnp.zeros_like(block))


def diagonal(square):
    rows = lax.broadcasted_iota(jnp.int32, square.shape, 0)
    columns = lax.broadcasted_iota(jnp.int32, square.shape, 1)
    return jnp.sum(jnp.where(rows == columns, square, 0.0), axis=0, keepdims=True)


def at_end(axis):
    return lax.axis_index(axis) == lax.axis_size(axis) - 1


def odd_slab():
    return lax.axis_index("slab") % 2 == 1


def call(body, outs, in_specs, out_specs, expected, **more):
    return pl.pallas_call(
        body,
        out_shape=outs,
        in_specs=in_specs,
        out_specs=out_specs,
        compiler_params=pltpu.CompilerParams(vmem_limit_bytes=32 * 1024 * 1024),
        cost_estimate=pl.CostEstimate(
            flops=0, bytes_accessed=int(expected * 3_690_000), transcendentals=0
        ),
        **more,
    )


def copied(source, target, sem):
    copy = pltpu.make_async_copy(source, target, sem)
    copy.start()
    return copy


def first_column(which, voxels, rim):
    return pl.multiple_of(rim + which * (voxels // 2), 128)


def rolled(block):
    half = block.shape[1] // 2
    return jnp.concatenate([block[:, half:], block[:, :half]], axis=1)


def packed(which, middle):
    frames = middle.shape[0] // 2
    top, bottom = middle[:frames], middle[frames:]
    low = jnp.where(which == 0, top, rolled(top))
    high = jnp.where(which == 0, rolled(bottom), bottom)
    slots = lax.broadcasted_iota(jnp.int32, low.shape, 1)
    return jnp.where(slots < low.shape[1] // 2, low, high)


def unpacked(which, block):
    turned = rolled(block)
    top = jnp.where(which == 0, block, turned)
    bottom = jnp.where(which == 0, turned, block)
    return jnp.concatenate([top, bottom], axis=0)


def for_near_and_far(forward, backward):
    odd = odd_slab()
    return jnp.where(odd, backward, forward), jnp.where(odd, forward, backward)


def from_prev_and_next(near, far):
    odd = odd_slab()
    return jnp.where(odd, near, far), jnp.where(odd, far, near)


def rim_kernel(voxels, live, movie, foot, start, far, near, count, traces, *rest):
    numbers, rims, edge, middle, sems = rest[-5:]
    rim = edge.shape[1]
    frames = edge.shape[0]
    there = 1 - lax.axis_index("tm")
    small = [
        copied(live, numbers, sems.at[0]),
        copied(start, traces, sems.at[1]),
        copied(foot.at[pl.ds(0, rim)], rims.at[pl.ds(0, rim)], sems.at[2]),
        copied(foot.at[pl.ds(voxels, rim)], rims.at[pl.ds(rim, rim)], sems.at[3]),
        copied(movie.at[:, pl.ds(0, rim)], edge, sems.at[4]),
        copied(movie.at[:, pl.ds(voxels // 2, rim)], middle, sems.at[5]),
    ]
    large = []
    if len(rest) > 5:
        first = first_column(there, voxels, rim)
        for i in range(voxels // 2 // rim - 1):
            column = movie.at[:, pl.ds(pl.multiple_of(first + i * rim, 128), rim)]
            large.append(copied(column, rest[0].at[pl.ds(i * frames, frames)], sems.at[6 + i]))
    for copy in small:
        copy.wait()
    alive = numbers[lax.axis_index("slab")]
    count[...] = jnp.full(count.shape, alive, jnp.int32)
    high, low = halves(living(alive, traces[...]))
    seen = mm_t(high, rims[...]) + mm_t(low, rims[...])
    backward = edge[...].astype(F32) - seen[:, :rim]
    one, two = for_near_and_far(seen[:, rim:], backward)
    near[...] = one
    far[...] = two
    if large:
        rest[0][(voxels // 2 // rim - 1) * frames:] = packed(there, middle[...])
    for copy in large:
        copy.wait()


def drive_kernel(
    voxels, count, movie, foot, start, plan, scale, cross_high, cross_low, rims, flat, masked, shown, sems
):
    rim = foot.shape[0] - voxels
    step = voxels // 2
    loads = []
    for i in range(2):
        columns = pl.ds(i * step, step)
        loads.append(copied(movie.at[:, columns], shown.at[:, columns], sems.at[i]))
    alive = count[0:1]
    masked[:voxels] = living(alive, foot[:voxels])
    ends = living(alive, foot[voxels:])
    masked[voxels:] = jnp.where(at_end("slab"), jnp.zeros_like(ends), ends)
    rims[:rim] = -masked[:rim]
    rims[rim:] = masked[voxels:]
    gram = t_mm(masked[...], masked[...])
    loads[0].wait()
    flat[...] = shown[:, :rim].T
    drive = mm(shown[:, :step], masked[:step])
    loads[1].wait()
    drive = drive + mm(shown[:, step:], masked[step:voxels])
    inverse = 1.0 / (diagonal(gram) + 1e-06)
    scale[...] = jnp.broadcast_to(inverse, scale.shape)
    gram_high, gram_low = halves(gram)
    cross_high[...] = gram_high[:GROUP, GROUP:]
    cross_low[...] = gram_low[:GROUP, GROUP:]
    current = living(alive, start[...])
    high, low = halves(current)
    for at in range(0, current.shape[1], GROUP):
        columns = slice(at, at + GROUP)
        coupled = mm(high[:, at:], gram_high[at:, columns]) + mm(high[:, at:], gram_low[at:, columns])
        coupled = coupled + mm(low[:, at:], gram_high[at:, columns])
        plan[:, columns] = current[:, columns] + (drive[:, columns] - coupled) * inverse[:, columns]


def sweep_kernel(
    plan, scale, cross_high, cross_low, rims, flat, far, near, traces, rounded, far_next, near_next
):
    rim = flat.shape[0]
    edges = rims[...]
    beside = jnp.concatenate(from_prev_and_next(near[...], far[...]), axis=1)
    high, low = halves(beside)
    stepped = plan[...] + (mm(high, edges) + mm(low, edges)) * scale[0:1]
    first = jnp.maximum(stepped[:, :GROUP], 0.0)
    high, low = halves(first)
    cross = cross_high[...]
    coupled = mm(
        jnp.concatenate([high, low, high], axis=1), jnp.concatenate([cross, cross, cross_low[...]], axis=0)
    )
    second = jnp.maximum(stepped[:, GROUP:] - coupled * scale[0:1, GROUP:], 0.0)
    whole = jnp.concatenate([high, second.astype(BF)], axis=1)
    rounded[...] = whole
    seen = mm_t(edges, whole)
    one, two = for_near_and_far(seen[rim:], flat[...].astype(F32) + seen[:rim])
    near_next[...] = one.astype(BF)
    far_next[...] = two.astype(BF)
    traces[:, :GROUP] = first
    traces[:, GROUP:] = second


def own_kernel(voxels, movie, foot, fit, flat, total, quad, rim_part):
    rim = flat.shape[0]
    main = voxels // 2 - rim
    traces = fit[...]
    square = t_mm(traces, traces)
    quad[...] = square
    high, low = halves(square)
    begins, ends = foot[:rim], foot[voxels:]
    rim_part[:rim] = mm(flat[...], traces) - (mm(begins, high) + mm(begins, low))
    rim_part[rim:] = -(mm(ends, high) + mm(ends, low))
    first = first_column(lax.axis_index("tm"), voxels, rim)
    total[:main] = t_mm(movie[:, pl.ds(first, main)], traces)
    total[main:] = t_mm(movie[:, voxels // 2:voxels // 2 + rim], traces)


def both_kernel(rim_part, fit, far, near, lead, sent):
    rim = lead.shape[0]
    first = lax.axis_index("tm") == 0
    before, after = from_prev_and_next(near[...], far[...])
    traces = fit[...]
    begins = rim_part[:rim] - mm(before, traces)
    ends = rim_part[rim:] + mm(after, traces)
    lead[...] = jnp.where(first, begins, ends)
    sent[...] = jnp.where(first, ends, begins).astype(BF)


def main_kernel(voxels, rim, foot, total, quad, movie, fit, traces, out, new_tr, scale, moved, sems):
    here = lax.axis_index("tm")
    frames = fit.shape[0]
    width = voxels // 2
    main = width - rim
    written = [copied(traces, new_tr, sems.at[0])]
    fitted = fit[...]
    square = quad[...] + t_mm(fitted, fitted)
    inverse = 1.0 / jnp.maximum(diagonal(square), 1.0)
    scale[...] = jnp.broadcast_to(inverse, scale.shape)
    high, low = halves(square)
    first = first_column(here, voxels, rim)
    row = pl.multiple_of(rim - here * (rim // 2), 64)
    for begin, end in ((0, width // 2), (width // 2, main), (main, width)):
        if begin < main:
            own = foot[pl.ds(pl.multiple_of(first + begin, 128), end - begin)]
            columns = range(begin // rim, end // rim)
            shown = jnp.concatenate([movie[i * frames:(i + 1) * frames] for i in columns], axis=1)
        else:
            own = foot[width:width + rim]
            shown = unpacked(here, movie[main // rim * frames:])
        part = total[begin:end] + t_mm(shown, fitted) - (mm(own, high) + mm(own, low))
        moved[begin:end] = jnp.maximum(own.astype(F32) + part * inverse, 0.0).astype(BF)
        if begin < main:
            target = out.at[pl.ds(row + begin, end - begin)]
            written.append(copied(moved.at[pl.ds(begin, end - begin)], target, sems.at[len(written)]))
        else:
            half = rim // 2
            source = moved.at[pl.ds(pl.multiple_of(main + here * half, 64), half)]
            target = out.at[pl.ds(pl.multiple_of((1 - here) * (out.shape[0] - half), 64), half)]
            written.append(copied(source, target, sems.at[len(written)]))
    for copy in written:
        copy.wait()


def edge_kernel(voxels, sofar, foot, lead, came, scale, out, moved, sem):
    rim = lead.shape[0]
    here = lax.axis_index("tm")
    own = foot[pl.ds(pl.multiple_of(here * voxels, 128), rim)].astype(F32)
    moved[...] = jnp.maximum(own + (lead[...] + came[...].astype(F32)) * scale[0:1], 0.0).astype(BF)
    row = pl.multiple_of(here * (out.shape[0] - rim), 64)
    copied(moved, out.at[pl.ds(row, rim)], sem).wait()


def swapped(block, first):
    route = [(i, i + 1) for i in range(first, lax.axis_size("slab") - 1, 2)]
    return lax.ppermute(block, "slab", [(j, i) for i, j in route] + route)


def halved(voxels, rim, foot, recording, flat, outgoing, new_tr, rounded, far, near):
    frames = recording.shape[0]
    extended, neurons = foot.shape
    width, share = voxels // 2, extended // 2
    across = [(0, 1), (1, 0)]
    movie = lax.ppermute(outgoing, "tm", across)
    far = swapped(far, 1)
    near = swapped(near, 0)
    other = lax.ppermute(rounded, "tm", across)
    total, quad, rim_part = call(
        functools.partial(own_kernel, voxels),
        [
            shape((width, neurons), F32),
            shape((neurons, neurons), F32),
            shape((2 * rim, neurons), F32),
        ],
        [WHOLE] * 4,
        [WHOLE] * 3,
        0.6,
    )(recording, foot, rounded, flat)
    lead, sent = call(
        both_kernel,
        [shape((rim, neurons), F32), pltpu.VMEM((rim, neurons), BF)],
        [WHOLE] * 4,
        [WHOLE] * 2,
        0.3,
    )(rim_part, rounded, far, near)
    came = lax.ppermute(sent, "tm", across)
    sofar, new_tr, scale = call(
        functools.partial(main_kernel, voxels, rim),
        [pltpu.HBM((share, neurons), BF), pltpu.HBM((frames, neurons), F32), shape((8, neurons), F32)],
        [WHOLE] * 6,
        [LEFT_THERE] * 2 + [WHOLE],
        2.0,
        scratch_shapes=[pltpu.VMEM((width, neurons), BF), COPIES((4,))],
    )(foot, total, quad, movie, other, new_tr)
    new_foot = call(
        functools.partial(edge_kernel, voxels),
        pltpu.HBM((share, neurons), BF),
        [LEFT_THERE] + [WHOLE] * 4,
        LEFT_THERE,
        0.8,
        input_output_aliases={0: 0},
        scratch_shapes=[pltpu.VMEM((rim, neurons), BF), COPIES],
    )(sofar, foot, lead, came, scale)
    return new_tr, new_foot


def spread(voxels, rim, foot, recording, rounded):
    slabs, parts = lax.axis_size("slab"), lax.axis_size("tm")
    extended, neurons = foot.shape
    share = extended // parts
    here = lax.axis_index("tm")
    closing = here == parts - 1
    exact = lax.Precision.HIGHEST
    cut = voxels - (share - rim)
    columns = jnp.concatenate([recording[:, :cut], recording[:, :rim], recording[:, cut:]], 1)
    movie = lax.all_to_all(columns, "tm", split_axis=1, concat_axis=0, tiled=True)
    fit = lax.all_gather(rounded, "tm", axis=0, tiled=True)
    edge = jnp.where(here == 0, foot[voxels:], foot[:rim])
    seen = movie[:, :rim].astype(F32)
    sent = jnp.where(here == 0, 0.0, seen) - mm_t(fit, edge)
    ahead = [(i * parts, (i + 1) * parts) for i in range(slabs - 1)]
    behind = [((i + 2) * parts - 1, (i + 1) * parts - 1) for i in range(slabs - 1)]
    lead = jnp.where(closing, 0.0, seen) + lax.ppermute(sent, ("slab", "tm"), ahead + behind)
    lead = lax.dot_general(lead, fit.astype(F32), (((0,), (0,)), ((), ())), precision=exact)
    inner = t_mm(movie[:, rim:], fit)
    total = jnp.where(
        closing, jnp.concatenate([inner, lead], 0), jnp.concatenate([lead, inner], 0)
    )
    square = t_mm(fit, fit)
    own = lax.dynamic_slice_in_dim(foot, here * share, share, 0).astype(F32)
    total = total - jnp.dot(own, square, precision=exact)
    return jnp.maximum(own + total / jnp.maximum(jnp.diagonal(square), 1.0), 0.0).astype(BF)


def on_device(recording, footprints, traces, live_count):
    frames, voxels = recording.shape
    extended, neurons = footprints.shape
    rim = extended - voxels
    main = voxels // 2 // rim - 1
    split = lax.axis_size("tm") == 2
    share_shape = [pltpu.VMEM((main * frames + frames // 2, rim), BF)] if split else []
    pinned = [
        pltpu.with_memory_space_constraint(x, pltpu.HBM)
        for x in (live_count, recording, footprints, traces)
    ]
    far, near, count, begun, *outgoing = call(
        functools.partial(rim_kernel, voxels),
        [
            pltpu.VMEM((frames, rim), F32),
            pltpu.VMEM((frames, rim), F32),
            pltpu.VMEM((8, neurons), jnp.int32),
            pltpu.VMEM((frames, neurons), F32),
        ]
        + share_shape,
        [LEFT_THERE] * 4,
        [WHOLE] * (4 + len(share_shape)),
        1.5,
        scratch_shapes=[
            pltpu.SMEM(live_count.shape, jnp.int32),
            pltpu.VMEM((2 * rim, neurons), BF),
            pltpu.VMEM((frames, rim), BF),
            pltpu.VMEM((frames, rim), BF),
            COPIES((6 + main,)),
        ],
    )(*pinned)
    far = swapped(far, 1)
    near = swapped(near, 0)
    plan, scale, cross_high, cross_low, rims, flat, masked, shown = call(
        functools.partial(drive_kernel, voxels),
        [
            shape((frames, neurons), F32),
            shape((8, neurons), F32),
            shape((GROUP, GROUP), BF),
            shape((GROUP, GROUP), BF),
            shape((2 * rim, neurons), BF),
            shape((rim, frames), BF),
            pltpu.VMEM((extended, neurons), BF),
            pltpu.VMEM((frames, voxels), BF),
        ],
        [WHOLE, LEFT_THERE, WHOLE, WHOLE],
        [WHOLE] * 8,
        1.6,
        scratch_shapes=[COPIES((2,))],
    )(count, pinned[1], footprints, begun)
    new_tr, rounded, far, near = call(
        sweep_kernel,
        [
            pltpu.VMEM((frames, neurons), F32),
            pltpu.VMEM((frames, neurons), BF),
            pltpu.VMEM((rim, frames), BF),
            pltpu.VMEM((rim, frames), BF),
        ],
        [WHOLE] * 8,
        [WHOLE] * 4,
        0.5,
    )(plan, scale, cross_high, cross_low, rims, flat, far, near)
    if split:
        return halved(voxels, rim, masked, shown, flat, outgoing[0], new_tr, rounded, far, near)
    return new_tr, spread(voxels, rim, masked, recording, rounded)


def solution(mesh):
    placed = (P("tm", "slab"), P(None, "slab"), P("tm", "slab"), P())
    return jax.shard_map(
        on_device,
        mesh=mesh,
        in_specs=placed,
        out_specs=(P("tm", "slab"), P("tm", "slab")),
        check_vma=False,
    )
```

```python
import functools

import jax
import jax.numpy as jnp
from jax import lax
from jax.experimental import pallas as pl
from jax.experimental.pallas import tpu as pltpu
from jax.sharding import PartitionSpec as P

GROUP = 128
BF = jnp.bfloat16
F32 = jnp.float32
WHOLE = pl.BlockSpec(memory_space=pltpu.VMEM)
LEFT_THERE = pl.BlockSpec(memory_space=pl.ANY)
COPIES = pltpu.SemaphoreType.DMA
shape = jax.ShapeDtypeStruct


def mm(left, right):
    return jnp.dot(left, right, preferred_element_type=F32)


def mm_t(left, right):
    return lax.dot_general(left, right, (((1,), (1,)), ((), ())), preferred_element_type=F32)


def t_mm(left, right):
    return lax.dot_general(left, right, (((0,), (0,)), ((), ())), preferred_element_type=F32)


def halves(wide):
    high = wide.astype(BF)
    return high, (wide - high.astype(F32)).astype(BF)


def coded(block):
    square = block * block
    fourth = square * square
    eighth = fourth * fourth
    return jnp.where(block < 0, -eighth, eighth).astype(BF)


def decoded(block):
    wide = block.astype(F32)
    size = jnp.abs(wide)
    root = jnp.where(size > 0, jnp.exp2(jnp.log2(size) * 0.125), 0.0)
    return jnp.where(wide < 0, -root, root)


def living(count, block):
    slots = lax.broadcasted_iota(jnp.int32, block.shape, 1)
    return jnp.where(slots < count, block, jnp.zeros_like(block))


def diagonal(square):
    rows = lax.broadcasted_iota(jnp.int32, square.shape, 0)
    columns = lax.broadcasted_iota(jnp.int32, square.shape, 1)
    return jnp.sum(jnp.where(rows == columns, square, 0.0), axis=0, keepdims=True)


def at_end(axis):
    return lax.axis_index(axis) == lax.axis_size(axis) - 1


def odd_slab():
    return lax.axis_index("slab") % 2 == 1


def call(body, outs, in_specs, out_specs, expected, **more):
    return pl.pallas_call(
        body,
        out_shape=outs,
        in_specs=in_specs,
        out_specs=out_specs,
        compiler_params=pltpu.CompilerParams(vmem_limit_bytes=32 * 1024 * 1024),
        cost_estimate=pl.CostEstimate(
            flops=0, bytes_accessed=int(expected * 3_690_000), transcendentals=0
        ),
        **more,
    )


def copied(source, target, sem):
    copy = pltpu.make_async_copy(source, target, sem)
    copy.start()
    return copy


def first_column(which, voxels, rim):
    return pl.multiple_of(rim + which * (voxels // 2), 128)


def rolled(block):
    half = block.shape[1] // 2
    return jnp.concatenate([block[:, half:], block[:, :half]], axis=1)


def packed(which, middle):
    frames = middle.shape[0] // 2
    top, bottom = middle[:frames], middle[frames:]
    low = jnp.where(which == 0, top, rolled(top))
    high = jnp.where(which == 0, rolled(bottom), bottom)
    slots = lax.broadcasted_iota(jnp.int32, low.shape, 1)
    return jnp.where(slots < low.shape[1] // 2, low, high)


def unpacked(which, block):
    turned = rolled(block)
    top = jnp.where(which == 0, block, turned)
    bottom = jnp.where(which == 0, turned, block)
    return jnp.concatenate([top, bottom], axis=0)


def for_near_and_far(forward, backward):
    odd = odd_slab()
    return jnp.where(odd, backward, forward), jnp.where(odd, forward, backward)


def from_prev_and_next(near, far):
    odd = odd_slab()
    return jnp.where(odd, near, far), jnp.where(odd, far, near)


def rim_kernel(voxels, live, movie, foot, start, far, near, count, traces, *rest):
    numbers, rims, edge, middle, sems = rest[-5:]
    rim = edge.shape[1]
    frames = edge.shape[0]
    there = 1 - lax.axis_index("tm")
    small = [
        copied(live, numbers, sems.at[0]),
        copied(start, traces, sems.at[1]),
        copied(foot.at[pl.ds(0, rim)], rims.at[pl.ds(0, rim)], sems.at[2]),
        copied(foot.at[pl.ds(voxels, rim)], rims.at[pl.ds(rim, rim)], sems.at[3]),
        copied(movie.at[:, pl.ds(0, rim)], edge, sems.at[4]),
        copied(movie.at[:, pl.ds(voxels // 2, rim)], middle, sems.at[5]),
    ]
    large = []
    if len(rest) > 5:
        first = first_column(there, voxels, rim)
        for i in range(voxels // 2 // rim - 1):
            column = movie.at[:, pl.ds(pl.multiple_of(first + i * rim, 128), rim)]
            large.append(copied(column, rest[0].at[pl.ds(i * frames, frames)], sems.at[6 + i]))
    for copy in small:
        copy.wait()
    alive = numbers[lax.axis_index("slab")]
    count[...] = jnp.full(count.shape, alive, jnp.int32)
    high, low = halves(living(alive, traces[...]))
    seen = mm_t(high, rims[...]) + mm_t(low, rims[...])
    backward = edge[...].astype(F32) - seen[:, :rim]
    one, two = for_near_and_far(seen[:, rim:], backward)
    near[...] = coded(one)
    far[...] = coded(two)
    if large:
        rest[0][(voxels // 2 // rim - 1) * frames:] = packed(there, middle[...])
    for copy in large:
        copy.wait()


def drive_kernel(
    voxels, count, movie, foot, start, plan, scale, cross_high, cross_low, rims, flat, masked, shown, sems
):
    rim = foot.shape[0] - voxels
    step = voxels // 2
    loads = []
    for i in range(2):
        columns = pl.ds(i * step, step)
        loads.append(copied(movie.at[:, columns], shown.at[:, columns], sems.at[i]))
    alive = count[0:1]
    masked[:voxels] = living(alive, foot[:voxels])
    ends = living(alive, foot[voxels:])
    masked[voxels:] = jnp.where(at_end("slab"), jnp.zeros_like(ends), ends)
    rims[:rim] = -masked[:rim]
    rims[rim:] = masked[voxels:]
    gram = t_mm(masked[...], masked[...])
    loads[0].wait()
    flat[...] = shown[:, :rim].T
    drive = mm(shown[:, :step], masked[:step])
    loads[1].wait()
    drive = drive + mm(shown[:, step:], masked[step:voxels])
    inverse = 1.0 / (diagonal(gram) + 1e-06)
    scale[...] = jnp.broadcast_to(inverse, scale.shape)
    gram_high, gram_low = halves(gram)
    cross_high[...] = gram_high[:GROUP, GROUP:]
    cross_low[...] = gram_low[:GROUP, GROUP:]
    current = living(alive, start[...])
    high, low = halves(current)
    for at in range(0, current.shape[1], GROUP):
        columns = slice(at, at + GROUP)
        coupled = mm(high[:, at:], gram_high[at:, columns]) + mm(high[:, at:], gram_low[at:, columns])
        coupled = coupled + mm(low[:, at:], gram_high[at:, columns])
        plan[:, columns] = current[:, columns] + (drive[:, columns] - coupled) * inverse[:, columns]


def sweep_kernel(
    plan, scale, cross_high, cross_low, rims, flat, far, near, traces, rounded, far_next, near_next
):
    rim = flat.shape[0]
    edges = rims[...]
    high, low = halves(decoded(jnp.concatenate(from_prev_and_next(near[...], far[...]), axis=1)))
    stepped = plan[...] + (mm(high, edges) + mm(low, edges)) * scale[0:1]
    first = jnp.maximum(stepped[:, :GROUP], 0.0)
    high, low = halves(first)
    cross = cross_high[...]
    coupled = mm(
        jnp.concatenate([high, low, high], axis=1), jnp.concatenate([cross, cross, cross_low[...]], axis=0)
    )
    second = jnp.maximum(stepped[:, GROUP:] - coupled * scale[0:1, GROUP:], 0.0)
    whole = jnp.concatenate([high, second.astype(BF)], axis=1)
    rounded[...] = whole
    seen = mm_t(edges, whole)
    one, two = for_near_and_far(seen[rim:], flat[...].astype(F32) + seen[:rim])
    near_next[...] = one.astype(BF)
    far_next[...] = two.astype(BF)
    traces[:, :GROUP] = first
    traces[:, GROUP:] = second


def own_kernel(voxels, movie, foot, fit, flat, total, quad, rim_part):
    rim = flat.shape[0]
    main = voxels // 2 - rim
    traces = fit[...]
    square = t_mm(traces, traces)
    quad[...] = square
    high, low = halves(square)
    begins, ends = foot[:rim], foot[voxels:]
    rim_part[:rim] = mm(flat[...], traces) - (mm(begins, high) + mm(begins, low))
    rim_part[rim:] = -(mm(ends, high) + mm(ends, low))
    first = first_column(lax.axis_index("tm"), voxels, rim)
    total[:main] = t_mm(movie[:, pl.ds(first, main)], traces)
    total[main:] = t_mm(movie[:, voxels // 2:voxels // 2 + rim], traces)


def both_kernel(rim_part, fit, far, near, lead, sent):
    rim = lead.shape[0]
    first = lax.axis_index("tm") == 0
    before, after = from_prev_and_next(near[...], far[...])
    traces = fit[...]
    begins = rim_part[:rim] - mm(before, traces)
    ends = rim_part[rim:] + mm(after, traces)
    lead[...] = jnp.where(first, begins, ends)
    sent[...] = jnp.where(first, ends, begins).astype(BF)


def main_kernel(voxels, rim, foot, total, quad, movie, fit, traces, out, new_tr, scale, moved, sems):
    here = lax.axis_index("tm")
    frames = fit.shape[0]
    width = voxels // 2
    main = width - rim
    written = [copied(traces, new_tr, sems.at[0])]
    fitted = fit[...]
    square = quad[...] + t_mm(fitted, fitted)
    inverse = 1.0 / jnp.maximum(diagonal(square), 1.0)
    scale[...] = jnp.broadcast_to(inverse, scale.shape)
    high, low = halves(square)
    first = first_column(here, voxels, rim)
    row = pl.multiple_of(rim - here * (rim // 2), 64)
    for begin, end in ((0, width // 2), (width // 2, main), (main, width)):
        if begin < main:
            own = foot[pl.ds(pl.multiple_of(first + begin, 128), end - begin)]
            columns = range(begin // rim, end // rim)
            shown = jnp.concatenate([movie[i * frames:(i + 1) * frames] for i in columns], axis=1)
        else:
            own = foot[width:width + rim]
            shown = unpacked(here, movie[main // rim * frames:])
        part = total[begin:end] + t_mm(shown, fitted) - (mm(own, high) + mm(own, low))
        moved[begin:end] = jnp.maximum(own.astype(F32) + part * inverse, 0.0).astype(BF)
        if begin < main:
            target = out.at[pl.ds(row + begin, end - begin)]
            written.append(copied(moved.at[pl.ds(begin, end - begin)], target, sems.at[len(written)]))
        else:
            half = rim // 2
            source = moved.at[pl.ds(pl.multiple_of(main + here * half, 64), half)]
            target = out.at[pl.ds(pl.multiple_of((1 - here) * (out.shape[0] - half), 64), half)]
            written.append(copied(source, target, sems.at[len(written)]))
    for copy in written:
        copy.wait()


def edge_kernel(voxels, sofar, foot, lead, came, scale, out, moved, sem):
    rim = lead.shape[0]
    here = lax.axis_index("tm")
    own = foot[pl.ds(pl.multiple_of(here * voxels, 128), rim)].astype(F32)
    moved[...] = jnp.maximum(own + (lead[...] + came[...].astype(F32)) * scale[0:1], 0.0).astype(BF)
    row = pl.multiple_of(here * (out.shape[0] - rim), 64)
    copied(moved, out.at[pl.ds(row, rim)], sem).wait()


def swapped(block, first):
    route = [(i, i + 1) for i in range(first, lax.axis_size("slab") - 1, 2)]
    return lax.ppermute(block, "slab", [(j, i) for i, j in route] + route)


def halved(voxels, rim, foot, recording, flat, outgoing, new_tr, rounded, far, near):
    frames = recording.shape[0]
    extended, neurons = foot.shape
    width, share = voxels // 2, extended // 2
    across = [(0, 1), (1, 0)]
    movie = lax.ppermute(outgoing, "tm", across)
    far = swapped(far, 1)
    near = swapped(near, 0)
    other = lax.ppermute(rounded, "tm", across)
    total, quad, rim_part = call(
        functools.partial(own_kernel, voxels),
        [
            shape((width, neurons), F32),
            shape((neurons, neurons), F32),
            shape((2 * rim, neurons), F32),
        ],
        [WHOLE] * 4,
        [WHOLE] * 3,
        0.6,
    )(recording, foot, rounded, flat)
    lead, sent = call(
        both_kernel,
        [shape((rim, neurons), F32), pltpu.VMEM((rim, neurons), BF)],
        [WHOLE] * 4,
        [WHOLE] * 2,
        0.3,
    )(rim_part, rounded, far, near)
    came = lax.ppermute(sent, "tm", across)
    sofar, new_tr, scale = call(
        functools.partial(main_kernel, voxels, rim),
        [pltpu.HBM((share, neurons), BF), pltpu.HBM((frames, neurons), F32), shape((8, neurons), F32)],
        [WHOLE] * 6,
        [LEFT_THERE] * 2 + [WHOLE],
        2.0,
        scratch_shapes=[pltpu.VMEM((width, neurons), BF), COPIES((4,))],
    )(foot, total, quad, movie, other, new_tr)
    new_foot = call(
        functools.partial(edge_kernel, voxels),
        pltpu.HBM((share, neurons), BF),
        [LEFT_THERE] + [WHOLE] * 4,
        LEFT_THERE,
        0.8,
        input_output_aliases={0: 0},
        scratch_shapes=[pltpu.VMEM((rim, neurons), BF), COPIES],
    )(sofar, foot, lead, came, scale)
    return new_tr, new_foot


def spread(voxels, rim, foot, recording, rounded):
    slabs, parts = lax.axis_size("slab"), lax.axis_size("tm")
    extended, neurons = foot.shape
    share = extended // parts
    here = lax.axis_index("tm")
    closing = here == parts - 1
    exact = lax.Precision.HIGHEST
    cut = voxels - (share - rim)
    columns = jnp.concatenate([recording[:, :cut], recording[:, :rim], recording[:, cut:]], 1)
    movie = lax.all_to_all(columns, "tm", split_axis=1, concat_axis=0, tiled=True)
    fit = lax.all_gather(rounded, "tm", axis=0, tiled=True)
    edge = jnp.where(here == 0, foot[voxels:], foot[:rim])
    seen = movie[:, :rim].astype(F32)
    sent = jnp.where(here == 0, 0.0, seen) - mm_t(fit, edge)
    ahead = [(i * parts, (i + 1) * parts) for i in range(slabs - 1)]
    behind = [((i + 2) * parts - 1, (i + 1) * parts - 1) for i in range(slabs - 1)]
    lead = jnp.where(closing, 0.0, seen) + lax.ppermute(sent, ("slab", "tm"), ahead + behind)
    lead = lax.dot_general(lead, fit.astype(F32), (((0,), (0,)), ((), ())), precision=exact)
    inner = t_mm(movie[:, rim:], fit)
    total = jnp.where(
        closing, jnp.concatenate([inner, lead], 0), jnp.concatenate([lead, inner], 0)
    )
    square = t_mm(fit, fit)
    own = lax.dynamic_slice_in_dim(foot, here * share, share, 0).astype(F32)
    total = total - jnp.dot(own, square, precision=exact)
    return jnp.maximum(own + total / jnp.maximum(jnp.diagonal(square), 1.0), 0.0).astype(BF)


def on_device(recording, footprints, traces, live_count):
    frames, voxels = recording.shape
    extended, neurons = footprints.shape
    rim = extended - voxels
    main = voxels // 2 // rim - 1
    split = lax.axis_size("tm") == 2
    share_shape = [pltpu.VMEM((main * frames + frames // 2, rim), BF)] if split else []
    pinned = [
        pltpu.with_memory_space_constraint(x, pltpu.HBM)
        for x in (live_count, recording, footprints, traces)
    ]
    far, near, count, begun, *outgoing = call(
        functools.partial(rim_kernel, voxels),
        [
            pltpu.VMEM((frames, rim), BF),
            pltpu.VMEM((frames, rim), BF),
            pltpu.VMEM((8, neurons), jnp.int32),
            pltpu.VMEM((frames, neurons), F32),
        ]
        + share_shape,
        [LEFT_THERE] * 4,
        [WHOLE] * (4 + len(share_shape)),
        1.5,
        scratch_shapes=[
            pltpu.SMEM(live_count.shape, jnp.int32),
            pltpu.VMEM((2 * rim, neurons), BF),
            pltpu.VMEM((frames, rim), BF),
            pltpu.VMEM((frames, rim), BF),
            COPIES((6 + main,)),
        ],
    )(*pinned)
    far = swapped(far, 1)
    near = swapped(near, 0)
    plan, scale, cross_high, cross_low, rims, flat, masked, shown = call(
        functools.partial(drive_kernel, voxels),
        [
            shape((frames, neurons), F32),
            shape((8, neurons), F32),
            shape((GROUP, GROUP), BF),
            shape((GROUP, GROUP), BF),
            shape((2 * rim, neurons), BF),
            shape((rim, frames), BF),
            pltpu.VMEM((extended, neurons), BF),
            pltpu.VMEM((frames, voxels), BF),
        ],
        [WHOLE, LEFT_THERE, WHOLE, WHOLE],
        [WHOLE] * 8,
        1.6,
        scratch_shapes=[COPIES((2,))],
    )(count, pinned[1], footprints, begun)
    new_tr, rounded, far, near = call(
        sweep_kernel,
        [
            pltpu.VMEM((frames, neurons), F32),
            pltpu.VMEM((frames, neurons), BF),
            pltpu.VMEM((rim, frames), BF),
            pltpu.VMEM((rim, frames), BF),
        ],
        [WHOLE] * 8,
        [WHOLE] * 4,
        0.5,
    )(plan, scale, cross_high, cross_low, rims, flat, far, near)
    if split:
        return halved(voxels, rim, masked, shown, flat, outgoing[0], new_tr, rounded, far, near)
    return new_tr, spread(voxels, rim, masked, recording, rounded)


def solution(mesh):
    placed = (P("tm", "slab"), P(None, "slab"), P("tm", "slab"), P())
    return jax.shard_map(
        on_device,
        mesh=mesh,
        in_specs=placed,
        out_specs=(P("tm", "slab"), P("tm", "slab")),
        check_vma=False,
    )
```

```python
import functools

import jax
import jax.numpy as jnp
from jax import lax
from jax.experimental import pallas as pl
from jax.experimental.pallas import tpu as pltpu
from jax.sharding import PartitionSpec as P

GROUP = 128
BF = jnp.bfloat16
F32 = jnp.float32
WHOLE = pl.BlockSpec(memory_space=pltpu.VMEM)
LEFT_THERE = pl.BlockSpec(memory_space=pl.ANY)
COPIES = pltpu.SemaphoreType.DMA
shape = jax.ShapeDtypeStruct


def mm(left, right):
    return jnp.dot(left, right, preferred_element_type=F32)


def mm_t(left, right):
    return lax.dot_general(left, right, (((1,), (1,)), ((), ())), preferred_element_type=F32)


def t_mm(left, right):
    return lax.dot_general(left, right, (((0,), (0,)), ((), ())), preferred_element_type=F32)


def halves(wide):
    high = wide.astype(BF)
    return high, (wide - high.astype(F32)).astype(BF)


def coded(block):
    square = block * block
    fourth = square * square
    eighth = fourth * fourth
    return jnp.where(block < 0, -eighth, eighth).astype(BF)


def decoded(block):
    wide = block.astype(F32)
    size = jnp.abs(wide)
    root = jnp.where(size > 0, jnp.exp2(jnp.log2(size) * 0.125), 0.0)
    return jnp.where(wide < 0, -root, root)


def living(count, block):
    slots = lax.broadcasted_iota(jnp.int32, block.shape, 1)
    return jnp.where(slots < count, block, jnp.zeros_like(block))


def diagonal(square):
    rows = lax.broadcasted_iota(jnp.int32, square.shape, 0)
    columns = lax.broadcasted_iota(jnp.int32, square.shape, 1)
    return jnp.sum(jnp.where(rows == columns, square, 0.0), axis=0, keepdims=True)


def at_end(axis):
    return lax.axis_index(axis) == lax.axis_size(axis) - 1


def odd_slab():
    return lax.axis_index("slab") % 2 == 1


def call(body, outs, in_specs, out_specs, expected, **more):
    return pl.pallas_call(
        body,
        out_shape=outs,
        in_specs=in_specs,
        out_specs=out_specs,
        compiler_params=pltpu.CompilerParams(vmem_limit_bytes=32 * 1024 * 1024),
        cost_estimate=pl.CostEstimate(
            flops=0, bytes_accessed=int(expected * 3_690_000), transcendentals=0
        ),
        **more,
    )


def copied(source, target, sem):
    copy = pltpu.make_async_copy(source, target, sem)
    copy.start()
    return copy


def first_column(which, voxels, rim):
    return pl.multiple_of(rim + which * (voxels // 2), 128)


def rolled(block):
    half = block.shape[1] // 2
    return jnp.concatenate([block[:, half:], block[:, :half]], axis=1)


def packed(which, middle):
    frames = middle.shape[0] // 2
    top, bottom = middle[:frames], middle[frames:]
    low = jnp.where(which == 0, top, rolled(top))
    high = jnp.where(which == 0, rolled(bottom), bottom)
    slots = lax.broadcasted_iota(jnp.int32, low.shape, 1)
    return jnp.where(slots < low.shape[1] // 2, low, high)


def unpacked(which, block):
    turned = rolled(block)
    top = jnp.where(which == 0, block, turned)
    bottom = jnp.where(which == 0, turned, block)
    return jnp.concatenate([top, bottom], axis=0)


def for_near_and_far(forward, backward):
    odd = odd_slab()
    return jnp.where(odd, backward, forward), jnp.where(odd, forward, backward)


def from_prev_and_next(near, far):
    odd = odd_slab()
    return jnp.where(odd, near, far), jnp.where(odd, far, near)


def rim_kernel(voxels, live, movie, foot, start, far, near, count, traces, *rest):
    numbers, rims, edge, middle, sems = rest[-5:]
    rim = edge.shape[1]
    frames = edge.shape[0]
    there = 1 - lax.axis_index("tm")
    part = frames // 2
    pieces = [pl.ds(i * part, part) for i in range(2)]
    begun = [copied(start.at[piece], traces.at[piece], sems.at[i]) for i, piece in enumerate(pieces)]
    column = copied(movie.at[:, pl.ds(voxels // 2, rim)], middle, sems.at[5])
    small = [
        copied(live, numbers, sems.at[sems.shape[0] - 1]),
        copied(foot.at[pl.ds(0, rim)], rims.at[pl.ds(0, rim)], sems.at[2]),
        copied(foot.at[pl.ds(voxels, rim)], rims.at[pl.ds(rim, rim)], sems.at[3]),
        copied(movie.at[:, pl.ds(0, rim)], edge, sems.at[4]),
    ]
    large = []
    if len(rest) > 5:
        first = first_column(there, voxels, rim)
        for i in range(voxels // 2 // rim - 1):
            block = movie.at[:, pl.ds(pl.multiple_of(first + i * rim, 128), rim)]
            large.append(copied(block, rest[0].at[pl.ds(i * frames, frames)], sems.at[6 + i]))
    for copy in small:
        copy.wait()
    alive = numbers[lax.axis_index("slab")]
    count[...] = jnp.full(count.shape, alive, jnp.int32)
    both = rims[...]
    both = jnp.concatenate([both, both], axis=1)
    column.wait()
    if large:
        rest[0][(voxels // 2 // rim - 1) * frames:] = packed(there, middle[...])
    for i in range(2):
        begun[i].wait()
        rows = slice(i * part, (i + 1) * part)
        seen = mm_t(jnp.concatenate(halves(living(alive, traces[rows])), axis=1), both)
        one, two = for_near_and_far(seen[:, rim:], edge[rows].astype(F32) - seen[:, :rim])
        near[rows] = coded(one)
        far[rows] = coded(two)
    for copy in large:
        copy.wait()


def drive_kernel(
    voxels, count, movie, foot, start, plan, scale, cross_high, cross_low, rims, flat, masked, shown, sems
):
    rim = foot.shape[0] - voxels
    step = voxels // 2
    loads = []
    for i in range(2):
        columns = pl.ds(i * step, step)
        loads.append(copied(movie.at[:, columns], shown.at[:, columns], sems.at[i]))
    alive = count[0:1]
    masked[:voxels] = living(alive, foot[:voxels])
    ends = living(alive, foot[voxels:])
    masked[voxels:] = jnp.where(at_end("slab"), jnp.zeros_like(ends), ends)
    rims[:rim] = -masked[:rim]
    rims[rim:] = masked[voxels:]
    gram = t_mm(masked[...], masked[...])
    loads[0].wait()
    flat[...] = shown[:, :rim].T
    drive = mm(shown[:, :step], masked[:step])
    loads[1].wait()
    drive = drive + mm(shown[:, step:], masked[step:voxels])
    inverse = 1.0 / (diagonal(gram) + 1e-06)
    scale[...] = jnp.broadcast_to(inverse, scale.shape)
    gram_high, gram_low = halves(gram)
    cross_high[...] = gram_high[:GROUP, GROUP:]
    cross_low[...] = gram_low[:GROUP, GROUP:]
    current = living(alive, start[...])
    high, low = halves(current)
    for at in range(0, current.shape[1], GROUP):
        columns = slice(at, at + GROUP)
        coupled = mm(high[:, at:], gram_high[at:, columns]) + mm(high[:, at:], gram_low[at:, columns])
        coupled = coupled + mm(low[:, at:], gram_high[at:, columns])
        plan[:, columns] = current[:, columns] + (drive[:, columns] - coupled) * inverse[:, columns]


def sweep_kernel(
    plan, scale, cross_high, cross_low, rims, flat, far, near, traces, rounded, far_next, near_next
):
    rim = flat.shape[0]
    edges = rims[...]
    high, low = halves(decoded(jnp.concatenate(from_prev_and_next(near[...], far[...]), axis=1)))
    both = jnp.concatenate([edges, edges], axis=0)
    stepped = plan[...] + mm(jnp.concatenate([high, low], axis=1), both) * scale[0:1]
    first = jnp.maximum(stepped[:, :GROUP], 0.0)
    high, low = halves(first)
    cross = cross_high[...]
    coupled = mm(
        jnp.concatenate([high, low, high], axis=1), jnp.concatenate([cross, cross, cross_low[...]], axis=0)
    )
    second = jnp.maximum(stepped[:, GROUP:] - coupled * scale[0:1, GROUP:], 0.0)
    whole = jnp.concatenate([high, second.astype(BF)], axis=1)
    rounded[...] = whole
    seen = mm_t(edges, whole)
    one, two = for_near_and_far(seen[rim:], flat[...].astype(F32) + seen[:rim])
    near_next[...] = one.astype(BF)
    far_next[...] = two.astype(BF)
    traces[:, :GROUP] = first
    traces[:, GROUP:] = second


def own_kernel(voxels, movie, foot, fit, flat, total, quad, rim_part):
    rim = flat.shape[0]
    main = voxels // 2 - rim
    traces = fit[...]
    square = t_mm(traces, traces)
    quad[...] = square
    high, low = halves(square)
    begins, ends = foot[:rim], foot[voxels:]
    rim_part[:rim] = mm(flat[...], traces) - (mm(begins, high) + mm(begins, low))
    rim_part[rim:] = -(mm(ends, high) + mm(ends, low))
    first = first_column(lax.axis_index("tm"), voxels, rim)
    total[:main] = t_mm(movie[:, pl.ds(first, main)], traces)
    total[main:] = t_mm(movie[:, voxels // 2:voxels // 2 + rim], traces)


def both_kernel(rim_part, fit, far, near, lead, sent):
    rim = lead.shape[0]
    first = lax.axis_index("tm") == 0
    before, after = from_prev_and_next(near[...], far[...])
    traces = fit[...]
    begins = rim_part[:rim] - mm(before, traces)
    ends = rim_part[rim:] + mm(after, traces)
    lead[...] = jnp.where(first, begins, ends)
    sent[...] = jnp.where(first, ends, begins).astype(BF)


def main_kernel(voxels, rim, foot, total, quad, movie, fit, traces, out, new_tr, scale, moved, sems):
    here = lax.axis_index("tm")
    frames = fit.shape[0]
    width = voxels // 2
    main = width - rim
    written = [copied(traces, new_tr, sems.at[0])]
    fitted = fit[...]
    square = quad[...] + t_mm(fitted, fitted)
    inverse = 1.0 / jnp.maximum(diagonal(square), 1.0)
    scale[...] = jnp.broadcast_to(inverse, scale.shape)
    high, low = halves(square)
    first = first_column(here, voxels, rim)
    row = pl.multiple_of(rim - here * (rim // 2), 64)
    for begin, end in ((0, width // 2), (width // 2, main), (main, width)):
        if begin < main:
            own = foot[pl.ds(pl.multiple_of(first + begin, 128), end - begin)]
            columns = range(begin // rim, end // rim)
            shown = jnp.concatenate([movie[i * frames:(i + 1) * frames] for i in columns], axis=1)
        else:
            own = foot[width:width + rim]
            shown = unpacked(here, movie[main // rim * frames:])
        part = total[begin:end] + t_mm(shown, fitted) - (mm(own, high) + mm(own, low))
        moved[begin:end] = jnp.maximum(own.astype(F32) + part * inverse, 0.0).astype(BF)
        if begin < main:
            target = out.at[pl.ds(row + begin, end - begin)]
            written.append(copied(moved.at[pl.ds(begin, end - begin)], target, sems.at[len(written)]))
        else:
            half = rim // 2
            source = moved.at[pl.ds(pl.multiple_of(main + here * half, 64), half)]
            target = out.at[pl.ds(pl.multiple_of((1 - here) * (out.shape[0] - half), 64), half)]
            written.append(copied(source, target, sems.at[len(written)]))
    for copy in written:
        copy.wait()


def edge_kernel(voxels, sofar, foot, lead, came, scale, out, moved, sem):
    rim = lead.shape[0]
    here = lax.axis_index("tm")
    own = foot[pl.ds(pl.multiple_of(here * voxels, 128), rim)].astype(F32)
    moved[...] = jnp.maximum(own + (lead[...] + came[...].astype(F32)) * scale[0:1], 0.0).astype(BF)
    row = pl.multiple_of(here * (out.shape[0] - rim), 64)
    copied(moved, out.at[pl.ds(row, rim)], sem).wait()


def swapped(block, first):
    route = [(i, i + 1) for i in range(first, lax.axis_size("slab") - 1, 2)]
    return lax.ppermute(block, "slab", [(j, i) for i, j in route] + route)


def halved(voxels, rim, foot, recording, flat, outgoing, new_tr, rounded, far, near):
    frames = recording.shape[0]
    extended, neurons = foot.shape
    width, share = voxels // 2, extended // 2
    across = [(0, 1), (1, 0)]
    movie = lax.ppermute(outgoing, "tm", across)
    far = swapped(far, 1)
    near = swapped(near, 0)
    other = lax.ppermute(rounded, "tm", across)
    total, quad, rim_part = call(
        functools.partial(own_kernel, voxels),
        [
            shape((width, neurons), F32),
            shape((neurons, neurons), F32),
            shape((2 * rim, neurons), F32),
        ],
        [WHOLE] * 4,
        [WHOLE] * 3,
        0.6,
    )(recording, foot, rounded, flat)
    lead, sent = call(
        both_kernel,
        [shape((rim, neurons), F32), pltpu.VMEM((rim, neurons), BF)],
        [WHOLE] * 4,
        [WHOLE] * 2,
        0.3,
    )(rim_part, rounded, far, near)
    came = lax.ppermute(sent, "tm", across)
    sofar, new_tr, scale = call(
        functools.partial(main_kernel, voxels, rim),
        [pltpu.HBM((share, neurons), BF), pltpu.HBM((frames, neurons), F32), shape((8, neurons), F32)],
        [WHOLE] * 6,
        [LEFT_THERE] * 2 + [WHOLE],
        2.0,
        scratch_shapes=[pltpu.VMEM((width, neurons), BF), COPIES((4,))],
    )(foot, total, quad, movie, other, new_tr)
    new_foot = call(
        functools.partial(edge_kernel, voxels),
        pltpu.HBM((share, neurons), BF),
        [LEFT_THERE] + [WHOLE] * 4,
        LEFT_THERE,
        0.8,
        input_output_aliases={0: 0},
        scratch_shapes=[pltpu.VMEM((rim, neurons), BF), COPIES],
    )(sofar, foot, lead, came, scale)
    return new_tr, new_foot


def spread(voxels, rim, foot, recording, rounded):
    slabs, parts = lax.axis_size("slab"), lax.axis_size("tm")
    extended, neurons = foot.shape
    share = extended // parts
    here = lax.axis_index("tm")
    closing = here == parts - 1
    exact = lax.Precision.HIGHEST
    cut = voxels - (share - rim)
    columns = jnp.concatenate([recording[:, :cut], recording[:, :rim], recording[:, cut:]], 1)
    movie = lax.all_to_all(columns, "tm", split_axis=1, concat_axis=0, tiled=True)
    fit = lax.all_gather(rounded, "tm", axis=0, tiled=True)
    edge = jnp.where(here == 0, foot[voxels:], foot[:rim])
    seen = movie[:, :rim].astype(F32)
    sent = jnp.where(here == 0, 0.0, seen) - mm_t(fit, edge)
    ahead = [(i * parts, (i + 1) * parts) for i in range(slabs - 1)]
    behind = [((i + 2) * parts - 1, (i + 1) * parts - 1) for i in range(slabs - 1)]
    lead = jnp.where(closing, 0.0, seen) + lax.ppermute(sent, ("slab", "tm"), ahead + behind)
    lead = lax.dot_general(lead, fit.astype(F32), (((0,), (0,)), ((), ())), precision=exact)
    inner = t_mm(movie[:, rim:], fit)
    total = jnp.where(
        closing, jnp.concatenate([inner, lead], 0), jnp.concatenate([lead, inner], 0)
    )
    square = t_mm(fit, fit)
    own = lax.dynamic_slice_in_dim(foot, here * share, share, 0).astype(F32)
    total = total - jnp.dot(own, square, precision=exact)
    return jnp.maximum(own + total / jnp.maximum(jnp.diagonal(square), 1.0), 0.0).astype(BF)


def on_device(recording, footprints, traces, live_count):
    frames, voxels = recording.shape
    extended, neurons = footprints.shape
    rim = extended - voxels
    main = voxels // 2 // rim - 1
    split = lax.axis_size("tm") == 2
    share_shape = [pltpu.VMEM((main * frames + frames // 2, rim), BF)] if split else []
    pinned = [
        pltpu.with_memory_space_constraint(x, pltpu.HBM)
        for x in (live_count, recording, footprints, traces)
    ]
    far, near, count, begun, *outgoing = call(
        functools.partial(rim_kernel, voxels),
        [
            pltpu.VMEM((frames, rim), BF),
            pltpu.VMEM((frames, rim), BF),
            pltpu.VMEM((8, neurons), jnp.int32),
            pltpu.VMEM((frames, neurons), F32),
        ]
        + share_shape,
        [LEFT_THERE] * 4,
        [WHOLE] * (4 + len(share_shape)),
        1.5,
        scratch_shapes=[
            pltpu.SMEM(live_count.shape, jnp.int32),
            pltpu.VMEM((2 * rim, neurons), BF),
            pltpu.VMEM((frames, rim), BF),
            pltpu.VMEM((frames, rim), BF),
            COPIES((7 + main,)),
        ],
    )(*pinned)
    far = swapped(far, 1)
    near = swapped(near, 0)
    plan, scale, cross_high, cross_low, rims, flat, masked, shown = call(
        functools.partial(drive_kernel, voxels),
        [
            shape((frames, neurons), F32),
            shape((8, neurons), F32),
            shape((GROUP, GROUP), BF),
            shape((GROUP, GROUP), BF),
            shape((2 * rim, neurons), BF),
            shape((rim, frames), BF),
            pltpu.VMEM((extended, neurons), BF),
            pltpu.VMEM((frames, voxels), BF),
        ],
        [WHOLE, LEFT_THERE, WHOLE, WHOLE],
        [WHOLE] * 8,
        1.6,
        scratch_shapes=[COPIES((2,))],
    )(count, pinned[1], footprints, begun)
    new_tr, rounded, far, near = call(
        sweep_kernel,
        [
            pltpu.VMEM((frames, neurons), F32),
            pltpu.VMEM((frames, neurons), BF),
            pltpu.VMEM((rim, frames), BF),
            pltpu.VMEM((rim, frames), BF),
        ],
        [WHOLE] * 8,
        [WHOLE] * 4,
        0.5,
    )(plan, scale, cross_high, cross_low, rims, flat, far, near)
    if split:
        return halved(voxels, rim, masked, shown, flat, outgoing[0], new_tr, rounded, far, near)
    return new_tr, spread(voxels, rim, masked, recording, rounded)


def solution(mesh):
    placed = (P("tm", "slab"), P(None, "slab"), P("tm", "slab"), P())
    return jax.shard_map(
        on_device,
        mesh=mesh,
        in_specs=placed,
        out_specs=(P("tm", "slab"), P("tm", "slab")),
        check_vma=False,
    )
```

```python
import functools

import jax
import jax.numpy as jnp
from jax import lax
from jax.experimental import pallas as pl
from jax.experimental.pallas import tpu as pltpu
from jax.sharding import PartitionSpec as P

GROUP = 128
BF = jnp.bfloat16
F32 = jnp.float32
WHOLE = pl.BlockSpec(memory_space=pltpu.VMEM)
LEFT_THERE = pl.BlockSpec(memory_space=pl.ANY)
COPIES = pltpu.SemaphoreType.DMA
shape = jax.ShapeDtypeStruct


def mm(left, right):
    return jnp.dot(left, right, preferred_element_type=F32)


def mm_t(left, right):
    return lax.dot_general(left, right, (((1,), (1,)), ((), ())), preferred_element_type=F32)


def t_mm(left, right):
    return lax.dot_general(left, right, (((0,), (0,)), ((), ())), preferred_element_type=F32)


def halves(wide):
    high = wide.astype(BF)
    return high, (wide - high.astype(F32)).astype(BF)


def coded(block):
    square = block * block
    fourth = square * square
    eighth = fourth * fourth
    return jnp.where(block < 0, -eighth, eighth).astype(BF)


def decoded(block):
    wide = block.astype(F32)
    size = jnp.abs(wide)
    root = jnp.where(size > 0, jnp.exp2(jnp.log2(size) * 0.125), 0.0)
    return jnp.where(wide < 0, -root, root)


def living(count, block):
    slots = lax.broadcasted_iota(jnp.int32, block.shape, 1)
    return jnp.where(slots < count, block, jnp.zeros_like(block))


def diagonal(square):
    rows = lax.broadcasted_iota(jnp.int32, square.shape, 0)
    columns = lax.broadcasted_iota(jnp.int32, square.shape, 1)
    return jnp.sum(jnp.where(rows == columns, square, 0.0), axis=0, keepdims=True)


def at_end(axis):
    return lax.axis_index(axis) == lax.axis_size(axis) - 1


def odd_slab():
    return lax.axis_index("slab") % 2 == 1


def call(body, outs, in_specs, out_specs, expected, **more):
    return pl.pallas_call(
        body,
        out_shape=outs,
        in_specs=in_specs,
        out_specs=out_specs,
        compiler_params=pltpu.CompilerParams(vmem_limit_bytes=32 * 1024 * 1024),
        cost_estimate=pl.CostEstimate(
            flops=0, bytes_accessed=int(expected * 3_690_000), transcendentals=0
        ),
        **more,
    )


def copied(source, target, sem):
    copy = pltpu.make_async_copy(source, target, sem)
    copy.start()
    return copy


def first_column(which, voxels, rim):
    return pl.multiple_of(rim + which * (voxels // 2), 128)


def rolled(block):
    half = block.shape[1] // 2
    return jnp.concatenate([block[:, half:], block[:, :half]], axis=1)


def packed(which, middle):
    frames = middle.shape[0] // 2
    top, bottom = middle[:frames], middle[frames:]
    low = jnp.where(which == 0, top, rolled(top))
    high = jnp.where(which == 0, rolled(bottom), bottom)
    slots = lax.broadcasted_iota(jnp.int32, low.shape, 1)
    return jnp.where(slots < low.shape[1] // 2, low, high)


def unpacked(which, block):
    turned = rolled(block)
    top = jnp.where(which == 0, block, turned)
    bottom = jnp.where(which == 0, turned, block)
    return jnp.concatenate([top, bottom], axis=0)


def for_near_and_far(forward, backward):
    odd = odd_slab()
    return jnp.where(odd, backward, forward), jnp.where(odd, forward, backward)


def from_prev_and_next(near, far):
    odd = odd_slab()
    return jnp.where(odd, near, far), jnp.where(odd, far, near)


def rim_kernel(voxels, live, movie, foot, start, far, near, count, traces, *rest):
    numbers, rims, edge, middle, sems = rest[-5:]
    rim = edge.shape[1]
    frames = edge.shape[0]
    there = 1 - lax.axis_index("tm")
    small = [
        copied(live, numbers, sems.at[0]),
        copied(start, traces, sems.at[1]),
        copied(foot.at[pl.ds(0, rim)], rims.at[pl.ds(0, rim)], sems.at[2]),
        copied(foot.at[pl.ds(voxels, rim)], rims.at[pl.ds(rim, rim)], sems.at[3]),
        copied(movie.at[:, pl.ds(0, rim)], edge, sems.at[4]),
        copied(movie.at[:, pl.ds(voxels // 2, rim)], middle, sems.at[5]),
    ]
    large = []
    if len(rest) > 5:
        first = first_column(there, voxels, rim)
        for i in range(voxels // 2 // rim - 1):
            column = movie.at[:, pl.ds(pl.multiple_of(first + i * rim, 128), rim)]
            large.append(copied(column, rest[0].at[pl.ds(i * frames, frames)], sems.at[6 + i]))
    for copy in small:
        copy.wait()
    alive = numbers[lax.axis_index("slab")]
    count[...] = jnp.full(count.shape, alive, jnp.int32)
    seen = mm_t(jnp.concatenate(halves(living(alive, traces[...])), axis=0), rims[...])
    seen = seen[:frames] + seen[frames:]
    backward = edge[...].astype(F32) - seen[:, :rim]
    one, two = for_near_and_far(seen[:, rim:], backward)
    near[...] = coded(one)
    far[...] = coded(two)
    if large:
        rest[0][(voxels // 2 // rim - 1) * frames:] = packed(there, middle[...])
    for copy in large:
        copy.wait()


def drive_kernel(
    voxels, count, movie, foot, start, plan, scale, cross_high, cross_low, rims, flat, masked, shown, sems
):
    rim = foot.shape[0] - voxels
    step = voxels // 2
    loads = []
    for i in range(2):
        columns = pl.ds(i * step, step)
        loads.append(copied(movie.at[:, columns], shown.at[:, columns], sems.at[i]))
    alive = count[0:1]
    masked[:voxels] = living(alive, foot[:voxels])
    ends = living(alive, foot[voxels:])
    masked[voxels:] = jnp.where(at_end("slab"), jnp.zeros_like(ends), ends)
    rims[:rim] = -masked[:rim]
    rims[rim:] = masked[voxels:]
    gram = t_mm(masked[...], masked[...])
    loads[0].wait()
    flat[...] = shown[:, :rim].T
    drive = mm(shown[:, :step], masked[:step])
    loads[1].wait()
    drive = drive + mm(shown[:, step:], masked[step:voxels])
    inverse = 1.0 / (diagonal(gram) + 1e-06)
    scale[...] = jnp.broadcast_to(inverse, scale.shape)
    gram_high, gram_low = halves(gram)
    cross_high[...] = gram_high[:GROUP, GROUP:]
    cross_low[...] = gram_low[:GROUP, GROUP:]
    current = living(alive, start[...])
    high, low = halves(current)
    for at in range(0, current.shape[1], GROUP):
        columns = slice(at, at + GROUP)
        coupled = mm(high[:, at:], gram_high[at:, columns]) + mm(high[:, at:], gram_low[at:, columns])
        coupled = coupled + mm(low[:, at:], gram_high[at:, columns])
        plan[:, columns] = current[:, columns] + (drive[:, columns] - coupled) * inverse[:, columns]


def sweep_kernel(
    plan, scale, cross_high, cross_low, rims, flat, far, near, traces, rounded, far_next, near_next
):
    rim = flat.shape[0]
    edges = rims[...]
    high, low = halves(decoded(jnp.concatenate(from_prev_and_next(near[...], far[...]), axis=1)))
    both = jnp.concatenate([edges, edges], axis=0)
    stepped = plan[...] + mm(jnp.concatenate([high, low], axis=1), both) * scale[0:1]
    first = jnp.maximum(stepped[:, :GROUP], 0.0)
    high, low = halves(first)
    cross = cross_high[...]
    coupled = mm(
        jnp.concatenate([high, low, high], axis=1), jnp.concatenate([cross, cross, cross_low[...]], axis=0)
    )
    second = jnp.maximum(stepped[:, GROUP:] - coupled * scale[0:1, GROUP:], 0.0)
    whole = jnp.concatenate([high, second.astype(BF)], axis=1)
    rounded[...] = whole
    seen = mm_t(edges, whole)
    one, two = for_near_and_far(seen[rim:], flat[...].astype(F32) + seen[:rim])
    near_next[...] = one.astype(BF)
    far_next[...] = two.astype(BF)
    traces[:, :GROUP] = first
    traces[:, GROUP:] = second


def own_kernel(voxels, movie, foot, fit, flat, total, quad, rim_part):
    rim = flat.shape[0]
    main = voxels // 2 - rim
    traces = fit[...]
    square = t_mm(traces, traces)
    quad[...] = square
    high, low = halves(square)
    begins, ends = foot[:rim], foot[voxels:]
    rim_part[:rim] = mm(flat[...], traces) - (mm(begins, high) + mm(begins, low))
    rim_part[rim:] = -(mm(ends, high) + mm(ends, low))
    first = first_column(lax.axis_index("tm"), voxels, rim)
    total[:main] = t_mm(movie[:, pl.ds(first, main)], traces)
    total[main:] = t_mm(movie[:, voxels // 2:voxels // 2 + rim], traces)


def both_kernel(rim_part, fit, far, near, lead, sent):
    rim = lead.shape[0]
    first = lax.axis_index("tm") == 0
    before, after = from_prev_and_next(near[...], far[...])
    traces = fit[...]
    begins = rim_part[:rim] - mm(before, traces)
    ends = rim_part[rim:] + mm(after, traces)
    lead[...] = jnp.where(first, begins, ends)
    sent[...] = jnp.where(first, ends, begins).astype(BF)


def main_kernel(voxels, rim, foot, total, quad, movie, fit, traces, out, new_tr, scale, moved, sems):
    here = lax.axis_index("tm")
    frames = fit.shape[0]
    width = voxels // 2
    main = width - rim
    written = [copied(traces, new_tr, sems.at[0])]
    fitted = fit[...]
    square = quad[...] + t_mm(fitted, fitted)
    inverse = 1.0 / jnp.maximum(diagonal(square), 1.0)
    scale[...] = jnp.broadcast_to(inverse, scale.shape)
    high, low = halves(square)
    first = first_column(here, voxels, rim)
    row = pl.multiple_of(rim - here * (rim // 2), 64)
    for begin, end in ((0, width // 2), (width // 2, main), (main, width)):
        if begin < main:
            own = foot[pl.ds(pl.multiple_of(first + begin, 128), end - begin)]
            columns = range(begin // rim, end // rim)
            shown = jnp.concatenate([movie[i * frames:(i + 1) * frames] for i in columns], axis=1)
        else:
            own = foot[width:width + rim]
            shown = unpacked(here, movie[main // rim * frames:])
        part = total[begin:end] + t_mm(shown, fitted) - (mm(own, high) + mm(own, low))
        moved[begin:end] = jnp.maximum(own.astype(F32) + part * inverse, 0.0).astype(BF)
        if begin < main:
            target = out.at[pl.ds(row + begin, end - begin)]
            written.append(copied(moved.at[pl.ds(begin, end - begin)], target, sems.at[len(written)]))
        else:
            half = rim // 2
            source = moved.at[pl.ds(pl.multiple_of(main + here * half, 64), half)]
            target = out.at[pl.ds(pl.multiple_of((1 - here) * (out.shape[0] - half), 64), half)]
            written.append(copied(source, target, sems.at[len(written)]))
    for copy in written:
        copy.wait()


def edge_kernel(voxels, sofar, foot, lead, came, scale, out, moved, sem):
    rim = lead.shape[0]
    here = lax.axis_index("tm")
    own = foot[pl.ds(pl.multiple_of(here * voxels, 128), rim)].astype(F32)
    moved[...] = jnp.maximum(own + (lead[...] + came[...].astype(F32)) * scale[0:1], 0.0).astype(BF)
    row = pl.multiple_of(here * (out.shape[0] - rim), 64)
    copied(moved, out.at[pl.ds(row, rim)], sem).wait()


def swapped(block, first):
    route = [(i, i + 1) for i in range(first, lax.axis_size("slab") - 1, 2)]
    return lax.ppermute(block, "slab", [(j, i) for i, j in route] + route)


def halved(voxels, rim, foot, recording, flat, outgoing, new_tr, rounded, far, near):
    frames = recording.shape[0]
    extended, neurons = foot.shape
    width, share = voxels // 2, extended // 2
    across = [(0, 1), (1, 0)]
    movie = lax.ppermute(outgoing, "tm", across)
    far = swapped(far, 1)
    near = swapped(near, 0)
    other = lax.ppermute(rounded, "tm", across)
    total, quad, rim_part = call(
        functools.partial(own_kernel, voxels),
        [
            shape((width, neurons), F32),
            shape((neurons, neurons), F32),
            shape((2 * rim, neurons), F32),
        ],
        [WHOLE] * 4,
        [WHOLE] * 3,
        0.6,
    )(recording, foot, rounded, flat)
    lead, sent = call(
        both_kernel,
        [shape((rim, neurons), F32), pltpu.VMEM((rim, neurons), BF)],
        [WHOLE] * 4,
        [WHOLE] * 2,
        0.3,
    )(rim_part, rounded, far, near)
    came = lax.ppermute(sent, "tm", across)
    sofar, new_tr, scale = call(
        functools.partial(main_kernel, voxels, rim),
        [pltpu.HBM((share, neurons), BF), pltpu.HBM((frames, neurons), F32), shape((8, neurons), F32)],
        [WHOLE] * 6,
        [LEFT_THERE] * 2 + [WHOLE],
        2.0,
        scratch_shapes=[pltpu.VMEM((width, neurons), BF), COPIES((4,))],
    )(foot, total, quad, movie, other, new_tr)
    new_foot = call(
        functools.partial(edge_kernel, voxels),
        pltpu.HBM((share, neurons), BF),
        [LEFT_THERE] + [WHOLE] * 4,
        LEFT_THERE,
        0.8,
        input_output_aliases={0: 0},
        scratch_shapes=[pltpu.VMEM((rim, neurons), BF), COPIES],
    )(sofar, foot, lead, came, scale)
    return new_tr, new_foot


def spread(voxels, rim, foot, recording, rounded):
    slabs, parts = lax.axis_size("slab"), lax.axis_size("tm")
    extended, neurons = foot.shape
    share = extended // parts
    here = lax.axis_index("tm")
    closing = here == parts - 1
    exact = lax.Precision.HIGHEST
    cut = voxels - (share - rim)
    columns = jnp.concatenate([recording[:, :cut], recording[:, :rim], recording[:, cut:]], 1)
    movie = lax.all_to_all(columns, "tm", split_axis=1, concat_axis=0, tiled=True)
    fit = lax.all_gather(rounded, "tm", axis=0, tiled=True)
    edge = jnp.where(here == 0, foot[voxels:], foot[:rim])
    seen = movie[:, :rim].astype(F32)
    sent = jnp.where(here == 0, 0.0, seen) - mm_t(fit, edge)
    ahead = [(i * parts, (i + 1) * parts) for i in range(slabs - 1)]
    behind = [((i + 2) * parts - 1, (i + 1) * parts - 1) for i in range(slabs - 1)]
    lead = jnp.where(closing, 0.0, seen) + lax.ppermute(sent, ("slab", "tm"), ahead + behind)
    lead = lax.dot_general(lead, fit.astype(F32), (((0,), (0,)), ((), ())), precision=exact)
    inner = t_mm(movie[:, rim:], fit)
    total = jnp.where(
        closing, jnp.concatenate([inner, lead], 0), jnp.concatenate([lead, inner], 0)
    )
    square = t_mm(fit, fit)
    own = lax.dynamic_slice_in_dim(foot, here * share, share, 0).astype(F32)
    total = total - jnp.dot(own, square, precision=exact)
    return jnp.maximum(own + total / jnp.maximum(jnp.diagonal(square), 1.0), 0.0).astype(BF)


def on_device(recording, footprints, traces, live_count):
    frames, voxels = recording.shape
    extended, neurons = footprints.shape
    rim = extended - voxels
    main = voxels // 2 // rim - 1
    split = lax.axis_size("tm") == 2
    share_shape = [pltpu.VMEM((main * frames + frames // 2, rim), BF)] if split else []
    pinned = [
        pltpu.with_memory_space_constraint(x, pltpu.HBM)
        for x in (live_count, recording, footprints, traces)
    ]
    far, near, count, begun, *outgoing = call(
        functools.partial(rim_kernel, voxels),
        [
            pltpu.VMEM((frames, rim), BF),
            pltpu.VMEM((frames, rim), BF),
            pltpu.VMEM((8, neurons), jnp.int32),
            pltpu.VMEM((frames, neurons), F32),
        ]
        + share_shape,
        [LEFT_THERE] * 4,
        [WHOLE] * (4 + len(share_shape)),
        1.5,
        scratch_shapes=[
            pltpu.SMEM(live_count.shape, jnp.int32),
            pltpu.VMEM((2 * rim, neurons), BF),
            pltpu.VMEM((frames, rim), BF),
            pltpu.VMEM((frames, rim), BF),
            COPIES((6 + main,)),
        ],
    )(*pinned)
    far = swapped(far, 1)
    near = swapped(near, 0)
    plan, scale, cross_high, cross_low, rims, flat, masked, shown = call(
        functools.partial(drive_kernel, voxels),
        [
            shape((frames, neurons), F32),
            shape((8, neurons), F32),
            shape((GROUP, GROUP), BF),
            shape((GROUP, GROUP), BF),
            shape((2 * rim, neurons), BF),
            shape((rim, frames), BF),
            pltpu.VMEM((extended, neurons), BF),
            pltpu.VMEM((frames, voxels), BF),
        ],
        [WHOLE, LEFT_THERE, WHOLE, WHOLE],
        [WHOLE] * 8,
        1.6,
        scratch_shapes=[COPIES((2,))],
    )(count, pinned[1], footprints, begun)
    new_tr, rounded, far, near = call(
        sweep_kernel,
        [
            pltpu.VMEM((frames, neurons), F32),
            pltpu.VMEM((frames, neurons), BF),
            pltpu.VMEM((rim, frames), BF),
            pltpu.VMEM((rim, frames), BF),
        ],
        [WHOLE] * 8,
        [WHOLE] * 4,
        0.5,
    )(plan, scale, cross_high, cross_low, rims, flat, far, near)
    if split:
        return halved(voxels, rim, masked, shown, flat, outgoing[0], new_tr, rounded, far, near)
    return new_tr, spread(voxels, rim, masked, recording, rounded)


def solution(mesh):
    placed = (P("tm", "slab"), P(None, "slab"), P("tm", "slab"), P())
    return jax.shard_map(
        on_device,
        mesh=mesh,
        in_specs=placed,
        out_specs=(P("tm", "slab"), P("tm", "slab")),
        check_vma=False,
    )
```

```python
import functools

import jax
import jax.numpy as jnp
from jax import lax
from jax.experimental import pallas as pl
from jax.experimental.pallas import tpu as pltpu
from jax.sharding import PartitionSpec as P

GROUP = 128
BF = jnp.bfloat16
F32 = jnp.float32
WHOLE = pl.BlockSpec(memory_space=pltpu.VMEM)
LEFT_THERE = pl.BlockSpec(memory_space=pl.ANY)
COPIES = pltpu.SemaphoreType.DMA
shape = jax.ShapeDtypeStruct


def mm(left, right):
    return jnp.dot(left, right, preferred_element_type=F32)


def mm_t(left, right):
    return lax.dot_general(left, right, (((1,), (1,)), ((), ())), preferred_element_type=F32)


def t_mm(left, right):
    return lax.dot_general(left, right, (((0,), (0,)), ((), ())), preferred_element_type=F32)


def halves(wide):
    high = wide.astype(BF)
    return high, (wide - high.astype(F32)).astype(BF)


def coded(block):
    square = block * block
    fourth = square * square
    eighth = fourth * fourth
    return jnp.where(block < 0, -eighth, eighth).astype(BF)


def decoded(block):
    wide = block.astype(F32)
    size = jnp.abs(wide)
    root = jnp.where(size > 0, jnp.exp2(jnp.log2(size) * 0.125), 0.0)
    return jnp.where(wide < 0, -root, root)


def living(count, block):
    slots = lax.broadcasted_iota(jnp.int32, block.shape, 1)
    return jnp.where(slots < count, block, jnp.zeros_like(block))


def diagonal(square):
    rows = lax.broadcasted_iota(jnp.int32, square.shape, 0)
    columns = lax.broadcasted_iota(jnp.int32, square.shape, 1)
    return jnp.sum(jnp.where(rows == columns, square, 0.0), axis=0, keepdims=True)


def at_end(axis):
    return lax.axis_index(axis) == lax.axis_size(axis) - 1


def odd_slab():
    return lax.axis_index("slab") % 2 == 1


def call(body, outs, in_specs, out_specs, expected, **more):
    return pl.pallas_call(
        body,
        out_shape=outs,
        in_specs=in_specs,
        out_specs=out_specs,
        compiler_params=pltpu.CompilerParams(vmem_limit_bytes=32 * 1024 * 1024),
        cost_estimate=pl.CostEstimate(
            flops=0, bytes_accessed=int(expected * 3_690_000), transcendentals=0
        ),
        **more,
    )


def copied(source, target, sem):
    copy = pltpu.make_async_copy(source, target, sem)
    copy.start()
    return copy


def first_column(which, voxels, rim):
    return pl.multiple_of(rim + which * (voxels // 2), 128)


def rolled(block):
    half = block.shape[1] // 2
    return jnp.concatenate([block[:, half:], block[:, :half]], axis=1)


def packed(which, middle):
    frames = middle.shape[0] // 2
    top, bottom = middle[:frames], middle[frames:]
    low = jnp.where(which == 0, top, rolled(top))
    high = jnp.where(which == 0, rolled(bottom), bottom)
    slots = lax.broadcasted_iota(jnp.int32, low.shape, 1)
    return jnp.where(slots < low.shape[1] // 2, low, high)


def unpacked(which, block):
    turned = rolled(block)
    top = jnp.where(which == 0, block, turned)
    bottom = jnp.where(which == 0, turned, block)
    return jnp.concatenate([top, bottom], axis=0)


def for_near_and_far(forward, backward):
    odd = odd_slab()
    return jnp.where(odd, backward, forward), jnp.where(odd, forward, backward)


def from_prev_and_next(near, far):
    odd = odd_slab()
    return jnp.where(odd, near, far), jnp.where(odd, far, near)


def rim_kernel(voxels, live, movie, foot, start, far, near, count, traces, *rest):
    numbers, rims, edge, middle, sems = rest[-5:]
    rim = edge.shape[1]
    frames = edge.shape[0]
    there = 1 - lax.axis_index("tm")
    small = [
        copied(live, numbers, sems.at[0]),
        copied(start, traces, sems.at[1]),
        copied(foot.at[pl.ds(0, rim)], rims.at[pl.ds(0, rim)], sems.at[2]),
        copied(foot.at[pl.ds(voxels, rim)], rims.at[pl.ds(rim, rim)], sems.at[3]),
        copied(movie.at[:, pl.ds(0, rim)], edge, sems.at[4]),
        copied(movie.at[:, pl.ds(voxels // 2, rim)], middle, sems.at[5]),
    ]
    large = []
    if len(rest) > 5:
        first = first_column(there, voxels, rim)
        for i in range(voxels // 2 // rim - 1):
            column = movie.at[:, pl.ds(pl.multiple_of(first + i * rim, 128), rim)]
            large.append(copied(column, rest[0].at[pl.ds(i * frames, frames)], sems.at[6 + i]))
    small.pop().wait()
    if large:
        rest[0][(voxels // 2 // rim - 1) * frames:] = packed(there, middle[...])
    for copy in small:
        copy.wait()
    alive = numbers[lax.axis_index("slab")]
    count[...] = jnp.full(count.shape, alive, jnp.int32)
    seen = mm_t(jnp.concatenate(halves(living(alive, traces[...])), axis=0), rims[...])
    seen = seen[:frames] + seen[frames:]
    backward = edge[...].astype(F32) - seen[:, :rim]
    one, two = for_near_and_far(seen[:, rim:], backward)
    near[...] = coded(one)
    far[...] = coded(two)
    for copy in large:
        copy.wait()


def drive_kernel(
    voxels, count, movie, foot, start, plan, scale, cross_high, cross_low, rims, flat, masked, shown, sems
):
    rim = foot.shape[0] - voxels
    step = voxels // 2
    loads = []
    for i in range(2):
        columns = pl.ds(i * step, step)
        loads.append(copied(movie.at[:, columns], shown.at[:, columns], sems.at[i]))
    alive = count[0:1]
    masked[:voxels] = living(alive, foot[:voxels])
    ends = living(alive, foot[voxels:])
    masked[voxels:] = jnp.where(at_end("slab"), jnp.zeros_like(ends), ends)
    rims[:rim] = -masked[:rim]
    rims[rim:] = masked[voxels:]
    gram = t_mm(masked[...], masked[...])
    loads[0].wait()
    flat[...] = shown[:, :rim].T
    drive = mm(shown[:, :step], masked[:step])
    loads[1].wait()
    drive = drive + mm(shown[:, step:], masked[step:voxels])
    inverse = 1.0 / (diagonal(gram) + 1e-06)
    scale[...] = jnp.broadcast_to(inverse, scale.shape)
    gram_high, gram_low = halves(gram)
    cross_high[...] = gram_high[:GROUP, GROUP:]
    cross_low[...] = gram_low[:GROUP, GROUP:]
    current = living(alive, start[...])
    high, low = halves(current)
    for at in range(0, current.shape[1], GROUP):
        columns = slice(at, at + GROUP)
        coupled = mm(high[:, at:], gram_high[at:, columns]) + mm(high[:, at:], gram_low[at:, columns])
        coupled = coupled + mm(low[:, at:], gram_high[at:, columns])
        plan[:, columns] = current[:, columns] + (drive[:, columns] - coupled) * inverse[:, columns]


def sweep_kernel(
    plan, scale, cross_high, cross_low, rims, flat, far, near, traces, rounded, far_next, near_next
):
    rim = flat.shape[0]
    edges = rims[...]
    high, low = halves(decoded(jnp.concatenate(from_prev_and_next(near[...], far[...]), axis=1)))
    both = jnp.concatenate([edges, edges], axis=0)
    stepped = plan[...] + mm(jnp.concatenate([high, low], axis=1), both) * scale[0:1]
    first = jnp.maximum(stepped[:, :GROUP], 0.0)
    high, low = halves(first)
    cross = cross_high[...]
    coupled = mm(
        jnp.concatenate([high, low, high], axis=1), jnp.concatenate([cross, cross, cross_low[...]], axis=0)
    )
    second = jnp.maximum(stepped[:, GROUP:] - coupled * scale[0:1, GROUP:], 0.0)
    whole = jnp.concatenate([high, second.astype(BF)], axis=1)
    rounded[...] = whole
    seen = mm_t(edges, whole)
    one, two = for_near_and_far(seen[rim:], flat[...].astype(F32) + seen[:rim])
    near_next[...] = one.astype(BF)
    far_next[...] = two.astype(BF)
    traces[:, :GROUP] = first
    traces[:, GROUP:] = second


def own_kernel(voxels, movie, foot, fit, flat, total, quad, rim_part):
    rim = flat.shape[0]
    main = voxels // 2 - rim
    traces = fit[...]
    square = t_mm(traces, traces)
    quad[...] = square
    high, low = halves(square)
    begins, ends = foot[:rim], foot[voxels:]
    rim_part[:rim] = mm(flat[...], traces) - (mm(begins, high) + mm(begins, low))
    rim_part[rim:] = -(mm(ends, high) + mm(ends, low))
    first = first_column(lax.axis_index("tm"), voxels, rim)
    total[:main] = t_mm(movie[:, pl.ds(first, main)], traces)
    total[main:] = t_mm(movie[:, voxels // 2:voxels // 2 + rim], traces)


def both_kernel(rim_part, fit, far, near, lead, sent):
    rim = lead.shape[0]
    first = lax.axis_index("tm") == 0
    before, after = from_prev_and_next(near[...], far[...])
    traces = fit[...]
    begins = rim_part[:rim] - mm(before, traces)
    ends = rim_part[rim:] + mm(after, traces)
    lead[...] = jnp.where(first, begins, ends)
    sent[...] = jnp.where(first, ends, begins).astype(BF)


def main_kernel(voxels, rim, foot, total, quad, movie, fit, traces, out, new_tr, scale, moved, sems):
    here = lax.axis_index("tm")
    frames = fit.shape[0]
    width = voxels // 2
    main = width - rim
    written = [copied(traces, new_tr, sems.at[0])]
    fitted = fit[...]
    square = quad[...] + t_mm(fitted, fitted)
    inverse = 1.0 / jnp.maximum(diagonal(square), 1.0)
    scale[...] = jnp.broadcast_to(inverse, scale.shape)
    high, low = halves(square)
    first = first_column(here, voxels, rim)
    row = pl.multiple_of(rim - here * (rim // 2), 64)
    for begin, end in ((0, width // 2), (width // 2, main), (main, width)):
        if begin < main:
            own = foot[pl.ds(pl.multiple_of(first + begin, 128), end - begin)]
            columns = range(begin // rim, end // rim)
            shown = jnp.concatenate([movie[i * frames:(i + 1) * frames] for i in columns], axis=1)
        else:
            own = foot[width:width + rim]
            shown = unpacked(here, movie[main // rim * frames:])
        part = total[begin:end] + t_mm(shown, fitted) - (mm(own, high) + mm(own, low))
        moved[begin:end] = jnp.maximum(own.astype(F32) + part * inverse, 0.0).astype(BF)
        if begin < main:
            target = out.at[pl.ds(row + begin, end - begin)]
            written.append(copied(moved.at[pl.ds(begin, end - begin)], target, sems.at[len(written)]))
        else:
            half = rim // 2
            source = moved.at[pl.ds(pl.multiple_of(main + here * half, 64), half)]
            target = out.at[pl.ds(pl.multiple_of((1 - here) * (out.shape[0] - half), 64), half)]
            written.append(copied(source, target, sems.at[len(written)]))
    for copy in written:
        copy.wait()


def edge_kernel(voxels, sofar, foot, lead, came, scale, out, moved, sem):
    rim = lead.shape[0]
    here = lax.axis_index("tm")
    own = foot[pl.ds(pl.multiple_of(here * voxels, 128), rim)].astype(F32)
    moved[...] = jnp.maximum(own + (lead[...] + came[...].astype(F32)) * scale[0:1], 0.0).astype(BF)
    row = pl.multiple_of(here * (out.shape[0] - rim), 64)
    copied(moved, out.at[pl.ds(row, rim)], sem).wait()


def swapped(block, first):
    route = [(i, i + 1) for i in range(first, lax.axis_size("slab") - 1, 2)]
    return lax.ppermute(block, "slab", [(j, i) for i, j in route] + route)


def halved(voxels, rim, foot, recording, flat, outgoing, new_tr, rounded, far, near):
    frames = recording.shape[0]
    extended, neurons = foot.shape
    width, share = voxels // 2, extended // 2
    across = [(0, 1), (1, 0)]
    movie = lax.ppermute(outgoing, "tm", across)
    far = swapped(far, 1)
    near = swapped(near, 0)
    other = lax.ppermute(rounded, "tm", across)
    total, quad, rim_part = call(
        functools.partial(own_kernel, voxels),
        [
            shape((width, neurons), F32),
            shape((neurons, neurons), F32),
            shape((2 * rim, neurons), F32),
        ],
        [WHOLE] * 4,
        [WHOLE] * 3,
        0.6,
    )(recording, foot, rounded, flat)
    lead, sent = call(
        both_kernel,
        [shape((rim, neurons), F32), pltpu.VMEM((rim, neurons), BF)],
        [WHOLE] * 4,
        [WHOLE] * 2,
        0.3,
    )(rim_part, rounded, far, near)
    came = lax.ppermute(sent, "tm", across)
    sofar, new_tr, scale = call(
        functools.partial(main_kernel, voxels, rim),
        [pltpu.HBM((share, neurons), BF), pltpu.HBM((frames, neurons), F32), shape((8, neurons), F32)],
        [WHOLE] * 6,
        [LEFT_THERE] * 2 + [WHOLE],
        2.0,
        scratch_shapes=[pltpu.VMEM((width, neurons), BF), COPIES((4,))],
    )(foot, total, quad, movie, other, new_tr)
    new_foot = call(
        functools.partial(edge_kernel, voxels),
        pltpu.HBM((share, neurons), BF),
        [LEFT_THERE] + [WHOLE] * 4,
        LEFT_THERE,
        0.8,
        input_output_aliases={0: 0},
        scratch_shapes=[pltpu.VMEM((rim, neurons), BF), COPIES],
    )(sofar, foot, lead, came, scale)
    return new_tr, new_foot


def spread(voxels, rim, foot, recording, rounded):
    slabs, parts = lax.axis_size("slab"), lax.axis_size("tm")
    extended, neurons = foot.shape
    share = extended // parts
    here = lax.axis_index("tm")
    closing = here == parts - 1
    exact = lax.Precision.HIGHEST
    cut = voxels - (share - rim)
    columns = jnp.concatenate([recording[:, :cut], recording[:, :rim], recording[:, cut:]], 1)
    movie = lax.all_to_all(columns, "tm", split_axis=1, concat_axis=0, tiled=True)
    fit = lax.all_gather(rounded, "tm", axis=0, tiled=True)
    edge = jnp.where(here == 0, foot[voxels:], foot[:rim])
    seen = movie[:, :rim].astype(F32)
    sent = jnp.where(here == 0, 0.0, seen) - mm_t(fit, edge)
    ahead = [(i * parts, (i + 1) * parts) for i in range(slabs - 1)]
    behind = [((i + 2) * parts - 1, (i + 1) * parts - 1) for i in range(slabs - 1)]
    lead = jnp.where(closing, 0.0, seen) + lax.ppermute(sent, ("slab", "tm"), ahead + behind)
    lead = lax.dot_general(lead, fit.astype(F32), (((0,), (0,)), ((), ())), precision=exact)
    inner = t_mm(movie[:, rim:], fit)
    total = jnp.where(
        closing, jnp.concatenate([inner, lead], 0), jnp.concatenate([lead, inner], 0)
    )
    square = t_mm(fit, fit)
    own = lax.dynamic_slice_in_dim(foot, here * share, share, 0).astype(F32)
    total = total - jnp.dot(own, square, precision=exact)
    return jnp.maximum(own + total / jnp.maximum(jnp.diagonal(square), 1.0), 0.0).astype(BF)


def on_device(recording, footprints, traces, live_count):
    frames, voxels = recording.shape
    extended, neurons = footprints.shape
    rim = extended - voxels
    main = voxels // 2 // rim - 1
    split = lax.axis_size("tm") == 2
    share_shape = [pltpu.VMEM((main * frames + frames // 2, rim), BF)] if split else []
    pinned = [
        pltpu.with_memory_space_constraint(x, pltpu.HBM)
        for x in (live_count, recording, footprints, traces)
    ]
    far, near, count, begun, *outgoing = call(
        functools.partial(rim_kernel, voxels),
        [
            pltpu.VMEM((frames, rim), BF),
            pltpu.VMEM((frames, rim), BF),
            pltpu.VMEM((8, neurons), jnp.int32),
            pltpu.VMEM((frames, neurons), F32),
        ]
        + share_shape,
        [LEFT_THERE] * 4,
        [WHOLE] * (4 + len(share_shape)),
        1.5,
        scratch_shapes=[
            pltpu.SMEM(live_count.shape, jnp.int32),
            pltpu.VMEM((2 * rim, neurons), BF),
            pltpu.VMEM((frames, rim), BF),
            pltpu.VMEM((frames, rim), BF),
            COPIES((6 + main,)),
        ],
    )(*pinned)
    far = swapped(far, 1)
    near = swapped(near, 0)
    plan, scale, cross_high, cross_low, rims, flat, masked, shown = call(
        functools.partial(drive_kernel, voxels),
        [
            shape((frames, neurons), F32),
            shape((8, neurons), F32),
            shape((GROUP, GROUP), BF),
            shape((GROUP, GROUP), BF),
            shape((2 * rim, neurons), BF),
            shape((rim, frames), BF),
            pltpu.VMEM((extended, neurons), BF),
            pltpu.VMEM((frames, voxels), BF),
        ],
        [WHOLE, LEFT_THERE, WHOLE, WHOLE],
        [WHOLE] * 8,
        1.6,
        scratch_shapes=[COPIES((2,))],
    )(count, pinned[1], footprints, begun)
    new_tr, rounded, far, near = call(
        sweep_kernel,
        [
            pltpu.VMEM((frames, neurons), F32),
            pltpu.VMEM((frames, neurons), BF),
            pltpu.VMEM((rim, frames), BF),
            pltpu.VMEM((rim, frames), BF),
        ],
        [WHOLE] * 8,
        [WHOLE] * 4,
        0.5,
    )(plan, scale, cross_high, cross_low, rims, flat, far, near)
    if split:
        return halved(voxels, rim, masked, shown, flat, outgoing[0], new_tr, rounded, far, near)
    return new_tr, spread(voxels, rim, masked, recording, rounded)


def solution(mesh):
    placed = (P("tm", "slab"), P(None, "slab"), P("tm", "slab"), P())
    return jax.shard_map(
        on_device,
        mesh=mesh,
        in_specs=placed,
        out_specs=(P("tm", "slab"), P("tm", "slab")),
        check_vma=False,
    )
```

```python
import functools

import jax
import jax.numpy as jnp
from jax import lax
from jax.experimental import pallas as pl
from jax.experimental.pallas import tpu as pltpu
from jax.sharding import PartitionSpec as P

GROUP = 128
BF = jnp.bfloat16
F32 = jnp.float32
WHOLE = pl.BlockSpec(memory_space=pltpu.VMEM)
LEFT_THERE = pl.BlockSpec(memory_space=pl.ANY)
COPIES = pltpu.SemaphoreType.DMA
shape = jax.ShapeDtypeStruct


def mm(left, right):
    return jnp.dot(left, right, preferred_element_type=F32)


def mm_t(left, right):
    return lax.dot_general(left, right, (((1,), (1,)), ((), ())), preferred_element_type=F32)


def t_mm(left, right):
    return lax.dot_general(left, right, (((0,), (0,)), ((), ())), preferred_element_type=F32)


def halves(wide):
    high = wide.astype(BF)
    return high, (wide - high.astype(F32)).astype(BF)


def coded(block):
    square = block * block
    fourth = square * square
    eighth = fourth * fourth
    return jnp.where(block < 0, -eighth, eighth).astype(BF)


def decoded(block):
    wide = block.astype(F32)
    size = jnp.abs(wide)
    root = jnp.where(size > 0, jnp.exp2(jnp.log2(size) * 0.125), 0.0)
    return jnp.where(wide < 0, -root, root)


def living(count, block):
    slots = lax.broadcasted_iota(jnp.int32, block.shape, 1)
    return jnp.where(slots < count, block, jnp.zeros_like(block))


def diagonal(square):
    rows = lax.broadcasted_iota(jnp.int32, square.shape, 0)
    columns = lax.broadcasted_iota(jnp.int32, square.shape, 1)
    return jnp.sum(jnp.where(rows == columns, square, 0.0), axis=0, keepdims=True)


def at_end(axis):
    return lax.axis_index(axis) == lax.axis_size(axis) - 1


def odd_slab():
    return lax.axis_index("slab") % 2 == 1


def call(body, outs, in_specs, out_specs, expected, **more):
    return pl.pallas_call(
        body,
        out_shape=outs,
        in_specs=in_specs,
        out_specs=out_specs,
        compiler_params=pltpu.CompilerParams(vmem_limit_bytes=32 * 1024 * 1024),
        cost_estimate=pl.CostEstimate(
            flops=0, bytes_accessed=int(expected * 3_690_000), transcendentals=0
        ),
        **more,
    )


def copied(source, target, sem):
    copy = pltpu.make_async_copy(source, target, sem)
    copy.start()
    return copy


def first_column(which, voxels, rim):
    return pl.multiple_of(rim + which * (voxels // 2), 128)


def rolled(block):
    half = block.shape[1] // 2
    return jnp.concatenate([block[:, half:], block[:, :half]], axis=1)


def packed(which, middle):
    frames = middle.shape[0] // 2
    top, bottom = middle[:frames], middle[frames:]
    low = jnp.where(which == 0, top, rolled(top))
    high = jnp.where(which == 0, rolled(bottom), bottom)
    slots = lax.broadcasted_iota(jnp.int32, low.shape, 1)
    return jnp.where(slots < low.shape[1] // 2, low, high)


def unpacked(which, block):
    turned = rolled(block)
    top = jnp.where(which == 0, block, turned)
    bottom = jnp.where(which == 0, turned, block)
    return jnp.concatenate([top, bottom], axis=0)


def for_near_and_far(forward, backward):
    odd = odd_slab()
    return jnp.where(odd, backward, forward), jnp.where(odd, forward, backward)


def from_prev_and_next(near, far):
    odd = odd_slab()
    return jnp.where(odd, near, far), jnp.where(odd, far, near)


def rim_kernel(voxels, live, movie, foot, start, far, near, count, traces, *rest):
    numbers, rims, edge, middle, sems = rest[-5:]
    rim = edge.shape[1]
    frames = edge.shape[0]
    there = 1 - lax.axis_index("tm")
    small = [
        copied(start, traces, sems.at[1]),
        copied(live, numbers, sems.at[0]),
        copied(foot.at[pl.ds(0, rim)], rims.at[pl.ds(0, rim)], sems.at[2]),
        copied(foot.at[pl.ds(voxels, rim)], rims.at[pl.ds(rim, rim)], sems.at[3]),
        copied(movie.at[:, pl.ds(0, rim)], edge, sems.at[4]),
        copied(movie.at[:, pl.ds(voxels // 2, rim)], middle, sems.at[5]),
    ]
    large = []
    if len(rest) > 5:
        first = first_column(there, voxels, rim)
        for i in range(voxels // 2 // rim - 1):
            column = movie.at[:, pl.ds(pl.multiple_of(first + i * rim, 128), rim)]
            large.append(copied(column, rest[0].at[pl.ds(i * frames, frames)], sems.at[6 + i]))
    for copy in small:
        copy.wait()
    alive = numbers[lax.axis_index("slab")]
    seen = mm_t(jnp.concatenate(halves(living(alive, traces[...])), axis=0), rims[...])
    seen = seen[:frames] + seen[frames:]
    backward = edge[...].astype(F32) - seen[:, :rim]
    one, two = for_near_and_far(seen[:, rim:], backward)
    near[...] = coded(one)
    far[...] = coded(two)
    count[...] = jnp.full(count.shape, alive, jnp.int32)
    if large:
        rest[0][(voxels // 2 // rim - 1) * frames:] = packed(there, middle[...])
    for copy in large:
        copy.wait()


def drive_kernel(
    voxels, count, movie, foot, start, plan, scale, cross_high, cross_low, rims, flat, masked, shown, sems
):
    rim = foot.shape[0] - voxels
    step = voxels // 2
    loads = []
    for i in range(2):
        columns = pl.ds(i * step, step)
        loads.append(copied(movie.at[:, columns], shown.at[:, columns], sems.at[i]))
    alive = count[0:1]
    masked[:voxels] = living(alive, foot[:voxels])
    ends = living(alive, foot[voxels:])
    masked[voxels:] = jnp.where(at_end("slab"), jnp.zeros_like(ends), ends)
    rims[:rim] = -masked[:rim]
    rims[rim:] = masked[voxels:]
    gram = t_mm(masked[...], masked[...])
    loads[0].wait()
    flat[...] = shown[:, :rim].T
    drive = mm(shown[:, :step], masked[:step])
    loads[1].wait()
    drive = drive + mm(shown[:, step:], masked[step:voxels])
    inverse = 1.0 / (diagonal(gram) + 1e-06)
    scale[...] = jnp.broadcast_to(inverse, scale.shape)
    gram_high, gram_low = halves(gram)
    cross_high[...] = gram_high[:GROUP, GROUP:]
    cross_low[...] = gram_low[:GROUP, GROUP:]
    current = living(alive, start[...])
    high, low = halves(current)
    for at in range(0, current.shape[1], GROUP):
        columns = slice(at, at + GROUP)
        coupled = mm(high[:, at:], gram_high[at:, columns]) + mm(high[:, at:], gram_low[at:, columns])
        coupled = coupled + mm(low[:, at:], gram_high[at:, columns])
        plan[:, columns] = current[:, columns] + (drive[:, columns] - coupled) * inverse[:, columns]


def sweep_kernel(
    plan, scale, cross_high, cross_low, rims, flat, far, near, traces, rounded, far_next, near_next
):
    rim = flat.shape[0]
    edges = rims[...]
    high, low = halves(decoded(jnp.concatenate(from_prev_and_next(near[...], far[...]), axis=1)))
    both = jnp.concatenate([edges, edges], axis=0)
    stepped = plan[...] + mm(jnp.concatenate([high, low], axis=1), both) * scale[0:1]
    first = jnp.maximum(stepped[:, :GROUP], 0.0)
    high, low = halves(first)
    cross = cross_high[...]
    coupled = mm(
        jnp.concatenate([high, low, high], axis=1), jnp.concatenate([cross, cross, cross_low[...]], axis=0)
    )
    second = jnp.maximum(stepped[:, GROUP:] - coupled * scale[0:1, GROUP:], 0.0)
    whole = jnp.concatenate([high, second.astype(BF)], axis=1)
    rounded[...] = whole
    seen = mm_t(edges, whole)
    one, two = for_near_and_far(seen[rim:], flat[...].astype(F32) + seen[:rim])
    near_next[...] = one.astype(BF)
    far_next[...] = two.astype(BF)
    traces[:, :GROUP] = first
    traces[:, GROUP:] = second


def own_kernel(voxels, movie, foot, fit, flat, total, quad, rim_part):
    rim = flat.shape[0]
    main = voxels // 2 - rim
    traces = fit[...]
    square = t_mm(traces, traces)
    quad[...] = square
    high, low = halves(square)
    begins, ends = foot[:rim], foot[voxels:]
    rim_part[:rim] = mm(flat[...], traces) - (mm(begins, high) + mm(begins, low))
    rim_part[rim:] = -(mm(ends, high) + mm(ends, low))
    first = first_column(lax.axis_index("tm"), voxels, rim)
    total[:main] = t_mm(movie[:, pl.ds(first, main)], traces)
    total[main:] = t_mm(movie[:, voxels // 2:voxels // 2 + rim], traces)


def both_kernel(rim_part, fit, far, near, lead, sent):
    rim = lead.shape[0]
    first = lax.axis_index("tm") == 0
    before, after = from_prev_and_next(near[...], far[...])
    traces = fit[...]
    begins = rim_part[:rim] - mm(before, traces)
    ends = rim_part[rim:] + mm(after, traces)
    lead[...] = jnp.where(first, begins, ends)
    sent[...] = jnp.where(first, ends, begins).astype(BF)


def main_kernel(voxels, rim, foot, total, quad, movie, fit, traces, out, new_tr, scale, moved, sems):
    here = lax.axis_index("tm")
    frames = fit.shape[0]
    width = voxels // 2
    main = width - rim
    written = [copied(traces, new_tr, sems.at[0])]
    fitted = fit[...]
    square = quad[...] + t_mm(fitted, fitted)
    inverse = 1.0 / jnp.maximum(diagonal(square), 1.0)
    scale[...] = jnp.broadcast_to(inverse, scale.shape)
    high, low = halves(square)
    first = first_column(here, voxels, rim)
    row = pl.multiple_of(rim - here * (rim // 2), 64)
    for begin, end in ((0, width // 2), (width // 2, main), (main, width)):
        if begin < main:
            own = foot[pl.ds(pl.multiple_of(first + begin, 128), end - begin)]
            columns = range(begin // rim, end // rim)
            shown = jnp.concatenate([movie[i * frames:(i + 1) * frames] for i in columns], axis=1)
        else:
            own = foot[width:width + rim]
            shown = unpacked(here, movie[main // rim * frames:])
        part = total[begin:end] + t_mm(shown, fitted) - (mm(own, high) + mm(own, low))
        moved[begin:end] = jnp.maximum(own.astype(F32) + part * inverse, 0.0).astype(BF)
        if begin < main:
            target = out.at[pl.ds(row + begin, end - begin)]
            written.append(copied(moved.at[pl.ds(begin, end - begin)], target, sems.at[len(written)]))
        else:
            half = rim // 2
            source = moved.at[pl.ds(pl.multiple_of(main + here * half, 64), half)]
            target = out.at[pl.ds(pl.multiple_of((1 - here) * (out.shape[0] - half), 64), half)]
            written.append(copied(source, target, sems.at[len(written)]))
    for copy in written:
        copy.wait()


def edge_kernel(voxels, sofar, foot, lead, came, scale, out, moved, sem):
    rim = lead.shape[0]
    here = lax.axis_index("tm")
    own = foot[pl.ds(pl.multiple_of(here * voxels, 128), rim)].astype(F32)
    moved[...] = jnp.maximum(own + (lead[...] + came[...].astype(F32)) * scale[0:1], 0.0).astype(BF)
    row = pl.multiple_of(here * (out.shape[0] - rim), 64)
    copied(moved, out.at[pl.ds(row, rim)], sem).wait()


def swapped(block, first):
    route = [(i, i + 1) for i in range(first, lax.axis_size("slab") - 1, 2)]
    return lax.ppermute(block, "slab", [(j, i) for i, j in route] + route)


def halved(voxels, rim, foot, recording, flat, outgoing, new_tr, rounded, far, near):
    frames = recording.shape[0]
    extended, neurons = foot.shape
    width, share = voxels // 2, extended // 2
    across = [(0, 1), (1, 0)]
    movie = lax.ppermute(outgoing, "tm", across)
    far = swapped(far, 1)
    near = swapped(near, 0)
    other = lax.ppermute(rounded, "tm", across)
    total, quad, rim_part = call(
        functools.partial(own_kernel, voxels),
        [
            shape((width, neurons), F32),
            shape((neurons, neurons), F32),
            shape((2 * rim, neurons), F32),
        ],
        [WHOLE] * 4,
        [WHOLE] * 3,
        0.6,
    )(recording, foot, rounded, flat)
    lead, sent = call(
        both_kernel,
        [shape((rim, neurons), F32), pltpu.VMEM((rim, neurons), BF)],
        [WHOLE] * 4,
        [WHOLE] * 2,
        0.3,
    )(rim_part, rounded, far, near)
    came = lax.ppermute(sent, "tm", across)
    sofar, new_tr, scale = call(
        functools.partial(main_kernel, voxels, rim),
        [pltpu.HBM((share, neurons), BF), pltpu.HBM((frames, neurons), F32), shape((8, neurons), F32)],
        [WHOLE] * 6,
        [LEFT_THERE] * 2 + [WHOLE],
        2.0,
        scratch_shapes=[pltpu.VMEM((width, neurons), BF), COPIES((4,))],
    )(foot, total, quad, movie, other, new_tr)
    new_foot = call(
        functools.partial(edge_kernel, voxels),
        pltpu.HBM((share, neurons), BF),
        [LEFT_THERE] + [WHOLE] * 4,
        LEFT_THERE,
        0.8,
        input_output_aliases={0: 0},
        scratch_shapes=[pltpu.VMEM((rim, neurons), BF), COPIES],
    )(sofar, foot, lead, came, scale)
    return new_tr, new_foot


def spread(voxels, rim, foot, recording, rounded):
    slabs, parts = lax.axis_size("slab"), lax.axis_size("tm")
    extended, neurons = foot.shape
    share = extended // parts
    here = lax.axis_index("tm")
    closing = here == parts - 1
    exact = lax.Precision.HIGHEST
    cut = voxels - (share - rim)
    columns = jnp.concatenate([recording[:, :cut], recording[:, :rim], recording[:, cut:]], 1)
    movie = lax.all_to_all(columns, "tm", split_axis=1, concat_axis=0, tiled=True)
    fit = lax.all_gather(rounded, "tm", axis=0, tiled=True)
    edge = jnp.where(here == 0, foot[voxels:], foot[:rim])
    seen = movie[:, :rim].astype(F32)
    sent = jnp.where(here == 0, 0.0, seen) - mm_t(fit, edge)
    ahead = [(i * parts, (i + 1) * parts) for i in range(slabs - 1)]
    behind = [((i + 2) * parts - 1, (i + 1) * parts - 1) for i in range(slabs - 1)]
    lead = jnp.where(closing, 0.0, seen) + lax.ppermute(sent, ("slab", "tm"), ahead + behind)
    lead = lax.dot_general(lead, fit.astype(F32), (((0,), (0,)), ((), ())), precision=exact)
    inner = t_mm(movie[:, rim:], fit)
    total = jnp.where(
        closing, jnp.concatenate([inner, lead], 0), jnp.concatenate([lead, inner], 0)
    )
    square = t_mm(fit, fit)
    own = lax.dynamic_slice_in_dim(foot, here * share, share, 0).astype(F32)
    total = total - jnp.dot(own, square, precision=exact)
    return jnp.maximum(own + total / jnp.maximum(jnp.diagonal(square), 1.0), 0.0).astype(BF)


def on_device(recording, footprints, traces, live_count):
    frames, voxels = recording.shape
    extended, neurons = footprints.shape
    rim = extended - voxels
    main = voxels // 2 // rim - 1
    split = lax.axis_size("tm") == 2
    share_shape = [pltpu.VMEM((main * frames + frames // 2, rim), BF)] if split else []
    pinned = [
        pltpu.with_memory_space_constraint(x, pltpu.HBM)
        for x in (live_count, recording, footprints, traces)
    ]
    far, near, count, begun, *outgoing = call(
        functools.partial(rim_kernel, voxels),
        [
            pltpu.VMEM((frames, rim), BF),
            pltpu.VMEM((frames, rim), BF),
            pltpu.VMEM((8, neurons), jnp.int32),
            pltpu.VMEM((frames, neurons), F32),
        ]
        + share_shape,
        [LEFT_THERE] * 4,
        [WHOLE] * (4 + len(share_shape)),
        1.5,
        scratch_shapes=[
            pltpu.SMEM(live_count.shape, jnp.int32),
            pltpu.VMEM((2 * rim, neurons), BF),
            pltpu.VMEM((frames, rim), BF),
            pltpu.VMEM((frames, rim), BF),
            COPIES((6 + main,)),
        ],
    )(*pinned)
    far = swapped(far, 1)
    near = swapped(near, 0)
    plan, scale, cross_high, cross_low, rims, flat, masked, shown = call(
        functools.partial(drive_kernel, voxels),
        [
            shape((frames, neurons), F32),
            shape((8, neurons), F32),
            shape((GROUP, GROUP), BF),
            shape((GROUP, GROUP), BF),
            shape((2 * rim, neurons), BF),
            shape((rim, frames), BF),
            pltpu.VMEM((extended, neurons), BF),
            pltpu.VMEM((frames, voxels), BF),
        ],
        [WHOLE, LEFT_THERE, WHOLE, WHOLE],
        [WHOLE] * 8,
        1.6,
        scratch_shapes=[COPIES((2,))],
    )(count, pinned[1], footprints, begun)
    new_tr, rounded, far, near = call(
        sweep_kernel,
        [
            pltpu.VMEM((frames, neurons), F32),
            pltpu.VMEM((frames, neurons), BF),
            pltpu.VMEM((rim, frames), BF),
            pltpu.VMEM((rim, frames), BF),
        ],
        [WHOLE] * 8,
        [WHOLE] * 4,
        0.5,
    )(plan, scale, cross_high, cross_low, rims, flat, far, near)
    if split:
        return halved(voxels, rim, masked, shown, flat, outgoing[0], new_tr, rounded, far, near)
    return new_tr, spread(voxels, rim, masked, recording, rounded)


def solution(mesh):
    placed = (P("tm", "slab"), P(None, "slab"), P("tm", "slab"), P())
    return jax.shard_map(
        on_device,
        mesh=mesh,
        in_specs=placed,
        out_specs=(P("tm", "slab"), P("tm", "slab")),
        check_vma=False,
    )
```
